128 devices in a mesh: pipe: 4 (over y), fsdp: 32 (over z, x, core).
Axes of the slice: x: 4, y: 4, z: 4, core: 2. Of those that a mesh axis runs over, the one named last changes fastest.
Arguments:
- tokens: bfloat16 [4096, 4096], P('fsdp'), may hold values from -6 to 6
- targets: bfloat16 [4096, 4096], P('fsdp'), may hold values from -6 to 6
- norm_gain: bfloat16 [4, 4096], P('pipe', 'fsdp'), may hold values from 0.099609375 to 1.8984375
- down_weight: bfloat16 [4, 4096, 256], P('pipe', 'fsdp'), may hold values from -0.09375 to 0.09375
- up_weight: bfloat16 [4, 256, 4096], P('pipe', None, 'fsdp'), may hold values from -0.375 to 0.375
- down_vector: bfloat16 [4, 4096, 256], P('pipe', 'fsdp'), may hold values from -1 to 1
- up_vector: bfloat16 [4, 256, 4096], P('pipe', None, 'fsdp'), may hold values from -1 to 1
Outputs:
- next_down: bfloat16 [4, 4096, 256], P('pipe', 'fsdp')
- next_up: bfloat16 [4, 256, 4096], P('pipe', None, 'fsdp')
- quotient: float32 [], replicated
The draws below stay inside these ranges and needn't reach their ends.
All inputs are finite; a program needn't handle non-finite values.
Results may differ from the reference program's by a relative error of at most 0.02.
Values may be sent and summed in bfloat16 or wider, within the bound.
No kernel may reach another device: no remote copies, remote signals or barrier semaphores. Data moves between devices by JAX's collectives and lax.ppermute only.
A program may use at most 128 MiB of HBM per device.

```python
import jax
import jax.numpy as jnp
from jax import lax

D = 4096
RANK = 256
LAYERS = 4
TOKENS = 4096


def envelope(key, extent, growth_dim):
    positions = lax.broadcasted_iota(jnp.float32, extent, growth_dim)
    growth = (1.0 + 2.0 * positions / (extent[growth_dim] - 1)) / 3.0
    jitter = 10.0 ** (jax.random.uniform(key, extent) - 1.0)
    return growth * jitter


def draw_down_vector(key, part):
    key = jax.random.fold_in(key, 7)
    subkeys = jax.random.split(key, 3)
    extent = (LAYERS, D, RANK)
    signal = jax.random.uniform(subkeys[0], extent, minval=-1.0, maxval=1.0)
    return (signal * envelope(subkeys[2], extent, 1)).astype(jnp.bfloat16)


def draw_up_vector(key, part):
    key = jax.random.fold_in(key, 13)
    subkeys = jax.random.split(key, 3)
    extent = (LAYERS, RANK, D)
    signal = jax.random.uniform(subkeys[0], extent, minval=-1.0, maxval=1.0)
    return (signal * envelope(subkeys[2], extent, 2)).astype(jnp.bfloat16)


def block_scale(key, shape, cuts, least, high):
    gain = 1.0
    for dim, blocks in cuts:
        draws = jax.random.uniform(jax.random.fold_in(jax.random.fold_in(key, 6), dim), (blocks,), jnp.float32, least / len(cuts), high / len(cuts))
        gain = gain * jnp.repeat(jnp.exp(draws), shape[dim] // blocks).reshape((-1,) + (1,) * (len(shape) - 1 - dim))
    return gain


def gaussian(rng, dims, spread, limit, pieces=(), kind=jnp.bfloat16):
    factor_of = block_scale(rng, dims, pieces, -0.22, 0.18) if pieces else 1.0
    entries = jax.random.normal(rng, dims, jnp.float32) * spread * factor_of
    return jnp.minimum(jnp.maximum(entries, -limit), limit).astype(kind)


def setup_inputs(seed: int = 0) -> dict:
    keys = jax.random.split(jax.random.key(seed), 8)
    tokens = gaussian(keys[0], (TOKENS, D), 1.0, 6.0, ((0, 32),))
    targets = gaussian(keys[1], (TOKENS, D), 1.0, 6.0, ((0, 32),))
    norm_gain = jnp.clip(1.0 + 0.18 * jax.random.normal(keys[2], (LAYERS, D), jnp.float32), 0.099609375, 1.8984375).astype(jnp.bfloat16)
    down_weight = gaussian(keys[3], (LAYERS, D, RANK), D ** -0.5, 0.09375, ((0, 4), (1, 32)))
    up_weight = gaussian(keys[4], (LAYERS, RANK, D), RANK ** -0.5, 0.375, ((0, 4), (2, 32)))
    down_vector = draw_down_vector(jax.random.fold_in(keys[7], 71), 0)
    up_vector = draw_up_vector(jax.random.fold_in(keys[7], 71), 0)
    return dict(tokens=tokens, targets=targets, norm_gain=norm_gain, down_weight=down_weight, up_weight=up_weight, down_vector=down_vector, up_vector=up_vector)


EPS = 1e-06

def norm_rows(hidden, norm_scale):
    mean_square = lax.optimization_barrier(jnp.mean(hidden * hidden, axis=-1, keepdims=True))
    return hidden * lax.rsqrt(mean_square + EPS) * norm_scale

def silu_slopes(pre_act):
    logistic = jax.nn.sigmoid(pre_act)
    slope_first = logistic * (1.0 + pre_act * (1.0 - logistic))
    slope_second = logistic * (1.0 - logistic) * (2.0 + pre_act * (1.0 - 2.0 * logistic))
    return (slope_first, slope_second)

def forward_parts(hidden_in, tangent_in, norm_scale, down_full, up_full, down_dir, up_dir):
    hidden = hidden_in.astype(jnp.float32)
    tangent = tangent_in.astype(jnp.float32)
    normed, normed_dot = jax.jvp(lambda values: norm_rows(values, norm_scale), (hidden,), (tangent,))
    normed = normed.astype(jnp.bfloat16)
    normed_dot = normed_dot.astype(jnp.bfloat16)
    pre_act = jnp.dot(normed, down_full, preferred_element_type=jnp.float32)
    pre_dot = jnp.dot(normed_dot, down_full, preferred_element_type=jnp.float32) + jnp.dot(normed, down_dir, preferred_element_type=jnp.float32)
    slope_first, slope_second = silu_slopes(pre_act)
    activated = jax.nn.silu(pre_act).astype(jnp.bfloat16)
    act_dot = (slope_first * pre_dot).astype(jnp.bfloat16)
    return (hidden, tangent, normed, normed_dot, pre_dot, slope_first, slope_second, activated, act_dot)

def forward_out(pair_in, norm_scale, down_full, up_full, down_dir, up_dir):
    parts = forward_parts(pair_in[0], pair_in[1], norm_scale, down_full, up_full, down_dir, up_dir)
    hidden, tangent, activated, act_dot = (parts[0], parts[1], parts[7], parts[8])
    output = hidden + jnp.dot(activated, up_full, preferred_element_type=jnp.float32)
    output_dot = tangent + jnp.dot(act_dot, up_full, preferred_element_type=jnp.float32) + jnp.dot(activated, up_dir, preferred_element_type=jnp.float32)
    return jnp.stack([output.astype(jnp.bfloat16), output_dot.astype(jnp.bfloat16)])

def backward_all(pair_in, cot_pair, norm_scale, down_full, up_full, down_dir, up_dir):
    parts = forward_parts(pair_in[0], pair_in[1], norm_scale, down_full, up_full, down_dir, up_dir)
    hidden, tangent, normed, normed_dot, pre_dot, slope_first, slope_second, activated, act_dot = parts
    cot_value = cot_pair[0]
    cot_dot = cot_pair[1]
    act_bar = jnp.dot(cot_value, up_full.T, preferred_element_type=jnp.float32)
    act_bar_dot = jnp.dot(cot_dot, up_full.T, preferred_element_type=jnp.float32) + jnp.dot(cot_value, up_dir.T, preferred_element_type=jnp.float32)
    pre_bar = (act_bar * slope_first).astype(jnp.bfloat16)
    pre_bar_dot = (act_bar_dot * slope_first + act_bar * slope_second * pre_dot).astype(jnp.bfloat16)
    normed_bar = jnp.dot(pre_bar, down_full.T, preferred_element_type=jnp.float32)
    normed_bar_dot = jnp.dot(pre_bar_dot, down_full.T, preferred_element_type=jnp.float32) + jnp.dot(pre_bar, down_dir.T, preferred_element_type=jnp.float32)

    def pull_back(values, weights_bar):
        return jax.vjp(lambda inner: norm_rows(inner, norm_scale), values)[1](weights_bar)[0]
    hidden_bar, hidden_bar_dot = jax.jvp(pull_back, (hidden, normed_bar), (tangent, normed_bar_dot))
    returned = jnp.stack([(cot_value.astype(jnp.float32) + hidden_bar).astype(jnp.bfloat16), (cot_dot.astype(jnp.float32) + hidden_bar_dot).astype(jnp.bfloat16)])
    hess_down = jnp.dot(normed_dot.T, pre_bar, preferred_element_type=jnp.float32) + jnp.dot(normed.T, pre_bar_dot, preferred_element_type=jnp.float32)
    hess_up = jnp.dot(act_dot.T, cot_value, preferred_element_type=jnp.float32) + jnp.dot(activated.T, cot_dot, preferred_element_type=jnp.float32)
    return (returned, hess_down, hess_up)

def reference(tokens, targets, norm_gain, down_weight, up_weight, down_vector, up_vector):
    hidden_pair = jnp.stack([tokens, jnp.zeros_like(tokens)])
    stored = []
    for layer_index in range(LAYERS):
        stored.append(hidden_pair)
        hidden_pair = forward_out(hidden_pair, norm_gain[layer_index].astype(jnp.float32), down_weight[layer_index], up_weight[layer_index], down_vector[layer_index], up_vector[layer_index])
    difference = (hidden_pair[0].astype(jnp.float32) - targets.astype(jnp.float32)).astype(jnp.bfloat16)
    cotangent = jnp.stack([difference, hidden_pair[1]])
    downs = []
    uppers = []
    for layer_index in reversed(range(LAYERS)):
        cotangent, hess_down, hess_up = backward_all(stored[layer_index], cotangent, norm_gain[layer_index].astype(jnp.float32), down_weight[layer_index], up_weight[layer_index], down_vector[layer_index], up_vector[layer_index])
        downs.append(hess_down)
        uppers.append(hess_up)
    hess_downs = jnp.stack(downs[::-1])
    hess_ups = jnp.stack(uppers[::-1])
    total_count = 2.0 * LAYERS * D * RANK
    down_dir = down_vector.astype(jnp.float32)
    up_dir = up_vector.astype(jnp.float32)
    square_mean = (jnp.sum(hess_downs * hess_downs) + jnp.sum(hess_ups * hess_ups)) / total_count
    cross_mean = (jnp.sum(down_dir * hess_downs) + jnp.sum(up_dir * hess_ups)) / total_count
    vector_mean = (jnp.sum(down_dir * down_dir) + jnp.sum(up_dir * up_dir)) / total_count
    scale_rms = jnp.sqrt(square_mean + EPS)
    quotient = cross_mean / (vector_mean + EPS) / TOKENS
    return ((hess_downs / scale_rms).astype(jnp.bfloat16), (hess_ups / scale_rms).astype(jnp.bfloat16), quotient)
```

```python
import jax
import jax.numpy as jnp
from jax import lax
from jax.sharding import Mesh, PartitionSpec as P

EPS = 1e-06
D = 4096
RANK = 256
LAYERS = 4
TOKENS = 4096
ROWS = 64
HALF = 2048
F32 = jnp.float32
BF16 = jnp.bfloat16


def shift(value, axis, steps):
    return lax.ppermute(value, axis, [(i, (i + steps) % 4) for i in range(4)])


def swap(value):
    return lax.ppermute(value, "c", [(0, 1), (1, 0)])


def dot(left, right, dims):
    return lax.dot_general(left, right, (dims, ((), ())), preferred_element_type=F32)


def mm(left, right):
    return dot(left, right, ((1,), (0,)))


def mm_nt(left, right):
    return dot(left, right, ((1,), (1,)))


def mm_tn(left, right):
    return dot(left, right, ((0,), (0,)))


def add_bf16(left, right):
    return (left.astype(F32) + right.astype(F32)).astype(BF16)


def core_rows(tokens, core):
    rows = lax.dynamic_slice_in_dim(tokens, lax.axis_index("y") * 32, 32, 0)
    rows = rows.reshape(32, 16, 2, 128)
    own = lax.dynamic_index_in_dim(rows, core, 2, keepdims=False).reshape(32, HALF)
    other = lax.dynamic_index_in_dim(rows, 1 - core, 2, keepdims=False).reshape(32, HALF)
    got = swap(other)
    first = jnp.where(core == 0, own, got)
    second = jnp.where(core == 0, got, own)
    return jnp.concatenate([first, second], 0)


def partial_down(h, t, w):
    hf, tf = h.astype(F32), t.astype(F32)
    u = mm(h, w[:, :256])
    v = mm(t, w[:, :256]) + mm(h, w[:, 256:512])
    s1 = jnp.sum(hf * hf, axis=1, keepdims=True)
    s2 = jnp.sum(hf * tf, axis=1, keepdims=True)
    lane = lax.broadcasted_iota(jnp.int32, (ROWS, 128), 1)
    return jnp.concatenate([u, v, jnp.where(lane < 64, s1, s2)], 1)


def middle(full):
    u, v = full[:, :256], full[:, 256:512]
    r = lax.rsqrt(full[:, 512:513] / D + EPS)
    c = full[:, 640 - 1 : 640] / D
    r3c = r * r * r * c
    pre = r * u
    pre_dot = r * v - r3c * u
    s = jax.nn.sigmoid(pre)
    slope = s * (1.0 + pre * (1.0 - s))
    slope2 = s * (1.0 - s) * (2.0 + pre * (1.0 - 2.0 * s))
    act = (pre * s).astype(BF16)
    act_dot = (slope * pre_dot).astype(BF16)
    return u, v, r, c, pre_dot, slope, slope2, act, act_dot


def ring_scatter(slots, axis):
    own, ahead, behind, across = slots
    cut = across.shape[0] // 2
    up = shift(across[:cut], axis, 1)
    down = shift(across[cut:], axis, -1)
    ahead = jnp.concatenate([add_bf16(ahead[:cut], up), ahead[cut:]], 0)
    behind = jnp.concatenate([behind[:cut], add_bf16(behind[cut:], down)], 0)
    got_up = shift(ahead, axis, 1)
    got_down = shift(behind, axis, -1)
    return own.astype(F32) + got_up.astype(F32) + got_down.astype(F32)


def direct_scatter(slots, axis):
    own, ahead, behind, across = slots
    return (
        own.astype(F32)
        + shift(ahead, axis, 1).astype(F32)
        + shift(behind, axis, -1).astype(F32)
        + shift(across, axis, 2).astype(F32)
    )


def slots_of(value, axis_name, dim):
    me = lax.axis_index(axis_name)
    return [
        lax.dynamic_index_in_dim(value, (me + step) % 4, dim, keepdims=False)
        for step in (0, 1, 3, 2)
    ]


def sum_all(value):
    value = value + swap(value)
    for axis in ("x", "z", "y"):
        value = value + shift(value, axis, 1) + shift(value, axis, -1) + shift(value, axis, 2)
    return value


def local(tokens, targets, norm_gain, down_weight, up_weight, down_vector, up_vector):
    core = lax.axis_index("c")
    gain = norm_gain[0].astype(F32)[:, None]
    chunk = jnp.concatenate(
        [
            (down_weight[0].astype(F32) * gain).astype(BF16),
            (down_vector[0].astype(F32) * gain).astype(BF16),
            up_weight[0].T,
            up_vector[0].T,
        ],
        1,
    )
    weights = lax.all_gather(chunk, ("y", "z", "x"), axis=0, tiled=True)
    weights = weights.reshape(LAYERS, HALF, 1024)
    h = core_rows(tokens, core)
    goal = core_rows(targets, core)
    t = jnp.zeros_like(h)

    states, mids = [], []
    for layer in range(LAYERS):
        w = weights[layer]
        part = partial_down(h, t, w)
        mid = middle(part + swap(part))
        states.append((h, t))
        mids.append(mid)
        act, act_dot = mid[7], mid[8]
        up, up_vec = w[:, 512:768], w[:, 768:]
        h, t = (
            (h.astype(F32) + mm_nt(act, up)).astype(BF16),
            (t.astype(F32) + mm_nt(act_dot, up) + mm_nt(act, up_vec)).astype(BF16),
        )

    cot = (h.astype(F32) - goal.astype(F32)).astype(BF16)
    cot_dot = t
    downs, ups = [None] * LAYERS, [None] * LAYERS
    for layer in reversed(range(LAYERS)):
        w = weights[layer]
        h, t = states[layer]
        u, v, r, c, pre_dot, slope, slope2, act, act_dot = mids[layer]
        up, up_vec = w[:, 512:768], w[:, 768:]
        part = jnp.concatenate([mm(cot, up), mm(cot_dot, up) + mm(cot, up_vec)], 1)
        full = part + swap(part)
        e, e_dot = full[:, :256], full[:, 256:]
        s = (e * slope).astype(BF16)
        s_dot = (e_dot * slope + e * slope2 * pre_dot).astype(BF16)
        hf, tf = h.astype(F32), t.astype(F32)
        r3 = r * r * r
        n = (r * hf).astype(BF16)
        n_dot = (r * tf - r3 * c * hf).astype(BF16)
        downs[layer] = (mm_tn(n_dot, s) + mm_tn(n, s_dot)).astype(BF16)
        ups[layer] = (mm_tn(cot, act_dot) + mm_tn(cot_dot, act)).astype(BF16)
        if layer > 0:
            sf, sdf = s.astype(F32), s_dot.astype(F32)
            q = jnp.sum(sf * u, axis=1, keepdims=True) / D
            q_dot = jnp.sum(sf * v + sdf * u, axis=1, keepdims=True) / D
            m = mm_nt(s, w[:, :256])
            m_dot = mm_nt(s_dot, w[:, :256]) + mm_nt(s, w[:, 256:512])
            bar = r * m - r3 * q * hf
            bar_dot = (
                r * m_dot
                - r3 * c * m
                - r3 * q * tf
                + (3.0 * r3 * r * r * c * q - r3 * q_dot) * hf
            )
            cot = (cot.astype(F32) + bar).astype(BF16)
            cot_dot = (cot_dot.astype(F32) + bar_dot).astype(BF16)

    hess_down = jnp.stack(downs).reshape(LAYERS, 4, 4, 128, RANK)
    hess_up = jnp.stack(ups).reshape(LAYERS, 4, 4, 128, RANK)
    down_1 = ring_scatter(slots_of(hess_down, "z", 1), "z").astype(BF16)
    up_1 = ring_scatter(slots_of(hess_up, "x", 2), "x").astype(BF16)
    down_2 = direct_scatter(slots_of(down_1, "x", 1), "x").astype(BF16)
    up_2 = direct_scatter(slots_of(up_1, "z", 1), "z").astype(BF16)
    both = jnp.concatenate([down_2, up_2], 1)
    share = direct_scatter(slots_of(both, "y", 0), "y")
    share_down = share[:128] * gain
    share_up = share[128:].T
    own_down = down_vector[0].astype(F32)
    own_up = up_vector[0].astype(F32)
    totals = jnp.stack(
        [
            jnp.sum(share_down * share_down) + jnp.sum(share_up * share_up),
            jnp.sum(own_down * share_down) + jnp.sum(own_up * share_up),
            jnp.sum(own_down * own_down) + jnp.sum(own_up * own_up),
        ]
    )
    totals = sum_all(totals)
    total_count = 2.0 * LAYERS * D * RANK
    square_mean = totals[0] / total_count
    cross_mean = totals[1] / total_count
    vector_mean = totals[2] / total_count
    scale_rms = jnp.sqrt(square_mean + EPS)
    quotient = cross_mean / (vector_mean + EPS) / TOKENS
    next_down = (share_down / scale_rms).astype(BF16)[None]
    next_up = (share_up / scale_rms).astype(BF16)[None]
    return (next_down, next_up, quotient)


def solution(mesh):
    fine = Mesh(mesh.devices.reshape(4, 4, 4, 2), ("y", "z", "x", "c"))
    fsdp = ("z", "x", "c")
    placed = (
        P(fsdp, None),
        P(fsdp, None),
        P("y", fsdp),
        P("y", fsdp, None),
        P("y", None, fsdp),
        P("y", fsdp, None),
        P("y", None, fsdp),
    )
    return jax.shard_map(
        local,
        mesh=fine,
        in_specs=placed,
        out_specs=(P("y", fsdp, None), P("y", None, fsdp), P()),
        check_vma=False,
    )
```

```python
import functools

import jax
import jax.numpy as jnp
from jax import lax
from jax.experimental import pallas as pl
from jax.experimental.pallas import tpu as pltpu
from jax.sharding import Mesh, PartitionSpec as P

EPS = 1e-06
D = 4096
RANK = 256
LAYERS = 4
TOKENS = 4096
ROWS = 64
HALF = 2048
F32 = jnp.float32
BF16 = jnp.bfloat16


def shift(value, axis, steps):
    return lax.ppermute(value, axis, [(i, (i + steps) % 4) for i in range(4)])


def swap(value):
    return lax.ppermute(value, "c", [(0, 1), (1, 0)])


def dot(left, right, dims):
    return lax.dot_general(left, right, (dims, ((), ())), preferred_element_type=F32)


def mm(left, right):
    return dot(left, right, ((1,), (0,)))


def mm_nt(left, right):
    return dot(left, right, ((1,), (1,)))


def mm_tn(left, right):
    return dot(left, right, ((0,), (0,)))


def core_rows(tokens, core):
    rows = lax.dynamic_slice_in_dim(tokens, lax.axis_index("y") * 32, 32, 0)
    rows = rows.reshape(32, 16, 2, 128)
    own = lax.dynamic_index_in_dim(rows, core, 2, keepdims=False).reshape(32, HALF)
    other = lax.dynamic_index_in_dim(rows, 1 - core, 2, keepdims=False).reshape(32, HALF)
    got = swap(other)
    first = jnp.where(core == 0, own, got)
    second = jnp.where(core == 0, got, own)
    return jnp.concatenate([first, second], 0)


def middle(full):
    u, v = full[:, :256], full[:, 256:512]
    r = lax.rsqrt(full[:, 512:513] * (1.0 / D) + EPS)
    c = full[:, 639:640] * (1.0 / D)
    r3c = r * r * r * c
    pre = r * u
    pre_dot = r * v - r3c * u
    s = jax.nn.sigmoid(pre)
    slope = s * (1.0 + pre * (1.0 - s))
    slope2 = s * (1.0 - s) * (2.0 + pre * (1.0 - 2.0 * s))
    act = (pre * s).astype(BF16)
    act_dot = (slope * pre_dot).astype(BF16)
    return u, v, r, c, pre_dot, slope, slope2, act, act_dot


def inner_cotangents(mid, e_full):
    e, e_dot = e_full[:, :256], e_full[:, 256:]
    pre_dot, slope, slope2 = mid[4], mid[5], mid[6]
    s = (e * slope).astype(BF16)
    s_dot = (e_dot * slope + e * slope2 * pre_dot).astype(BF16)
    return s, s_dot


def fetches(w_ref, layer, first, buf, sems):
    return [
        pltpu.make_async_copy(
            w_ref.at[layer, pl.ds(4 * i, 4), pl.ds(first, 2)],
            buf.at[pl.ds(4 * i, 4)],
            sems.at[i],
        )
        for i in range(4)
    ]


def pick(buf, i, which):
    return buf[4 * i : 4 * i + 4, which].reshape(512, RANK)


def write_sums(part_ref, u, v, s1, s2):
    lane = lax.broadcasted_iota(jnp.int32, (ROWS, 128), 1)
    part_ref[:, :256] = u
    part_ref[:, 256:512] = v
    part_ref[:, 512:] = jnp.where(lane < 64, s1, s2)


def first_kernel(x_ref, w_ref, part_ref, buf, sems):
    copies = fetches(w_ref, 0, 0, buf, sems)
    for copy in copies:
        copy.start()
    u = jnp.zeros((ROWS, RANK), F32)
    v = jnp.zeros((ROWS, RANK), F32)
    s1 = jnp.zeros((ROWS, 1), F32)
    for i in range(4):
        h = x_ref[:ROWS, 512 * i : 512 * i + 512]
        hf = h.astype(F32)
        s1 += jnp.sum(hf * hf, axis=1, keepdims=True)
        copies[i].wait()
        u += mm(h, pick(buf, i, 0))
        v += mm(h, pick(buf, i, 1))
    write_sums(part_ref, u, v, s1, jnp.zeros((ROWS, 1), F32))


def forward_kernel(
    layer, x_ref, own_ref, got_ref, w_ref, xo_ref, part_ref, buf0, buf1, sems0, sems1
):
    ends = fetches(w_ref, layer - 1, 2, buf0, sems0)
    starts = fetches(w_ref, layer, 0, buf1, sems1)
    for i in range(4):
        ends[i].start()
        starts[i].start()
    mid = middle(own_ref[...] + got_ref[...])
    act, act_dot = mid[7], mid[8]
    pair = jnp.concatenate([act, act_dot], 0)
    both = jnp.zeros((2 * ROWS, RANK), F32)
    cross = jnp.zeros((ROWS, RANK), F32)
    s1 = jnp.zeros((ROWS, 1), F32)
    s2 = jnp.zeros((ROWS, 1), F32)
    for i in range(4):
        cols = slice(512 * i, 512 * i + 512)
        ends[i].wait()
        step = mm_nt(pair, pick(buf0, i, 0))
        tail = mm_nt(act, pick(buf0, i, 1))
        h = (x_ref[:ROWS, cols].astype(F32) + step[:ROWS]).astype(BF16)
        t = (x_ref[ROWS:, cols].astype(F32) + step[ROWS:] + tail).astype(BF16)
        xo_ref[:ROWS, cols] = h
        xo_ref[ROWS:, cols] = t
        hf, tf = h.astype(F32), t.astype(F32)
        s1 += jnp.sum(hf * hf, axis=1, keepdims=True)
        s2 += jnp.sum(hf * tf, axis=1, keepdims=True)
        starts[i].wait()
        both += mm(jnp.concatenate([h, t], 0), pick(buf1, i, 0))
        cross += mm(h, pick(buf1, i, 1))
    write_sums(part_ref, both[:ROWS], both[ROWS:] + cross, s1, s2)


def seed_kernel(x_ref, own_ref, got_ref, goal_ref, w_ref, cot_ref, part_ref, buf, sems):
    ends = fetches(w_ref, LAYERS - 1, 2, buf, sems)
    for copy in ends:
        copy.start()
    mid = middle(own_ref[...] + got_ref[...])
    act, act_dot = mid[7], mid[8]
    pair = jnp.concatenate([act, act_dot], 0)
    both = jnp.zeros((2 * ROWS, RANK), F32)
    cross = jnp.zeros((ROWS, RANK), F32)
    for i in range(4):
        cols = slice(512 * i, 512 * i + 512)
        ends[i].wait()
        b, q = pick(buf, i, 0), pick(buf, i, 1)
        step = mm_nt(pair, b)
        tail = mm_nt(act, q)
        h = (x_ref[:ROWS, cols].astype(F32) + step[:ROWS]).astype(BF16)
        t = (x_ref[ROWS:, cols].astype(F32) + step[ROWS:] + tail).astype(BF16)
        d = (h.astype(F32) - goal_ref[:, cols].astype(F32)).astype(BF16)
        cot_ref[:ROWS, cols] = d
        cot_ref[ROWS:, cols] = t
        both += mm(jnp.concatenate([d, t], 0), b)
        cross += mm(d, q)
    part_ref[:, :256] = both[:ROWS]
    part_ref[:, 256:] = both[ROWS:] + cross


def backward_kernel(
    layer,
    x_ref,
    cot_ref,
    own_ref,
    got_ref,
    e_own_ref,
    e_got_ref,
    w_ref,
    out_ref,
    part_ref,
    buf0,
    buf1,
    sems0,
    sems1,
):
    ends = fetches(w_ref, layer, 0, buf0, sems0)
    starts = fetches(w_ref, layer - 1, 2, buf1, sems1)
    for i in range(4):
        ends[i].start()
        starts[i].start()
    mid = middle(own_ref[...] + got_ref[...])
    u, v, r, c = mid[:4]
    s, s_dot = inner_cotangents(mid, e_own_ref[...] + e_got_ref[...])
    pair = jnp.concatenate([s, s_dot], 0)
    sf, sdf = s.astype(F32), s_dot.astype(F32)
    mean = jnp.sum(sf * u, axis=1, keepdims=True) * (1.0 / D)
    mean_dot = jnp.sum(sf * v + sdf * u, axis=1, keepdims=True) * (1.0 / D)
    r3 = r * r * r
    r3c = r3 * c
    r3m = r3 * mean
    by_h = 3.0 * r3m * r * r * c - r3 * mean_dot
    both = jnp.zeros((2 * ROWS, RANK), F32)
    cross = jnp.zeros((ROWS, RANK), F32)
    for i in range(4):
        cols = slice(512 * i, 512 * i + 512)
        ends[i].wait()
        ms = mm_nt(pair, pick(buf0, i, 0))
        m = ms[:ROWS]
        m_dot = ms[ROWS:] + mm_nt(s, pick(buf0, i, 1))
        h, t = x_ref[:ROWS, cols].astype(F32), x_ref[ROWS:, cols].astype(F32)
        bar = r * m - r3m * h
        bar_dot = r * m_dot - r3c * m - r3m * t + by_h * h
        d = (cot_ref[:ROWS, cols].astype(F32) + bar).astype(BF16)
        d_dot = (cot_ref[ROWS:, cols].astype(F32) + bar_dot).astype(BF16)
        out_ref[:ROWS, cols] = d
        out_ref[ROWS:, cols] = d_dot
        starts[i].wait()
        both += mm(jnp.concatenate([d, d_dot], 0), pick(buf1, i, 0))
        cross += mm(d, pick(buf1, i, 1))
    part_ref[:, :256] = both[:ROWS]
    part_ref[:, 256:] = both[ROWS:] + cross


def hessian_kernel(place_ref, *refs):
    inputs, downs, ups = refs[:12], refs[12:16], refs[16:20]
    me_z, me_x = place_ref[0], place_ref[1]
    for i in range(2):
        x_ref, cot_ref, own_ref, got_ref, e_own_ref, e_got_ref = inputs[6 * i : 6 * i + 6]
        mid = middle(own_ref[...] + got_ref[...])
        r, c, act, act_dot = mid[2], mid[3], mid[7], mid[8]
        r3c = r * r * r * c
        s, s_dot = inner_cotangents(mid, e_own_ref[...] + e_got_ref[...])
        pair = jnp.concatenate([s, s_dot], 0)
        acts = jnp.concatenate([act_dot, act], 0)
        for slot_z, far_z in enumerate((0, 1, 3, 2)):
            for slot_x, far_x in enumerate((0, 1, 3, 2)):
                block = ((me_z + far_z) & 3) * 4 + ((me_x + far_x) & 3)
                cols = pl.ds(pl.multiple_of(block * 128, 128), 128)
                x = x_ref[:, cols].astype(F32)
                h, t = x[:ROWS], x[ROWS:]
                normed = jnp.concatenate(
                    [(r * t - r3c * h).astype(BF16), (r * h).astype(BF16)], 0
                )
                downs[slot_z][slot_x, i] = mm_tn(normed, pair).astype(BF16)
                ups[slot_x][slot_z, i] = mm_tn(cot_ref[:, cols], acts).astype(BF16)


VMEM = pl.BlockSpec(memory_space=pltpu.VMEM)
ANY = pl.BlockSpec(memory_space=pl.ANY)
SMEM = pl.BlockSpec(memory_space=pltpu.SMEM)
BUF = pltpu.VMEM((16, 2, 128, RANK), BF16)
SEMS = pltpu.SemaphoreType.DMA((4,))


def shape(dims, dtype):
    return jax.ShapeDtypeStruct(dims, dtype)


def call(kernel, in_specs, outs, scratch, flops, moved):
    return pl.pallas_call(
        kernel,
        in_specs=in_specs,
        out_specs=[VMEM] * len(outs),
        out_shape=outs,
        scratch_shapes=scratch,
        compiler_params=pltpu.CompilerParams(vmem_limit_bytes=40 * 1024 * 1024),
        cost_estimate=pl.CostEstimate(flops=flops, bytes_accessed=moved, transcendentals=0),
    )


def direct_scatter(slots, axis):
    own, ahead, behind, across = slots
    return (
        own.astype(F32)
        + shift(ahead, axis, 1).astype(F32)
        + shift(behind, axis, -1).astype(F32)
        + shift(across, axis, 2).astype(F32)
    )


def slots_of(value, axis_name, dim):
    me = lax.axis_index(axis_name)
    return [
        lax.dynamic_index_in_dim(value, (me + step) % 4, dim, keepdims=False)
        for step in (0, 1, 3, 2)
    ]


def sum_all(value):
    value = value + swap(value)
    for axis in ("x", "z", "y"):
        value = value + shift(value, axis, 1) + shift(value, axis, -1) + shift(value, axis, 2)
    return value


def local(tokens, targets, norm_gain, down_weight, up_weight, down_vector, up_vector):
    core = lax.axis_index("c")
    gain = norm_gain[0].astype(F32)[:, None]
    chunk = jnp.stack(
        [
            (down_weight[0].astype(F32) * gain).astype(BF16),
            (down_vector[0].astype(F32) * gain).astype(BF16),
            up_weight[0].T,
            up_vector[0].T,
        ]
    )[None]
    gathered = lax.all_gather(chunk, ("y", "z", "x"), axis=0, tiled=True)
    gathered = gathered.reshape(LAYERS, 16, 4, 128, RANK)
    h = core_rows(tokens, core)
    goal = core_rows(targets, core)
    x = jnp.concatenate([h, jnp.zeros_like(h)], 0)
    place = jnp.stack([lax.axis_index("z"), lax.axis_index("x")]).astype(jnp.int32)
    wide = shape((2 * ROWS, HALF), BF16)
    sums = shape((ROWS, 640), F32)
    e_sums = shape((ROWS, 512), F32)
    work = 6 * 2 * ROWS * HALF * RANK

    def exchanged(part):
        return part, swap(part)

    states, sides, cots, e_sides = [x], [], {}, {}
    (part,) = call(first_kernel, [VMEM, ANY], [sums], [BUF, SEMS], work // 3, 3 << 20)(x, gathered)
    sides.append(exchanged(part))
    for layer in range(1, LAYERS):
        x, part = call(
            functools.partial(forward_kernel, layer),
            [VMEM, VMEM, VMEM, ANY],
            [wide, sums],
            [BUF, BUF, SEMS, SEMS],
            work,
            5 << 20,
        )(x, *sides[-1], gathered)
        states.append(x)
        sides.append(exchanged(part))
    cot, part = call(
        seed_kernel,
        [VMEM, VMEM, VMEM, VMEM, ANY],
        [wide, e_sums],
        [BUF, SEMS],
        work,
        3 << 20,
    )(x, *sides[-1], goal, gathered)

    slot = shape((4, 2, 128, RANK), BF16)
    shares = [None, None]
    for layer in reversed(range(LAYERS)):
        cots[layer] = cot
        e_sides[layer] = exchanged(part)
        if layer > 0:
            cot, part = call(
                functools.partial(backward_kernel, layer),
                [VMEM] * 6 + [ANY],
                [wide, e_sums],
                [BUF, BUF, SEMS, SEMS],
                work,
                5 << 20,
            )(states[layer], cot, *sides[layer], *e_sides[layer], gathered)
        if layer in (2, 0):
            operands = []
            for one in (layer, layer + 1):
                operands += [states[one], cots[one], *sides[one], *e_sides[one]]
            blocks = call(
                hessian_kernel, [SMEM] + [VMEM] * 12, [slot] * 8, [], 2 * work, 6 << 20
            )(place, *operands)
            down = direct_scatter(blocks[:4], "z").astype(BF16)
            up = direct_scatter(blocks[4:], "x").astype(BF16)
            down = direct_scatter(list(down), "x").astype(BF16)
            up = direct_scatter(list(up), "z").astype(BF16)
            shares[layer // 2] = jnp.concatenate([down, up], 1)

    both = jnp.concatenate([shares[0], shares[1]], 0)
    share = direct_scatter(slots_of(both, "y", 0), "y")
    share_down = share[:128] * gain
    share_up = share[128:].T
    own_down = down_vector[0].astype(F32)
    own_up = up_vector[0].astype(F32)
    totals = jnp.stack(
        [
            jnp.sum(share_down * share_down) + jnp.sum(share_up * share_up),
            jnp.sum(own_down * share_down) + jnp.sum(own_up * share_up),
            jnp.sum(own_down * own_down) + jnp.sum(own_up * own_up),
        ]
    )
    totals = sum_all(totals)
    total_count = 2.0 * LAYERS * D * RANK
    square_mean = totals[0] / total_count
    cross_mean = totals[1] / total_count
    vector_mean = totals[2] / total_count
    scale_rms = jnp.sqrt(square_mean + EPS)
    quotient = cross_mean / (vector_mean + EPS) / TOKENS
    next_down = (share_down / scale_rms).astype(BF16)[None]
    next_up = (share_up / scale_rms).astype(BF16)[None]
    return (next_down, next_up, quotient)


def solution(mesh):
    fine = Mesh(mesh.devices.reshape(4, 4, 4, 2), ("y", "z", "x", "c"))
    fsdp = ("z", "x", "c")
    placed = (
        P(fsdp, None),
        P(fsdp, None),
        P("y", fsdp),
        P("y", fsdp, None),
        P("y", None, fsdp),
        P("y", fsdp, None),
        P("y", None, fsdp),
    )
    return jax.shard_map(
        local,
        mesh=fine,
        in_specs=placed,
        out_specs=(P("y", fsdp, None), P("y", None, fsdp), P()),
        check_vma=False,
    )
```

```python
import functools

import jax
import jax.numpy as jnp
from jax import lax
from jax.experimental import pallas as pl
from jax.experimental.pallas import tpu as pltpu
from jax.sharding import Mesh, PartitionSpec as P

EPS = 1e-06
D = 4096
RANK = 256
LAYERS = 4
TOKENS = 4096
ROWS = 64
HALF = 2048
F32 = jnp.float32
BF16 = jnp.bfloat16


def shift(value, axis, steps):
    return lax.ppermute(value, axis, [(i, (i + steps) % 4) for i in range(4)])


def swap(value):
    return lax.ppermute(value, "c", [(0, 1), (1, 0)])


def dot(left, right, dims):
    return lax.dot_general(left, right, (dims, ((), ())), preferred_element_type=F32)


def mm(left, right):
    return dot(left, right, ((1,), (0,)))


def mm_nt(left, right):
    return dot(left, right, ((1,), (1,)))


def mm_tn(left, right):
    return dot(left, right, ((0,), (0,)))


def core_rows(tokens, core):
    rows = lax.dynamic_slice_in_dim(tokens, lax.axis_index("y") * 32, 32, 0)
    rows = rows.reshape(32, 16, 2, 128)
    own = lax.dynamic_index_in_dim(rows, core, 2, keepdims=False).reshape(32, HALF)
    other = lax.dynamic_index_in_dim(rows, 1 - core, 2, keepdims=False).reshape(32, HALF)
    got = swap(other)
    first = jnp.where(core == 0, own, got)
    second = jnp.where(core == 0, got, own)
    return jnp.concatenate([first, second], 0)


def middle(full):
    u, v = full[:, :256], full[:, 256:512]
    r = lax.rsqrt(full[:, 512:513] * (1.0 / D) + EPS)
    c = full[:, 639:640] * (1.0 / D)
    r3c = r * r * r * c
    pre = r * u
    pre_dot = r * v - r3c * u
    s = jax.nn.sigmoid(pre)
    slope = s * (1.0 + pre * (1.0 - s))
    slope2 = s * (1.0 - s) * (2.0 + pre * (1.0 - 2.0 * s))
    act = (pre * s).astype(BF16)
    act_dot = (slope * pre_dot).astype(BF16)
    return u, v, r, c, pre_dot, slope, slope2, act, act_dot


def inner_cotangents(mid, e_full):
    e, e_dot = e_full[:, :256], e_full[:, 256:]
    pre_dot, slope, slope2 = mid[4], mid[5], mid[6]
    s = (e * slope).astype(BF16)
    s_dot = (e_dot * slope + e * slope2 * pre_dot).astype(BF16)
    return s, s_dot


def fetches(w_ref, layer, first, buf, sems):
    return [
        pltpu.make_async_copy(
            w_ref.at[layer, pl.ds(4 * i, 4), pl.ds(first, 2)],
            buf.at[pl.ds(4 * i, 4)],
            sems.at[i],
        )
        for i in range(4)
    ]


def pick(buf, i, which):
    return buf[4 * i : 4 * i + 4, which].reshape(512, RANK)


def write_sums(part_ref, u, v, s1, s2):
    lane = lax.broadcasted_iota(jnp.int32, (ROWS, 128), 1)
    part_ref[:, :256] = u
    part_ref[:, 256:512] = v
    part_ref[:, 512:] = jnp.where(lane < 64, s1, s2)


def first_kernel(x_ref, w_ref, part_ref, buf, sems):
    copies = fetches(w_ref, 0, 0, buf, sems)
    for copy in copies:
        copy.start()
    u = jnp.zeros((ROWS, RANK), F32)
    v = jnp.zeros((ROWS, RANK), F32)
    s1 = jnp.zeros((ROWS, 1), F32)
    for i in range(4):
        h = x_ref[:ROWS, 512 * i : 512 * i + 512]
        hf = h.astype(F32)
        s1 += jnp.sum(hf * hf, axis=1, keepdims=True)
        copies[i].wait()
        u += mm(h, pick(buf, i, 0))
        v += mm(h, pick(buf, i, 1))
    write_sums(part_ref, u, v, s1, jnp.zeros((ROWS, 1), F32))


def forward_kernel(
    layer, x_ref, own_ref, got_ref, w_ref, xo_ref, part_ref, full_ref, buf0, buf1, sems0, sems1
):
    ends = fetches(w_ref, layer - 1, 2, buf0, sems0)
    starts = fetches(w_ref, layer, 0, buf1, sems1)
    for i in range(4):
        ends[i].start()
        starts[i].start()
    full = own_ref[...] + got_ref[...]
    full_ref[...] = full
    mid = middle(full)
    act, act_dot = mid[7], mid[8]
    pair = jnp.concatenate([act, act_dot], 0)
    both = jnp.zeros((2 * ROWS, RANK), F32)
    cross = jnp.zeros((ROWS, RANK), F32)
    s1 = jnp.zeros((ROWS, 1), F32)
    s2 = jnp.zeros((ROWS, 1), F32)
    for i in range(4):
        cols = slice(512 * i, 512 * i + 512)
        ends[i].wait()
        step = mm_nt(pair, pick(buf0, i, 0))
        tail = mm_nt(act, pick(buf0, i, 1))
        h = (x_ref[:ROWS, cols].astype(F32) + step[:ROWS]).astype(BF16)
        t = (x_ref[ROWS:, cols].astype(F32) + step[ROWS:] + tail).astype(BF16)
        xo_ref[:ROWS, cols] = h
        xo_ref[ROWS:, cols] = t
        hf, tf = h.astype(F32), t.astype(F32)
        s1 += jnp.sum(hf * hf, axis=1, keepdims=True)
        s2 += jnp.sum(hf * tf, axis=1, keepdims=True)
        starts[i].wait()
        both += mm(jnp.concatenate([h, t], 0), pick(buf1, i, 0))
        cross += mm(h, pick(buf1, i, 1))
    write_sums(part_ref, both[:ROWS], both[ROWS:] + cross, s1, s2)


def seed_kernel(
    x_ref, own_ref, got_ref, goal_ref, w_ref, cot_ref, part_ref, full_ref, buf, sems
):
    ends = fetches(w_ref, LAYERS - 1, 2, buf, sems)
    for copy in ends:
        copy.start()
    full = own_ref[...] + got_ref[...]
    full_ref[...] = full
    mid = middle(full)
    act, act_dot = mid[7], mid[8]
    pair = jnp.concatenate([act, act_dot], 0)
    both = jnp.zeros((2 * ROWS, RANK), F32)
    cross = jnp.zeros((ROWS, RANK), F32)
    for i in range(4):
        cols = slice(512 * i, 512 * i + 512)
        ends[i].wait()
        b, q = pick(buf, i, 0), pick(buf, i, 1)
        step = mm_nt(pair, b)
        tail = mm_nt(act, q)
        h = (x_ref[:ROWS, cols].astype(F32) + step[:ROWS]).astype(BF16)
        t = (x_ref[ROWS:, cols].astype(F32) + step[ROWS:] + tail).astype(BF16)
        d = (h.astype(F32) - goal_ref[:, cols].astype(F32)).astype(BF16)
        cot_ref[:ROWS, cols] = d
        cot_ref[ROWS:, cols] = t
        both += mm(jnp.concatenate([d, t], 0), b)
        cross += mm(d, q)
    part_ref[:, :256] = both[:ROWS]
    part_ref[:, 256:] = both[ROWS:] + cross


def backward_kernel(
    layer,
    x_ref,
    cot_ref,
    full_ref,
    e_own_ref,
    e_got_ref,
    w_ref,
    out_ref,
    part_ref,
    e_full_ref,
    buf0,
    buf1,
    sems0,
    sems1,
):
    ends = fetches(w_ref, layer, 0, buf0, sems0)
    starts = fetches(w_ref, layer - 1, 2, buf1, sems1)
    for i in range(4):
        ends[i].start()
        starts[i].start()
    mid = middle(full_ref[...])
    u, v, r, c = mid[:4]
    e_full = e_own_ref[...] + e_got_ref[...]
    e_full_ref[...] = e_full
    s, s_dot = inner_cotangents(mid, e_full)
    pair = jnp.concatenate([s, s_dot], 0)
    sf, sdf = s.astype(F32), s_dot.astype(F32)
    mean = jnp.sum(sf * u, axis=1, keepdims=True) * (1.0 / D)
    mean_dot = jnp.sum(sf * v + sdf * u, axis=1, keepdims=True) * (1.0 / D)
    r3 = r * r * r
    r3c = r3 * c
    r3m = r3 * mean
    by_h = 3.0 * r3m * r * r * c - r3 * mean_dot
    both = jnp.zeros((2 * ROWS, RANK), F32)
    cross = jnp.zeros((ROWS, RANK), F32)
    for i in range(4):
        cols = slice(512 * i, 512 * i + 512)
        ends[i].wait()
        ms = mm_nt(pair, pick(buf0, i, 0))
        m = ms[:ROWS]
        m_dot = ms[ROWS:] + mm_nt(s, pick(buf0, i, 1))
        h, t = x_ref[:ROWS, cols].astype(F32), x_ref[ROWS:, cols].astype(F32)
        bar = r * m - r3m * h
        bar_dot = r * m_dot - r3c * m - r3m * t + by_h * h
        d = (cot_ref[:ROWS, cols].astype(F32) + bar).astype(BF16)
        d_dot = (cot_ref[ROWS:, cols].astype(F32) + bar_dot).astype(BF16)
        out_ref[:ROWS, cols] = d
        out_ref[ROWS:, cols] = d_dot
        starts[i].wait()
        both += mm(jnp.concatenate([d, d_dot], 0), pick(buf1, i, 0))
        cross += mm(d, pick(buf1, i, 1))
    part_ref[:, :256] = both[:ROWS]
    part_ref[:, 256:] = both[ROWS:] + cross


def hessian_kernel(place_ref, *refs):
    (x0, cot0, full0, e_own, e_got, x1, cot1, full1, e_full) = refs[:9]
    downs, ups = refs[9:13], refs[13:17]
    layers = (
        (x0, cot0, full0, lambda: e_own[...] + e_got[...]),
        (x1, cot1, full1, lambda: e_full[...]),
    )
    me_z, me_x = place_ref[0], place_ref[1]
    for i, (x_ref, cot_ref, full_ref, e_sum) in enumerate(layers):
        mid = middle(full_ref[...])
        r, c, act, act_dot = mid[2], mid[3], mid[7], mid[8]
        r3c = r * r * r * c
        s, s_dot = inner_cotangents(mid, e_sum())
        pair = jnp.concatenate([s, s_dot], 0)
        acts = jnp.concatenate([act_dot, act], 0)
        for slot_z, far_z in enumerate((0, 1, 3, 2)):
            for slot_x, far_x in enumerate((0, 1, 3, 2)):
                block = ((me_z + far_z) & 3) * 4 + ((me_x + far_x) & 3)
                cols = pl.ds(pl.multiple_of(block * 128, 128), 128)
                x = x_ref[:, cols].astype(F32)
                h, t = x[:ROWS], x[ROWS:]
                normed = jnp.concatenate(
                    [(r * t - r3c * h).astype(BF16), (r * h).astype(BF16)], 0
                )
                downs[slot_z][slot_x, i] = mm_tn(normed, pair).astype(BF16)
                ups[slot_x][slot_z, i] = mm_tn(cot_ref[:, cols], acts).astype(BF16)


def ring_kernel(*refs):
    groups, outs = (refs[4:8], refs[:4]), refs[8:]
    for slot in range(4):
        for group, parts in enumerate(groups):
            total = parts[0][slot].astype(F32)
            for part in parts[1:]:
                total += part[slot].astype(F32)
            outs[slot][2 * group : 2 * group + 2] = total.astype(BF16)


def layer_kernel(place_ref, *refs):
    downs, ups, outs = refs[:4], refs[4:8], refs[8:]
    for slot, far in enumerate((0, 1, 3, 2)):
        layer = (place_ref[2] + far) & 3
        for half, parts in enumerate((downs, ups)):
            total = parts[0][layer].astype(F32)
            for part in parts[1:]:
                total += part[layer].astype(F32)
            outs[slot][128 * half : 128 * half + 128] = total.astype(BF16)


def totals_kernel(b0, b1, b2, b3, gain_ref, vector_ref, share_ref, totals_ref):
    share = b0[...].astype(F32) + b1[...].astype(F32) + b2[...].astype(F32) + b3[...].astype(F32)
    share = jnp.concatenate([share[:128] * gain_ref[...], share[128:]], 0)
    share_ref[...] = share
    vector = vector_ref[...].astype(F32)
    row = lax.broadcasted_iota(jnp.int32, (8, 128), 0)
    totals = jnp.zeros((8, 128), F32)
    for i, product in enumerate((share * share, vector * share, vector * vector)):
        total = jnp.sum(jnp.sum(product, axis=0, keepdims=True), axis=1, keepdims=True)
        totals = jnp.where(row == i, total, totals)
    totals_ref[...] = totals


def output_kernel(share_ref, totals_ref, down_ref, up_ref, quotient_ref):
    means = totals_ref[...] * (1.0 / (2.0 * LAYERS * D * RANK))
    scale = 1.0 / jnp.sqrt(means[0:1, 0:1] + EPS)
    down_ref[...] = (share_ref[:128] * scale).astype(BF16)
    up_ref[...] = (share_ref[128:] * scale).T.astype(BF16)
    quotient_ref[...] = means[1:2] / (means[2:3] + EPS) * (1.0 / TOKENS)


VMEM = pl.BlockSpec(memory_space=pltpu.VMEM)
ANY = pl.BlockSpec(memory_space=pl.ANY)
SMEM = pl.BlockSpec(memory_space=pltpu.SMEM)
BUF = pltpu.VMEM((16, 2, 128, RANK), BF16)
SEMS = pltpu.SemaphoreType.DMA((4,))


def shape(dims, dtype):
    return jax.ShapeDtypeStruct(dims, dtype)


def call(kernel, in_specs, outs, scratch=(), flops=1 << 20, moved=1 << 20):
    return pl.pallas_call(
        kernel,
        in_specs=in_specs,
        out_specs=[VMEM] * len(outs),
        out_shape=outs,
        scratch_shapes=list(scratch),
        compiler_params=pltpu.CompilerParams(vmem_limit_bytes=40 * 1024 * 1024),
        cost_estimate=pl.CostEstimate(flops=flops, bytes_accessed=moved, transcendentals=0),
    )


def received(blocks, axis):
    own, ahead, behind, across = blocks
    return [own, shift(ahead, axis, 1), shift(behind, axis, -1), shift(across, axis, 2)]


def sum_all(value):
    value = value + swap(value)
    for axis in ("x", "z", "y"):
        value = value + shift(value, axis, 1) + shift(value, axis, -1) + shift(value, axis, 2)
    return value


def local(tokens, targets, norm_gain, down_weight, up_weight, down_vector, up_vector):
    core = lax.axis_index("c")
    gain = norm_gain[0].astype(F32)[:, None]
    chunk = jnp.stack(
        [
            (down_weight[0].astype(F32) * gain).astype(BF16),
            (down_vector[0].astype(F32) * gain).astype(BF16),
            up_weight[0].T,
            up_vector[0].T,
        ]
    )[None]
    gathered = lax.all_gather(chunk, ("y", "z", "x"), axis=0, tiled=True)
    gathered = gathered.reshape(LAYERS, 16, 4, 128, RANK)
    h = core_rows(tokens, core)
    goal = core_rows(targets, core)
    x = jnp.concatenate([h, jnp.zeros_like(h)], 0)
    place = jnp.stack([lax.axis_index("z"), lax.axis_index("x"), lax.axis_index("y")]).astype(jnp.int32)
    wide = shape((2 * ROWS, HALF), BF16)
    sums = shape((ROWS, 640), F32)
    e_sums = shape((ROWS, 512), F32)
    work = 6 * 2 * ROWS * HALF * RANK

    def exchanged(part):
        return part, swap(part)

    states, fulls, cots, e_fulls = [x], [], {}, {}
    (part,) = call(first_kernel, [VMEM, ANY], [sums], [BUF, SEMS], work // 3, 3 << 20)(x, gathered)
    for layer in range(1, LAYERS):
        x, part, full = call(
            functools.partial(forward_kernel, layer),
            [VMEM, VMEM, VMEM, ANY],
            [wide, sums, sums],
            [BUF, BUF, SEMS, SEMS],
            work,
            5 << 20,
        )(x, part, swap(part), gathered)
        states.append(x)
        fulls.append(full)
    cot, part, full = call(
        seed_kernel,
        [VMEM, VMEM, VMEM, VMEM, ANY],
        [wide, e_sums, sums],
        [BUF, SEMS],
        work,
        3 << 20,
    )(x, part, swap(part), goal, gathered)
    fulls.append(full)

    slot = shape((4, 2, 128, RANK), BF16)
    down_parts, up_parts = [], []
    for layer in reversed(range(LAYERS)):
        cots[layer] = cot
        e_own, e_got = part, swap(part)
        if layer > 0:
            cot, part, e_fulls[layer] = call(
                functools.partial(backward_kernel, layer),
                [VMEM] * 5 + [ANY],
                [wide, e_sums, e_sums],
                [BUF, BUF, SEMS, SEMS],
                work,
                5 << 20,
            )(states[layer], cot, fulls[layer], e_own, e_got, gathered)
        if layer in (2, 0):
            above = layer + 1
            blocks = call(
                hessian_kernel, [SMEM] + [VMEM] * 9, [slot] * 8, [], 2 * work, 6 << 20
            )(
                place,
                *(states[layer], cots[layer], fulls[layer], e_own, e_got),
                *(states[above], cots[above], fulls[above], e_fulls[above]),
            )
            down_parts += received(blocks[:4], "z")
            up_parts += received(blocks[4:], "x")

    four = shape((LAYERS, 128, RANK), BF16)
    downs = call(ring_kernel, [VMEM] * 8, [four] * 4, moved=5 << 20)(*down_parts)
    downs = received(downs, "x")
    ups = call(ring_kernel, [VMEM] * 8, [four] * 4, moved=5 << 20)(*up_parts)
    ups = received(ups, "z")
    blocks = call(
        layer_kernel, [SMEM] + [VMEM] * 8, [shape((256, RANK), BF16)] * 4, moved=2 << 20
    )(place, *downs, *ups)
    share, totals = call(
        totals_kernel,
        [VMEM] * 6,
        [shape((256, RANK), F32), shape((8, 128), F32)],
    )(*received(blocks, "y"), gain, jnp.concatenate([down_vector[0], up_vector[0].T], 0))
    totals = sum_all(totals)
    next_down, next_up, quotient = call(
        output_kernel,
        [VMEM] * 2,
        [shape((128, RANK), BF16), shape((RANK, 128), BF16), shape((1, 128), F32)],
    )(share, totals)
    return (next_down[None], next_up[None], quotient[0, 0])


def solution(mesh):
    fine = Mesh(mesh.devices.reshape(4, 4, 4, 2), ("y", "z", "x", "c"))
    fsdp = ("z", "x", "c")
    placed = (
        P(fsdp, None),
        P(fsdp, None),
        P("y", fsdp),
        P("y", fsdp, None),
        P("y", None, fsdp),
        P("y", fsdp, None),
        P("y", None, fsdp),
    )
    return jax.shard_map(
        local,
        mesh=fine,
        in_specs=placed,
        out_specs=(P("y", fsdp, None), P("y", None, fsdp), P()),
        check_vma=False,
    )
```

```python
import functools

import jax
import jax.numpy as jnp
from jax import lax
from jax.experimental import pallas as pl
from jax.experimental.pallas import tpu as pltpu
from jax.sharding import Mesh, PartitionSpec as P

EPS = 1e-06
D = 4096
RANK = 256
LAYERS = 4
TOKENS = 4096
ROWS = 64
HALF = 2048
F32 = jnp.float32
BF16 = jnp.bfloat16


def shift(value, axis, steps):
    return lax.ppermute(value, axis, [(i, (i + steps) % 4) for i in range(4)])


def swap(value):
    return lax.ppermute(value, "c", [(0, 1), (1, 0)])


def dot(left, right, dims):
    return lax.dot_general(left, right, (dims, ((), ())), preferred_element_type=F32)


def mm(left, right):
    return dot(left, right, ((1,), (0,)))


def mm_nt(left, right):
    return dot(left, right, ((1,), (1,)))


def mm_tn(left, right):
    return dot(left, right, ((0,), (0,)))


def core_rows(tokens, core):
    rows = lax.dynamic_slice_in_dim(tokens, lax.axis_index("y") * 32, 32, 0)
    rows = rows.reshape(32, 16, 2, 128)
    own = lax.dynamic_index_in_dim(rows, core, 2, keepdims=False).reshape(32, HALF)
    other = lax.dynamic_index_in_dim(rows, 1 - core, 2, keepdims=False).reshape(32, HALF)
    got = swap(other)
    first = jnp.where(core == 0, own, got)
    second = jnp.where(core == 0, got, own)
    return jnp.concatenate([first, second], 0)


def middle(full):
    u, v = full[:, :256], full[:, 256:512]
    r = lax.rsqrt(full[:, 512:513] * (1.0 / D) + EPS)
    c = full[:, 639:640] * (1.0 / D)
    r3c = r * r * r * c
    pre = r * u
    pre_dot = r * v - r3c * u
    s = jax.nn.sigmoid(pre)
    slope = s * (1.0 + pre * (1.0 - s))
    slope2 = s * (1.0 - s) * (2.0 + pre * (1.0 - 2.0 * s))
    act = (pre * s).astype(BF16)
    act_dot = (slope * pre_dot).astype(BF16)
    return u, v, r, c, pre_dot, slope, slope2, act, act_dot


def inner_cotangents(mid, e_full):
    e, e_dot = e_full[:, :256], e_full[:, 256:]
    pre_dot, slope, slope2 = mid[4], mid[5], mid[6]
    s = (e * slope).astype(BF16)
    s_dot = (e_dot * slope + e * slope2 * pre_dot).astype(BF16)
    return s, s_dot


def fetches(w_ref, layer, first, buf, sems):
    return [
        pltpu.make_async_copy(
            w_ref.at[layer, pl.ds(4 * i, 4), pl.ds(first, 2)],
            buf.at[pl.ds(4 * i, 4)],
            sems.at[i],
        )
        for i in range(4)
    ]


def pick(buf, i, which):
    return buf[4 * i : 4 * i + 4, which].reshape(512, RANK)


def write_sums(part_ref, u, v, s1, s2):
    lane = lax.broadcasted_iota(jnp.int32, (ROWS, 128), 1)
    part_ref[:, :256] = u
    part_ref[:, 256:512] = v
    part_ref[:, 512:] = jnp.where(lane < 64, s1, s2)


def first_kernel(x_ref, w_ref, part_ref, buf, sems):
    copies = fetches(w_ref, 0, 0, buf, sems)
    for copy in copies:
        copy.start()
    u = jnp.zeros((ROWS, RANK), F32)
    v = jnp.zeros((ROWS, RANK), F32)
    s1 = jnp.zeros((ROWS, 1), F32)
    for i in range(4):
        h = x_ref[:ROWS, 512 * i : 512 * i + 512]
        hf = h.astype(F32)
        s1 += jnp.sum(hf * hf, axis=1, keepdims=True)
        copies[i].wait()
        u += mm(h, pick(buf, i, 0))
        v += mm(h, pick(buf, i, 1))
    write_sums(part_ref, u, v, s1, jnp.zeros((ROWS, 1), F32))


def forward_kernel(
    layer, x_ref, own_ref, got_ref, w_ref, xo_ref, part_ref, full_ref, buf0, buf1, sems0, sems1
):
    ends = fetches(w_ref, layer - 1, 2, buf0, sems0)
    starts = fetches(w_ref, layer, 0, buf1, sems1)
    for i in range(4):
        ends[i].start()
        starts[i].start()
    full = own_ref[...] + got_ref[...]
    full_ref[...] = full
    mid = middle(full)
    act, act_dot = mid[7], mid[8]
    pair = jnp.concatenate([act, act_dot], 0)
    both = jnp.zeros((2 * ROWS, RANK), F32)
    cross = jnp.zeros((ROWS, RANK), F32)
    s1 = jnp.zeros((ROWS, 1), F32)
    s2 = jnp.zeros((ROWS, 1), F32)
    for i in range(4):
        cols = slice(512 * i, 512 * i + 512)
        ends[i].wait()
        step = mm_nt(pair, pick(buf0, i, 0))
        tail = mm_nt(act, pick(buf0, i, 1))
        h = (x_ref[:ROWS, cols].astype(F32) + step[:ROWS]).astype(BF16)
        t = (x_ref[ROWS:, cols].astype(F32) + step[ROWS:] + tail).astype(BF16)
        xo_ref[:ROWS, cols] = h
        xo_ref[ROWS:, cols] = t
        hf, tf = h.astype(F32), t.astype(F32)
        s1 += jnp.sum(hf * hf, axis=1, keepdims=True)
        s2 += jnp.sum(hf * tf, axis=1, keepdims=True)
        starts[i].wait()
        both += mm(jnp.concatenate([h, t], 0), pick(buf1, i, 0))
        cross += mm(h, pick(buf1, i, 1))
    write_sums(part_ref, both[:ROWS], both[ROWS:] + cross, s1, s2)


def seed_kernel(
    x_ref, own_ref, got_ref, goal_ref, w_ref, cot_ref, part_ref, full_ref, buf, sems
):
    ends = fetches(w_ref, LAYERS - 1, 2, buf, sems)
    for copy in ends:
        copy.start()
    full = own_ref[...] + got_ref[...]
    full_ref[...] = full
    mid = middle(full)
    act, act_dot = mid[7], mid[8]
    pair = jnp.concatenate([act, act_dot], 0)
    both = jnp.zeros((2 * ROWS, RANK), F32)
    cross = jnp.zeros((ROWS, RANK), F32)
    for i in range(4):
        cols = slice(512 * i, 512 * i + 512)
        ends[i].wait()
        b, q = pick(buf, i, 0), pick(buf, i, 1)
        step = mm_nt(pair, b)
        tail = mm_nt(act, q)
        h = (x_ref[:ROWS, cols].astype(F32) + step[:ROWS]).astype(BF16)
        t = (x_ref[ROWS:, cols].astype(F32) + step[ROWS:] + tail).astype(BF16)
        d = (h.astype(F32) - goal_ref[:, cols].astype(F32)).astype(BF16)
        cot_ref[:ROWS, cols] = d
        cot_ref[ROWS:, cols] = t
        both += mm(jnp.concatenate([d, t], 0), b)
        cross += mm(d, q)
    part_ref[:, :256] = both[:ROWS]
    part_ref[:, 256:] = both[ROWS:] + cross


def backward_kernel(
    layer,
    x_ref,
    cot_ref,
    full_ref,
    e_own_ref,
    e_got_ref,
    w_ref,
    out_ref,
    part_ref,
    e_full_ref,
    buf0,
    buf1,
    sems0,
    sems1,
):
    ends = fetches(w_ref, layer, 0, buf0, sems0)
    starts = fetches(w_ref, layer - 1, 2, buf1, sems1)
    for i in range(4):
        ends[i].start()
        starts[i].start()
    mid = middle(full_ref[...])
    u, v, r, c = mid[:4]
    e_full = e_own_ref[...] + e_got_ref[...]
    e_full_ref[...] = e_full
    s, s_dot = inner_cotangents(mid, e_full)
    pair = jnp.concatenate([s, s_dot], 0)
    sf, sdf = s.astype(F32), s_dot.astype(F32)
    mean = jnp.sum(sf * u, axis=1, keepdims=True) * (1.0 / D)
    mean_dot = jnp.sum(sf * v + sdf * u, axis=1, keepdims=True) * (1.0 / D)
    r3 = r * r * r
    r3c = r3 * c
    r3m = r3 * mean
    by_h = 3.0 * r3m * r * r * c - r3 * mean_dot
    both = jnp.zeros((2 * ROWS, RANK), F32)
    cross = jnp.zeros((ROWS, RANK), F32)
    for i in range(4):
        cols = slice(512 * i, 512 * i + 512)
        ends[i].wait()
        ms = mm_nt(pair, pick(buf0, i, 0))
        m = ms[:ROWS]
        m_dot = ms[ROWS:] + mm_nt(s, pick(buf0, i, 1))
        h, t = x_ref[:ROWS, cols].astype(F32), x_ref[ROWS:, cols].astype(F32)
        bar = r * m - r3m * h
        bar_dot = r * m_dot - r3c * m - r3m * t + by_h * h
        d = (cot_ref[:ROWS, cols].astype(F32) + bar).astype(BF16)
        d_dot = (cot_ref[ROWS:, cols].astype(F32) + bar_dot).astype(BF16)
        out_ref[:ROWS, cols] = d
        out_ref[ROWS:, cols] = d_dot
        starts[i].wait()
        both += mm(jnp.concatenate([d, d_dot], 0), pick(buf1, i, 0))
        cross += mm(d, pick(buf1, i, 1))
    part_ref[:, :256] = both[:ROWS]
    part_ref[:, 256:] = both[ROWS:] + cross


def hessian_kernel(place_ref, *refs):
    (x0, cot0, full0, e_own, e_got, x1, cot1, full1, e_full) = refs[:9]
    outs = refs[9:13] + refs[13:14], refs[14:18] + refs[18:19]
    layers = (
        (x0, cot0, full0, lambda: e_own[...] + e_got[...]),
        (x1, cot1, full1, lambda: e_full[...]),
    )
    me_z, me_x = place_ref[0], place_ref[1]
    for i, (x_ref, cot_ref, full_ref, e_sum) in enumerate(layers):
        mid = middle(full_ref[...])
        r, c, act, act_dot = mid[2], mid[3], mid[7], mid[8]
        r3c = r * r * r * c
        s, s_dot = inner_cotangents(mid, e_sum())
        pair = jnp.concatenate([s, s_dot], 0)
        acts = jnp.concatenate([act_dot, act], 0)
        for slot_z, far_z in enumerate((0, 1, 3, 2)):
            for slot_x, far_x in enumerate((0, 1, 3, 2)):
                block = ((me_z + far_z) & 3) * 4 + ((me_x + far_x) & 3)
                cols = pl.ds(pl.multiple_of(block * 128, 128), 128)
                x = x_ref[:, cols].astype(F32)
                h, t = x[:ROWS], x[ROWS:]
                normed = jnp.concatenate(
                    [(r * t - r3c * h).astype(BF16), (r * h).astype(BF16)], 0
                )
                down = mm_tn(normed, pair).astype(BF16)
                up = mm_tn(cot_ref[:, cols], acts).astype(BF16)
                for refs_, slot, inner, value in (
                    (outs[0], slot_z, slot_x, down),
                    (outs[1], slot_x, slot_z, up),
                ):
                    if slot < 3:
                        refs_[slot][inner, i] = value
                    else:
                        refs_[3 + inner // 2][inner % 2, i] = value


def step_kernel(*refs):
    for i in range(2):
        ahead, behind, first, second = refs[4 * i : 4 * i + 4]
        ahead_out, behind_out = refs[8 + 2 * i : 10 + 2 * i]
        ahead_out[:2] = (ahead[:2].astype(F32) + first[...].astype(F32)).astype(BF16)
        ahead_out[2:] = ahead[2:]
        behind_out[:2] = behind[:2]
        behind_out[2:] = (behind[2:].astype(F32) + second[...].astype(F32)).astype(BF16)


def ring_kernel(*refs):
    groups, outs = (refs[3:6], refs[:3]), refs[6:]
    for slot in range(4):
        for group, parts in enumerate(groups):
            total = parts[0][slot].astype(F32)
            for part in parts[1:]:
                total += part[slot].astype(F32)
            outs[slot][2 * group : 2 * group + 2] = total.astype(BF16)


def layer_kernel(place_ref, *refs):
    downs, ups, outs = refs[:4], refs[4:8], refs[8:]
    for slot, far in enumerate((0, 1, 3, 2)):
        layer = (place_ref[2] + far) & 3
        for half, parts in enumerate((downs, ups)):
            total = parts[0][layer].astype(F32)
            for part in parts[1:]:
                total += part[layer].astype(F32)
            outs[slot][128 * half : 128 * half + 128] = total.astype(BF16)


def totals_kernel(b0, b1, b2, b3, gain_ref, vector_ref, share_ref, totals_ref):
    share = b0[...].astype(F32) + b1[...].astype(F32) + b2[...].astype(F32) + b3[...].astype(F32)
    share = jnp.concatenate([share[:128] * gain_ref[...], share[128:]], 0)
    share_ref[...] = share
    vector = vector_ref[...].astype(F32)
    lane = lax.broadcasted_iota(jnp.int32, (1, 128), 1)
    totals = jnp.zeros((1, 128), F32)
    for i, product in enumerate((share * share, vector * share, vector * vector)):
        total = jnp.sum(jnp.sum(product, axis=0, keepdims=True), axis=1, keepdims=True)
        totals = jnp.where(lane == i, total, totals)
    totals_ref[...] = totals


def output_kernel(share_ref, totals_ref, down_ref, up_ref, quotient_ref):
    totals = jnp.sum(totals_ref[...], axis=0, keepdims=True)
    means = totals * (1.0 / (2.0 * LAYERS * D * RANK))
    scale = 1.0 / jnp.sqrt(means[:, 0:1] + EPS)
    down_ref[...] = (share_ref[:128] * scale).astype(BF16)
    up_ref[...] = (share_ref[128:] * scale).T.astype(BF16)
    quotient = means[:, 1:2] / (means[:, 2:3] + EPS) * (1.0 / TOKENS)
    quotient_ref[...] = jnp.broadcast_to(quotient, (1, 128))


VMEM = pl.BlockSpec(memory_space=pltpu.VMEM)
ANY = pl.BlockSpec(memory_space=pl.ANY)
SMEM = pl.BlockSpec(memory_space=pltpu.SMEM)
BUF = pltpu.VMEM((16, 2, 128, RANK), BF16)
SEMS = pltpu.SemaphoreType.DMA((4,))


def shape(dims, dtype):
    return jax.ShapeDtypeStruct(dims, dtype)


def call(kernel, in_specs, outs, scratch=(), flops=1 << 20, moved=1 << 20):
    return pl.pallas_call(
        kernel,
        in_specs=in_specs,
        out_specs=[VMEM] * len(outs),
        out_shape=outs,
        scratch_shapes=list(scratch),
        compiler_params=pltpu.CompilerParams(vmem_limit_bytes=40 * 1024 * 1024),
        cost_estimate=pl.CostEstimate(flops=flops, bytes_accessed=moved, transcendentals=0),
    )


def received(blocks, axis):
    own, ahead, behind, across = blocks
    return [own, shift(ahead, axis, 1), shift(behind, axis, -1), shift(across, axis, 2)]


def local(tokens, targets, norm_gain, down_weight, up_weight, down_vector, up_vector):
    core = lax.axis_index("c")
    gain = norm_gain[0].astype(F32)[:, None]
    chunk = jnp.stack(
        [
            (down_weight[0].astype(F32) * gain).astype(BF16),
            (down_vector[0].astype(F32) * gain).astype(BF16),
            up_weight[0].T,
            up_vector[0].T,
        ]
    )[None]
    gathered = lax.all_gather(chunk, ("y", "z", "x"), axis=0, tiled=True)
    gathered = gathered.reshape(LAYERS, 16, 4, 128, RANK)
    h = core_rows(tokens, core)
    goal = core_rows(targets, core)
    x = jnp.concatenate([h, jnp.zeros_like(h)], 0)
    place = jnp.stack([lax.axis_index("z"), lax.axis_index("x"), lax.axis_index("y")]).astype(jnp.int32)
    wide = shape((2 * ROWS, HALF), BF16)
    sums = shape((ROWS, 640), F32)
    e_sums = shape((ROWS, 512), F32)
    work = 6 * 2 * ROWS * HALF * RANK

    def exchanged(part):
        return part, swap(part)

    states, fulls, cots, e_fulls = [x], [], {}, {}
    (part,) = call(first_kernel, [VMEM, ANY], [sums], [BUF, SEMS], work // 3, 3 << 20)(x, gathered)
    for layer in range(1, LAYERS):
        x, part, full = call(
            functools.partial(forward_kernel, layer),
            [VMEM, VMEM, VMEM, ANY],
            [wide, sums, sums],
            [BUF, BUF, SEMS, SEMS],
            work,
            5 << 20,
        )(x, part, swap(part), gathered)
        states.append(x)
        fulls.append(full)
    cot, part, full = call(
        seed_kernel,
        [VMEM, VMEM, VMEM, VMEM, ANY],
        [wide, e_sums, sums],
        [BUF, SEMS],
        work,
        3 << 20,
    )(x, part, swap(part), goal, gathered)
    fulls.append(full)

    slot = shape((4, 2, 128, RANK), BF16)
    cut = shape((2, 2, 128, RANK), BF16)
    down_parts, up_parts = [], []
    def backward(layer, cot, e_own, e_got):
        return call(
            functools.partial(backward_kernel, layer),
            [VMEM] * 5 + [ANY],
            [wide, e_sums, e_sums],
            [BUF, BUF, SEMS, SEMS],
            work,
            5 << 20,
        )(states[layer], cot, fulls[layer], e_own, e_got, gathered)

    def hessians(layer, e_own, e_got):
        above = layer + 1
        return call(
            hessian_kernel,
            [SMEM] + [VMEM] * 9,
            [slot, slot, slot, cut, cut] * 2,
            [],
            2 * work,
            6 << 20,
        )(
            place,
            *(states[layer], cots[layer], fulls[layer], e_own, e_got),
            *(states[above], cots[above], fulls[above], e_fulls[above]),
        )

    def first_step(blocks):
        return (
            shift(blocks[3], "z", 1),
            shift(blocks[4], "z", -1),
            shift(blocks[8], "x", 1),
            shift(blocks[9], "x", -1),
        )

    def added(blocks, got):
        return call(step_kernel, [VMEM] * 8, [slot] * 4, moved=5 << 20)(
            *(blocks[1], blocks[2], got[0], got[1]), *(blocks[6], blocks[7], got[2], got[3])
        )

    def second_step(blocks, sent):
        down_parts.extend([blocks[0], shift(sent[0], "z", 1), shift(sent[1], "z", -1)])
        up_parts.extend([blocks[5], shift(sent[2], "x", 1), shift(sent[3], "x", -1)])

    cots[3] = cot
    cot, part, e_fulls[3] = backward(3, cot, part, swap(part))
    cots[2] = cot
    e_own, e_got = part, swap(part)
    blocks = hessians(2, e_own, e_got)
    cot, blocks = lax.optimization_barrier((cot, blocks))
    got = first_step(blocks)
    cot, part, e_fulls[2] = backward(2, cot, e_own, e_got)
    cots[1] = cot
    e_own, e_got = part, swap(part)
    sent = added(blocks, got)
    cot, sent = lax.optimization_barrier((cot, sent))
    second_step(blocks, sent)
    cot, part, e_fulls[1] = backward(1, cot, e_own, e_got)
    cots[0] = cot
    blocks = hessians(0, part, swap(part))
    blocks, down_parts, up_parts = lax.optimization_barrier((blocks, down_parts, up_parts))
    second_step(blocks, added(blocks, first_step(blocks)))

    four = shape((LAYERS, 128, RANK), BF16)
    downs = call(ring_kernel, [VMEM] * 6, [four] * 4, moved=5 << 20)(*down_parts)
    downs = received(downs, "x")
    ups = call(ring_kernel, [VMEM] * 6, [four] * 4, moved=5 << 20)(*up_parts)
    ups = received(ups, "z")
    blocks = call(
        layer_kernel, [SMEM] + [VMEM] * 8, [shape((256, RANK), BF16)] * 4, moved=2 << 20
    )(place, *downs, *ups)
    share, totals = call(
        totals_kernel,
        [VMEM] * 6,
        [shape((256, RANK), F32), shape((1, 128), F32)],
    )(*received(blocks, "y"), gain, jnp.concatenate([down_vector[0], up_vector[0].T], 0))
    totals = jnp.broadcast_to(totals[None], (128, 1, 128))
    totals = lax.all_to_all(totals, ("y", "z", "x", "c"), 0, 0).reshape(128, 128)
    next_down, next_up, quotient = call(
        output_kernel,
        [VMEM] * 2,
        [shape((128, RANK), BF16), shape((RANK, 128), BF16), shape((1, 128), F32)],
    )(share, totals)
    return (next_down[None], next_up[None], quotient[0, 0])


def solution(mesh):
    fine = Mesh(mesh.devices.reshape(4, 4, 4, 2), ("y", "z", "x", "c"))
    fsdp = ("z", "x", "c")
    placed = (
        P(fsdp, None),
        P(fsdp, None),
        P("y", fsdp),
        P("y", fsdp, None),
        P("y", None, fsdp),
        P("y", fsdp, None),
        P("y", None, fsdp),
    )
    return jax.shard_map(
        local,
        mesh=fine,
        in_specs=placed,
        out_specs=(P("y", fsdp, None), P("y", None, fsdp), P()),
        check_vma=False,
    )
```

```python
import functools

import jax
import jax.numpy as jnp
from jax import lax
from jax.experimental import pallas as pl
from jax.experimental.pallas import tpu as pltpu
from jax.sharding import Mesh, PartitionSpec as P

EPS = 1e-06
D = 4096
RANK = 256
LAYERS = 4
TOKENS = 4096
ROWS = 64
HALF = 2048
F32 = jnp.float32
BF16 = jnp.bfloat16


def shift(value, axis, steps):
    return lax.ppermute(value, axis, [(i, (i + steps) % 4) for i in range(4)])


def swap(value):
    return lax.ppermute(value, "c", [(0, 1), (1, 0)])


def dot(left, right, dims):
    return lax.dot_general(left, right, (dims, ((), ())), preferred_element_type=F32)


def mm(left, right):
    return dot(left, right, ((1,), (0,)))


def mm_nt(left, right):
    return dot(left, right, ((1,), (1,)))


def mm_tn(left, right):
    return dot(left, right, ((0,), (0,)))


def middle(full):
    u, v = full[:, :256], full[:, 256:512]
    r = lax.rsqrt(full[:, 512:513] * (1.0 / D) + EPS)
    c = full[:, 639:640] * (1.0 / D)
    r3c = r * r * r * c
    pre = r * u
    pre_dot = r * v - r3c * u
    s = jax.nn.sigmoid(pre)
    slope = s * (1.0 + pre * (1.0 - s))
    slope2 = s * (1.0 - s) * (2.0 + pre * (1.0 - 2.0 * s))
    act = (pre * s).astype(BF16)
    act_dot = (slope * pre_dot).astype(BF16)
    return u, v, r, c, pre_dot, slope, slope2, act, act_dot


def inner_cotangents(mid, e_full):
    e, e_dot = e_full[:, :256], e_full[:, 256:]
    pre_dot, slope, slope2 = mid[4], mid[5], mid[6]
    s = (e * slope).astype(BF16)
    s_dot = (e_dot * slope + e * slope2 * pre_dot).astype(BF16)
    return s, s_dot


FARS = (0, 3, 1, 2)


def chunk_kernel(gain_ref, down_ref, vector_ref, up_ref, up_vector_ref, chunk_ref, column_ref):
    column = jnp.broadcast_to(gain_ref[...].astype(F32), (128, 128)).T
    column_ref[...] = column
    gain = jnp.concatenate([column, column], 1)
    chunk_ref[0] = (down_ref[0].astype(F32) * gain).astype(BF16)
    chunk_ref[1] = (vector_ref[0].astype(F32) * gain).astype(BF16)
    chunk_ref[2] = up_ref[0].astype(F32).T.astype(BF16)
    chunk_ref[3] = up_vector_ref[0].astype(F32).T.astype(BF16)


def order_kernel(place_ref, own, behind, ahead, across, a_ref, b_ref):
    for far, chunk in zip(FARS, (own, behind, ahead, across)):
        layer = (place_ref[2] + far) & 3
        a_ref[layer] = chunk[:2]
        b_ref[layer] = chunk[2:]


def rows_kernel(place_ref, tokens_ref, targets_ref, keep_ref, give_ref):
    rows = pl.ds(pl.multiple_of(place_ref[2] * 32, 32), 32)
    for i, ref in enumerate((tokens_ref, targets_ref)):
        for slot_z, far_z in enumerate(FARS):
            for slot_x, far_x in enumerate(FARS):
                block = ((place_ref[0] + far_z) & 3) * 4 + ((place_ref[1] + far_x) & 3)
                slot = 4 * slot_z + slot_x
                for out_ref, core in ((keep_ref, place_ref[3]), (give_ref, 1 - place_ref[3])):
                    start = pl.multiple_of((2 * block + core) * 128, 128)
                    out_ref[i, :, 128 * slot : 128 * slot + 128] = ref[rows, pl.ds(start, 128)]


def fetch_a(refs, layer, buf, sems):
    return [
        [
            pltpu.make_async_copy(
                refs[x].at[z, layer] if x < 3 else refs[3 + z // 2].at[z % 2, layer],
                buf.at[z, x],
                sems.at[z, x],
            )
            for x in range(4)
        ]
        for z in range(4)
    ]


def fetch_b(refs, layer, buf, sems):
    return [
        [
            pltpu.make_async_copy(
                refs[z].at[x, layer] if z < 3 else refs[3 + x // 2].at[x % 2, layer],
                buf.at[z, x],
                sems.at[z, x],
            )
            for x in range(4)
        ]
        for z in range(4)
    ]


def start_all(*fetches):
    for i in range(4):
        for fetch in fetches:
            for copy in fetch[i]:
                copy.start()


def wait_all(copies):
    for copy in copies:
        copy.wait()


def pick(buf, i, which):
    return buf[i, :, which].reshape(512, RANK)


def write_sums(part_ref, u, v, s1, s2):
    lane = lax.broadcasted_iota(jnp.int32, (ROWS, 128), 1)
    part_ref[:, :256] = u
    part_ref[:, 256:512] = v
    part_ref[:, 512:] = jnp.where(lane < 64, s1, s2)


def first_kernel(x_ref, *refs):
    part_ref, buf, sems = refs[5:]
    copies = fetch_a(refs[:5], 0, buf, sems)
    start_all(copies)
    u = jnp.zeros((ROWS, RANK), F32)
    v = jnp.zeros((ROWS, RANK), F32)
    s1 = jnp.zeros((ROWS, 1), F32)
    for i in range(4):
        h = x_ref[:ROWS, 512 * i : 512 * i + 512]
        hf = h.astype(F32)
        s1 += jnp.sum(hf * hf, axis=1, keepdims=True)
        wait_all(copies[i])
        u += mm(h, pick(buf, i, 0))
        v += mm(h, pick(buf, i, 1))
    write_sums(part_ref, u, v, s1, jnp.zeros((ROWS, 1), F32))


def forward_kernel(layer, x_ref, own_ref, got_ref, *refs):
    xo_ref, part_ref, full_ref, buf0, buf1, sems0, sems1 = refs[10:]
    ends = fetch_b(refs[:5], (layer - 1) % 2, buf0, sems0)
    starts = fetch_a(refs[5:10], layer % 2, buf1, sems1)
    start_all(ends, starts)
    full = own_ref[...] + got_ref[...]
    full_ref[...] = full
    mid = middle(full)
    act, act_dot = mid[7], mid[8]
    pair = jnp.concatenate([act, act_dot], 0)
    both = jnp.zeros((2 * ROWS, RANK), F32)
    cross = jnp.zeros((ROWS, RANK), F32)
    s1 = jnp.zeros((ROWS, 1), F32)
    s2 = jnp.zeros((ROWS, 1), F32)
    for i in range(4):
        cols = slice(512 * i, 512 * i + 512)
        wait_all(ends[i])
        step = mm_nt(pair, pick(buf0, i, 0))
        tail = mm_nt(act, pick(buf0, i, 1))
        h = (x_ref[:ROWS, cols].astype(F32) + step[:ROWS]).astype(BF16)
        t = (x_ref[ROWS:, cols].astype(F32) + step[ROWS:] + tail).astype(BF16)
        xo_ref[:ROWS, cols] = h
        xo_ref[ROWS:, cols] = t
        hf, tf = h.astype(F32), t.astype(F32)
        s1 += jnp.sum(hf * hf, axis=1, keepdims=True)
        s2 += jnp.sum(hf * tf, axis=1, keepdims=True)
        wait_all(starts[i])
        both += mm(jnp.concatenate([h, t], 0), pick(buf1, i, 0))
        cross += mm(h, pick(buf1, i, 1))
    write_sums(part_ref, both[:ROWS], both[ROWS:] + cross, s1, s2)


def seed_kernel(x_ref, own_ref, got_ref, goal_ref, *refs):
    cot_ref, part_ref, full_ref, buf, sems = refs[5:]
    ends = fetch_b(refs[:5], (LAYERS - 1) % 2, buf, sems)
    start_all(ends)
    full = own_ref[...] + got_ref[...]
    full_ref[...] = full
    mid = middle(full)
    act, act_dot = mid[7], mid[8]
    pair = jnp.concatenate([act, act_dot], 0)
    both = jnp.zeros((2 * ROWS, RANK), F32)
    cross = jnp.zeros((ROWS, RANK), F32)
    for i in range(4):
        cols = slice(512 * i, 512 * i + 512)
        wait_all(ends[i])
        b, q = pick(buf, i, 0), pick(buf, i, 1)
        step = mm_nt(pair, b)
        tail = mm_nt(act, q)
        h = (x_ref[:ROWS, cols].astype(F32) + step[:ROWS]).astype(BF16)
        t = (x_ref[ROWS:, cols].astype(F32) + step[ROWS:] + tail).astype(BF16)
        d = (h.astype(F32) - goal_ref[:, cols].astype(F32)).astype(BF16)
        cot_ref[:ROWS, cols] = d
        cot_ref[ROWS:, cols] = t
        both += mm(jnp.concatenate([d, t], 0), b)
        cross += mm(d, q)
    part_ref[:, :256] = both[:ROWS]
    part_ref[:, 256:] = both[ROWS:] + cross


def backward_kernel(layer, x_ref, cot_ref, full_ref, e_own_ref, e_got_ref, *refs):
    out_ref, part_ref, e_full_ref, buf0, buf1, sems0, sems1 = refs[10:]
    ends = fetch_a(refs[:5], layer % 2, buf0, sems0)
    starts = fetch_b(refs[5:10], (layer - 1) % 2, buf1, sems1)
    start_all(ends, starts)
    mid = middle(full_ref[...])
    u, v, r, c = mid[:4]
    e_full = e_own_ref[...] + e_got_ref[...]
    e_full_ref[...] = e_full
    s, s_dot = inner_cotangents(mid, e_full)
    pair = jnp.concatenate([s, s_dot], 0)
    sf, sdf = s.astype(F32), s_dot.astype(F32)
    mean = jnp.sum(sf * u, axis=1, keepdims=True) * (1.0 / D)
    mean_dot = jnp.sum(sf * v + sdf * u, axis=1, keepdims=True) * (1.0 / D)
    r3 = r * r * r
    r3c = r3 * c
    r3m = r3 * mean
    by_h = 3.0 * r3m * r * r * c - r3 * mean_dot
    both = jnp.zeros((2 * ROWS, RANK), F32)
    cross = jnp.zeros((ROWS, RANK), F32)
    for i in range(4):
        cols = slice(512 * i, 512 * i + 512)
        wait_all(ends[i])
        ms = mm_nt(pair, pick(buf0, i, 0))
        m = ms[:ROWS]
        m_dot = ms[ROWS:] + mm_nt(s, pick(buf0, i, 1))
        h, t = x_ref[:ROWS, cols].astype(F32), x_ref[ROWS:, cols].astype(F32)
        bar = r * m - r3m * h
        bar_dot = r * m_dot - r3c * m - r3m * t + by_h * h
        d = (cot_ref[:ROWS, cols].astype(F32) + bar).astype(BF16)
        d_dot = (cot_ref[ROWS:, cols].astype(F32) + bar_dot).astype(BF16)
        out_ref[:ROWS, cols] = d
        out_ref[ROWS:, cols] = d_dot
        wait_all(starts[i])
        both += mm(jnp.concatenate([d, d_dot], 0), pick(buf1, i, 0))
        cross += mm(d, pick(buf1, i, 1))
    part_ref[:, :256] = both[:ROWS]
    part_ref[:, 256:] = both[ROWS:] + cross


def hessian_kernel(*refs):
    (x0, cot0, full0, e_own, e_got, x1, cot1, full1, e_full) = refs[:9]
    outs = refs[9:13] + refs[13:14], refs[14:18] + refs[18:19]
    layers = (
        (x0, cot0, full0, lambda: e_own[...] + e_got[...]),
        (x1, cot1, full1, lambda: e_full[...]),
    )
    for i, (x_ref, cot_ref, full_ref, e_sum) in enumerate(layers):
        mid = middle(full_ref[...])
        r, c, act, act_dot = mid[2], mid[3], mid[7], mid[8]
        r3c = r * r * r * c
        s, s_dot = inner_cotangents(mid, e_sum())
        pair = jnp.concatenate([s, s_dot], 0)
        acts = jnp.concatenate([act_dot, act], 0)
        for slot_z, z in enumerate((0, 2, 1, 3)):
            for slot_x, x_ in enumerate((0, 2, 1, 3)):
                block = 4 * z + x_
                cols = slice(128 * block, 128 * block + 128)
                x = x_ref[:, cols].astype(F32)
                h, t = x[:ROWS], x[ROWS:]
                normed = jnp.concatenate(
                    [(r * t - r3c * h).astype(BF16), (r * h).astype(BF16)], 0
                )
                down = mm_tn(normed, pair).astype(BF16)
                up = mm_tn(cot_ref[:, cols], acts).astype(BF16)
                for refs_, slot, inner, value in (
                    (outs[0], slot_z, slot_x, down),
                    (outs[1], slot_x, slot_z, up),
                ):
                    if slot < 3:
                        refs_[slot][inner, i] = value
                    else:
                        refs_[3 + inner // 2][inner % 2, i] = value


def step_kernel(*refs):
    for i in range(2):
        ahead, behind, first, second = refs[4 * i : 4 * i + 4]
        ahead_out, behind_out = refs[8 + 2 * i : 10 + 2 * i]
        ahead_out[:2] = (ahead[:2].astype(F32) + first[...].astype(F32)).astype(BF16)
        ahead_out[2:] = ahead[2:]
        behind_out[:2] = behind[:2]
        behind_out[2:] = (behind[2:].astype(F32) + second[...].astype(F32)).astype(BF16)


def ring_kernel(*refs):
    groups, outs = (refs[3:6], refs[:3]), refs[6:]
    for slot in range(4):
        for group, parts in enumerate(groups):
            total = parts[0][slot].astype(F32)
            for part in parts[1:]:
                total += part[slot].astype(F32)
            outs[slot][2 * group : 2 * group + 2] = total.astype(BF16)


def layer_kernel(place_ref, *refs):
    downs, ups, outs = refs[:4], refs[4:8], refs[8:]
    for slot, far in enumerate((0, 1, 3, 2)):
        layer = (place_ref[2] + far) & 3
        for half, parts in enumerate((downs, ups)):
            total = parts[0][layer].astype(F32)
            for part in parts[1:]:
                total += part[layer].astype(F32)
            outs[slot][128 * half : 128 * half + 128] = total.astype(BF16)


def totals_kernel(b0, b1, b2, b3, gain_ref, vector_ref, share_ref, totals_ref):
    share = b0[...].astype(F32) + b1[...].astype(F32) + b2[...].astype(F32) + b3[...].astype(F32)
    gain = jnp.concatenate([gain_ref[...], gain_ref[...]], 1)
    share = jnp.concatenate([share[:128] * gain, share[128:]], 0)
    share_ref[...] = share
    vector = vector_ref[...].astype(F32)
    lane = lax.broadcasted_iota(jnp.int32, (1, 128), 1)
    totals = jnp.zeros((1, 128), F32)
    for i, product in enumerate((share * share, vector * share, vector * vector)):
        total = jnp.sum(jnp.sum(product, axis=0, keepdims=True), axis=1, keepdims=True)
        totals = jnp.where(lane == i, total, totals)
    totals_ref[...] = totals


def output_kernel(share_ref, totals_ref, down_ref, up_ref, quotient_ref):
    totals = jnp.sum(totals_ref[...], axis=0, keepdims=True)
    means = totals * (1.0 / (2.0 * LAYERS * D * RANK))
    scale = 1.0 / jnp.sqrt(means[:, 0:1] + EPS)
    down_ref[...] = (share_ref[:128] * scale).astype(BF16)
    up_ref[...] = (share_ref[128:] * scale).T.astype(BF16)
    quotient = means[:, 1:2] / (means[:, 2:3] + EPS) * (1.0 / TOKENS)
    quotient_ref[...] = jnp.broadcast_to(quotient, (1, 128))


VMEM = pl.BlockSpec(memory_space=pltpu.VMEM)
ANY = pl.BlockSpec(memory_space=pl.ANY)
SMEM = pl.BlockSpec(memory_space=pltpu.SMEM)
BUF = pltpu.VMEM((4, 4, 2, 128, RANK), BF16)
SEMS = pltpu.SemaphoreType.DMA((4, 4))


def shape(dims, dtype):
    return jax.ShapeDtypeStruct(dims, dtype)


def call(kernel, in_specs, outs, scratch=(), flops=1 << 20, moved=1 << 20):
    return pl.pallas_call(
        kernel,
        in_specs=in_specs,
        out_specs=[VMEM] * len(outs),
        out_shape=outs,
        scratch_shapes=list(scratch),
        compiler_params=pltpu.CompilerParams(vmem_limit_bytes=40 * 1024 * 1024),
        cost_estimate=pl.CostEstimate(flops=flops, bytes_accessed=moved, transcendentals=0),
    )


def received(blocks, axis):
    own, ahead, behind, across = blocks
    return [own, shift(ahead, axis, 1), shift(behind, axis, -1), shift(across, axis, 2)]


def ring_gather(block, axis):
    behind, ahead = shift(block, axis, 1), shift(block, axis, -1)
    cut = block.shape[0] // 2
    return [block, behind, ahead, shift(behind[:cut], axis, 1), shift(ahead[cut:], axis, -1)]


def slots_stacked(parts, group):
    own, behind, ahead, *across = parts
    layers = slice(2 * group, 2 * group + 2)
    return jnp.stack([own[layers], behind[layers], ahead[layers], across[group]])


def local(tokens, targets, norm_gain, down_weight, up_weight, down_vector, up_vector):
    place = jnp.stack([lax.axis_index(axis) for axis in ("z", "x", "y", "c")]).astype(jnp.int32)
    core = place[3]
    chunk, column = call(
        chunk_kernel,
        [VMEM] * 5,
        [shape((4, 128, RANK), BF16), shape((128, 128), F32)],
    )(norm_gain, down_weight, down_vector, up_weight, up_vector)
    pair = shape((LAYERS, 2, 128, RANK), BF16)
    a_own, b_own = call(order_kernel, [SMEM] + [VMEM] * 4, [pair, pair])(
        place, chunk, shift(chunk, "y", 1), shift(chunk, "y", -1), shift(chunk, "y", 2)
    )
    a_all, b_all = ring_gather(a_own, "z"), ring_gather(b_own, "x")
    kept, given = call(
        rows_kernel, [SMEM, VMEM, VMEM], [shape((2, 32, HALF), BF16)] * 2, moved=3 << 20
    )(place, tokens, targets)
    got = swap(given)
    rows = jnp.where(
        core == 0, jnp.concatenate([kept, got], 1), jnp.concatenate([got, kept], 1)
    )
    groups = []
    for group in range(2):
        a_group = slots_stacked(a_all, group)
        b_group = slots_stacked(b_all, group)
        if not group:
            a_group, b_group, rows = lax.optimization_barrier((a_group, b_group, rows))
        else:
            a_group, b_group, groups[0] = lax.optimization_barrier(
                (a_group, b_group, groups[0])
            )
        groups.append((ring_gather(a_group, "x"), ring_gather(b_group, "z")))

    h, goal = rows[0], rows[1]
    x = jnp.concatenate([h, jnp.zeros_like(h)], 0)

    def a_of(layer):
        return groups[layer // 2][0]

    def b_of(layer):
        return groups[layer // 2][1]

    wide = shape((2 * ROWS, HALF), BF16)
    sums = shape((ROWS, 640), F32)
    e_sums = shape((ROWS, 512), F32)
    work = 6 * 2 * ROWS * HALF * RANK

    def exchanged(part):
        return part, swap(part)

    states, fulls, cots, e_fulls = [x], [], {}, {}
    (part,) = call(first_kernel, [VMEM] + [ANY] * 5, [sums], [BUF, SEMS], work // 3, 3 << 20)(
        x, *a_of(0)
    )
    for layer in range(1, LAYERS):
        x, part, full = call(
            functools.partial(forward_kernel, layer),
            [VMEM] * 3 + [ANY] * 10,
            [wide, sums, sums],
            [BUF, BUF, SEMS, SEMS],
            work,
            5 << 20,
        )(x, part, swap(part), *b_of(layer - 1), *a_of(layer))
        states.append(x)
        fulls.append(full)
    cot, part, full = call(
        seed_kernel,
        [VMEM] * 4 + [ANY] * 5,
        [wide, e_sums, sums],
        [BUF, SEMS],
        work,
        3 << 20,
    )(x, part, swap(part), goal, *b_of(LAYERS - 1))
    fulls.append(full)

    slot = shape((4, 2, 128, RANK), BF16)
    cut = shape((2, 2, 128, RANK), BF16)
    down_parts, up_parts = [], []
    def backward(layer, cot, e_own, e_got):
        return call(
            functools.partial(backward_kernel, layer),
            [VMEM] * 5 + [ANY] * 10,
            [wide, e_sums, e_sums],
            [BUF, BUF, SEMS, SEMS],
            work,
            5 << 20,
        )(states[layer], cot, fulls[layer], e_own, e_got, *a_of(layer), *b_of(layer - 1))

    def hessians(layer, e_own, e_got):
        above = layer + 1
        return call(
            hessian_kernel,
            [VMEM] * 9,
            [slot, slot, slot, cut, cut] * 2,
            [],
            2 * work,
            6 << 20,
        )(
            *(states[layer], cots[layer], fulls[layer], e_own, e_got),
            *(states[above], cots[above], fulls[above], e_fulls[above]),
        )

    def first_step(blocks):
        return (
            shift(blocks[3], "z", 1),
            shift(blocks[4], "z", -1),
            shift(blocks[8], "x", 1),
            shift(blocks[9], "x", -1),
        )

    def added(blocks, got):
        return call(step_kernel, [VMEM] * 8, [slot] * 4, moved=5 << 20)(
            *(blocks[1], blocks[2], got[0], got[1]), *(blocks[6], blocks[7], got[2], got[3])
        )

    def second_step(blocks, sent):
        down_parts.extend([blocks[0], shift(sent[0], "z", 1), shift(sent[1], "z", -1)])
        up_parts.extend([blocks[5], shift(sent[2], "x", 1), shift(sent[3], "x", -1)])

    cots[3] = cot
    cot, part, e_fulls[3] = backward(3, cot, part, swap(part))
    cots[2] = cot
    e_own, e_got = part, swap(part)
    blocks = hessians(2, e_own, e_got)
    cot, blocks = lax.optimization_barrier((cot, blocks))
    got = first_step(blocks)
    cot, part, e_fulls[2] = backward(2, cot, e_own, e_got)
    cots[1] = cot
    e_own, e_got = part, swap(part)
    got, e_got = lax.optimization_barrier((got, e_got))
    sent = added(blocks, got)
    cot, sent = lax.optimization_barrier((cot, sent))
    second_step(blocks, sent)
    cot, part, e_fulls[1] = backward(1, cot, e_own, e_got)
    cots[0] = cot
    blocks = hessians(0, part, swap(part))
    blocks, down_parts, up_parts = lax.optimization_barrier((blocks, down_parts, up_parts))
    second_step(blocks, added(blocks, first_step(blocks)))

    four = shape((LAYERS, 128, RANK), BF16)
    downs = call(ring_kernel, [VMEM] * 6, [four] * 4, moved=5 << 20)(*down_parts)
    downs = received(downs, "x")
    ups = call(ring_kernel, [VMEM] * 6, [four] * 4, moved=5 << 20)(*up_parts)
    ups = received(ups, "z")
    blocks = call(
        layer_kernel, [SMEM] + [VMEM] * 8, [shape((256, RANK), BF16)] * 4, moved=2 << 20
    )(place, *downs, *ups)
    share, totals = call(
        totals_kernel,
        [VMEM] * 6,
        [shape((256, RANK), F32), shape((1, 128), F32)],
    )(*received(blocks, "y"), column, jnp.concatenate([down_vector[0], chunk[3]], 0))
    totals = jnp.broadcast_to(totals[None], (128, 1, 128))
    totals = lax.all_to_all(totals, ("y", "z", "x", "c"), 0, 0).reshape(128, 128)
    next_down, next_up, quotient = call(
        output_kernel,
        [VMEM] * 2,
        [shape((128, RANK), BF16), shape((RANK, 128), BF16), shape((1, 128), F32)],
    )(share, totals)
    return (next_down[None], next_up[None], quotient[0, 0])


def solution(mesh):
    fine = Mesh(mesh.devices.reshape(4, 4, 4, 2), ("y", "z", "x", "c"))
    fsdp = ("z", "x", "c")
    placed = (
        P(fsdp, None),
        P(fsdp, None),
        P("y", fsdp),
        P("y", fsdp, None),
        P("y", None, fsdp),
        P("y", fsdp, None),
        P("y", None, fsdp),
    )
    return jax.shard_map(
        local,
        mesh=fine,
        in_specs=placed,
        out_specs=(P("y", fsdp, None), P("y", None, fsdp), P()),
        check_vma=False,
    )
```

```python
import functools

import jax
import jax.numpy as jnp
from jax import lax
from jax.experimental import pallas as pl
from jax.experimental.pallas import tpu as pltpu
from jax.sharding import Mesh, PartitionSpec as P

EPS = 1e-06
D = 4096
RANK = 256
LAYERS = 4
TOKENS = 4096
ROWS = 64
HALF = 2048
F32 = jnp.float32
BF16 = jnp.bfloat16


def shift(value, axis, steps):
    return lax.ppermute(value, axis, [(i, (i + steps) % 4) for i in range(4)])


def swap(value):
    return lax.ppermute(value, "c", [(0, 1), (1, 0)])


def dot(left, right, dims):
    return lax.dot_general(left, right, (dims, ((), ())), preferred_element_type=F32)


def mm(left, right):
    return dot(left, right, ((1,), (0,)))


def mm_nt(left, right):
    return dot(left, right, ((1,), (1,)))


def mm_tn(left, right):
    return dot(left, right, ((0,), (0,)))


def middle(full):
    u, v = full[:, :256], full[:, 256:512]
    r = lax.rsqrt(full[:, 512:513] * (1.0 / D) + EPS)
    c = full[:, 639:640] * (1.0 / D)
    r3c = r * r * r * c
    pre = r * u
    pre_dot = r * v - r3c * u
    s = jax.nn.sigmoid(pre)
    slope = s * (1.0 + pre * (1.0 - s))
    slope2 = s * (1.0 - s) * (2.0 + pre * (1.0 - 2.0 * s))
    act = (pre * s).astype(BF16)
    act_dot = (slope * pre_dot).astype(BF16)
    return u, v, r, c, pre_dot, slope, slope2, act, act_dot


def inner_cotangents(mid, e_full):
    e, e_dot = e_full[:, :256], e_full[:, 256:]
    pre_dot, slope, slope2 = mid[4], mid[5], mid[6]
    s = (e * slope).astype(BF16)
    s_dot = (e_dot * slope + e * slope2 * pre_dot).astype(BF16)
    return s, s_dot


FARS = (0, 3, 1, 2)


def chunk_kernel(gain_hbm, down_hbm, vector_hbm, up_hbm, up_vector_hbm, *refs):
    chunk_ref, column_ref, gain_ref, down_ref, vector_ref, up_ref, up_vector_ref, sems = refs
    copies = [
        pltpu.make_async_copy(source, target, sems.at[i])
        for i, (source, target) in enumerate(
            zip((gain_hbm, down_hbm, vector_hbm, up_hbm, up_vector_hbm), refs[2:7])
        )
    ]
    for copy in copies:
        copy.start()
    for copy in copies:
        copy.wait()
    column = jnp.broadcast_to(gain_ref[...].astype(F32), (128, 128)).T
    column_ref[...] = column
    gain = jnp.concatenate([column, column], 1)
    chunk_ref[0] = (down_ref[0].astype(F32) * gain).astype(BF16)
    chunk_ref[1] = (vector_ref[0].astype(F32) * gain).astype(BF16)
    chunk_ref[2] = up_ref[0].astype(F32).T.astype(BF16)
    chunk_ref[3] = up_vector_ref[0].astype(F32).T.astype(BF16)


def order_kernel(place_ref, own, behind, ahead, across, a_ref, b_ref):
    for far, chunk in zip(FARS, (own, behind, ahead, across)):
        layer = (place_ref[2] + far) & 3
        a_ref[layer] = chunk[:2]
        b_ref[layer] = chunk[2:]


def rows_kernel(place_ref, tokens_ref, targets_ref, keep_ref, give_ref):
    rows = pl.ds(pl.multiple_of(place_ref[2] * 32, 32), 32)
    for i, ref in enumerate((tokens_ref, targets_ref)):
        for slot_z, far_z in enumerate(FARS):
            for slot_x, far_x in enumerate(FARS):
                block = ((place_ref[0] + far_z) & 3) * 4 + ((place_ref[1] + far_x) & 3)
                slot = 4 * slot_z + slot_x
                for out_ref, core in ((keep_ref, place_ref[3]), (give_ref, 1 - place_ref[3])):
                    start = pl.multiple_of((2 * block + core) * 128, 128)
                    out_ref[i, :, 128 * slot : 128 * slot + 128] = ref[rows, pl.ds(start, 128)]


def part_a(refs, layer, i, which):
    return jnp.concatenate(
        [ref[i, layer, which] for ref in refs[:3]] + [refs[3 + i // 2][i % 2, layer, which]], 0
    )


def part_b(refs, layer, i, which):
    if i < 3:
        return refs[i][:, layer, which].reshape(512, RANK)
    return jnp.concatenate([ref[:, layer, which].reshape(256, RANK) for ref in refs[3:]], 0)


def write_sums(part_ref, u, v, s1, s2):
    lane = lax.broadcasted_iota(jnp.int32, (ROWS, 128), 1)
    part_ref[:, :256] = u
    part_ref[:, 256:512] = v
    part_ref[:, 512:] = jnp.where(lane < 64, s1, s2)


def first_kernel(x_ref, *refs):
    a, part_ref = refs[:5], refs[5]
    u = jnp.zeros((ROWS, RANK), F32)
    v = jnp.zeros((ROWS, RANK), F32)
    s1 = jnp.zeros((ROWS, 1), F32)
    for i in range(4):
        h = x_ref[:ROWS, 512 * i : 512 * i + 512]
        hf = h.astype(F32)
        s1 += jnp.sum(hf * hf, axis=1, keepdims=True)
        u += mm(h, part_a(a, 0, i, 0))
        v += mm(h, part_a(a, 0, i, 1))
    write_sums(part_ref, u, v, s1, jnp.zeros((ROWS, 1), F32))


def forward_kernel(layer, x_ref, own_ref, got_ref, *refs):
    b, a = refs[:5], refs[5:10]
    xo_ref, part_ref, full_ref = refs[10:]
    last, layer = (layer - 1) % 2, layer % 2
    full = own_ref[...] + got_ref[...]
    full_ref[...] = full
    mid = middle(full)
    act, act_dot = mid[7], mid[8]
    pair = jnp.concatenate([act, act_dot], 0)
    both = jnp.zeros((2 * ROWS, RANK), F32)
    cross = jnp.zeros((ROWS, RANK), F32)
    s1 = jnp.zeros((ROWS, 1), F32)
    s2 = jnp.zeros((ROWS, 1), F32)
    for i in range(4):
        cols = slice(512 * i, 512 * i + 512)
        step = mm_nt(pair, part_b(b, last, i, 0))
        tail = mm_nt(act, part_b(b, last, i, 1))
        h = (x_ref[:ROWS, cols].astype(F32) + step[:ROWS]).astype(BF16)
        t = (x_ref[ROWS:, cols].astype(F32) + step[ROWS:] + tail).astype(BF16)
        xo_ref[:ROWS, cols] = h
        xo_ref[ROWS:, cols] = t
        hf, tf = h.astype(F32), t.astype(F32)
        s1 += jnp.sum(hf * hf, axis=1, keepdims=True)
        s2 += jnp.sum(hf * tf, axis=1, keepdims=True)
        both += mm(jnp.concatenate([h, t], 0), part_a(a, layer, i, 0))
        cross += mm(h, part_a(a, layer, i, 1))
    write_sums(part_ref, both[:ROWS], both[ROWS:] + cross, s1, s2)


def seed_kernel(x_ref, own_ref, got_ref, goal_ref, *refs):
    cot_ref, part_ref, full_ref = refs[5:]
    full = own_ref[...] + got_ref[...]
    full_ref[...] = full
    mid = middle(full)
    act, act_dot = mid[7], mid[8]
    pair = jnp.concatenate([act, act_dot], 0)
    both = jnp.zeros((2 * ROWS, RANK), F32)
    cross = jnp.zeros((ROWS, RANK), F32)
    for i in range(4):
        cols = slice(512 * i, 512 * i + 512)
        b, q = part_b(refs[:5], 1, i, 0), part_b(refs[:5], 1, i, 1)
        step = mm_nt(pair, b)
        tail = mm_nt(act, q)
        h = (x_ref[:ROWS, cols].astype(F32) + step[:ROWS]).astype(BF16)
        t = (x_ref[ROWS:, cols].astype(F32) + step[ROWS:] + tail).astype(BF16)
        d = (h.astype(F32) - goal_ref[:, cols].astype(F32)).astype(BF16)
        cot_ref[:ROWS, cols] = d
        cot_ref[ROWS:, cols] = t
        both += mm(jnp.concatenate([d, t], 0), b)
        cross += mm(d, q)
    part_ref[:, :256] = both[:ROWS]
    part_ref[:, 256:] = both[ROWS:] + cross


def backward_kernel(layer, x_ref, cot_ref, full_ref, e_own_ref, e_got_ref, *refs):
    a, b = refs[:5], refs[5:10]
    out_ref, part_ref, e_full_ref = refs[10:]
    below, layer = (layer - 1) % 2, layer % 2
    mid = middle(full_ref[...])
    u, v, r, c = mid[:4]
    e_full = e_own_ref[...] + e_got_ref[...]
    e_full_ref[...] = e_full
    s, s_dot = inner_cotangents(mid, e_full)
    pair = jnp.concatenate([s, s_dot], 0)
    sf, sdf = s.astype(F32), s_dot.astype(F32)
    mean = jnp.sum(sf * u, axis=1, keepdims=True) * (1.0 / D)
    mean_dot = jnp.sum(sf * v + sdf * u, axis=1, keepdims=True) * (1.0 / D)
    r3 = r * r * r
    r3c = r3 * c
    r3m = r3 * mean
    by_h = 3.0 * r3m * r * r * c - r3 * mean_dot
    both = jnp.zeros((2 * ROWS, RANK), F32)
    cross = jnp.zeros((ROWS, RANK), F32)
    for i in range(4):
        cols = slice(512 * i, 512 * i + 512)
        ms = mm_nt(pair, part_a(a, layer, i, 0))
        m = ms[:ROWS]
        m_dot = ms[ROWS:] + mm_nt(s, part_a(a, layer, i, 1))
        h, t = x_ref[:ROWS, cols].astype(F32), x_ref[ROWS:, cols].astype(F32)
        bar = r * m - r3m * h
        bar_dot = r * m_dot - r3c * m - r3m * t + by_h * h
        d = (cot_ref[:ROWS, cols].astype(F32) + bar).astype(BF16)
        d_dot = (cot_ref[ROWS:, cols].astype(F32) + bar_dot).astype(BF16)
        out_ref[:ROWS, cols] = d
        out_ref[ROWS:, cols] = d_dot
        both += mm(jnp.concatenate([d, d_dot], 0), part_b(b, below, i, 0))
        cross += mm(d, part_b(b, below, i, 1))
    part_ref[:, :256] = both[:ROWS]
    part_ref[:, 256:] = both[ROWS:] + cross


def hessian_kernel(*refs):
    (x0, cot0, full0, e_own, e_got, x1, cot1, full1, e_full) = refs[:9]
    outs = refs[9:13] + refs[13:14], refs[14:18] + refs[18:19]
    layers = (
        (x0, cot0, full0, lambda: e_own[...] + e_got[...]),
        (x1, cot1, full1, lambda: e_full[...]),
    )
    for i, (x_ref, cot_ref, full_ref, e_sum) in enumerate(layers):
        mid = middle(full_ref[...])
        r, c, act, act_dot = mid[2], mid[3], mid[7], mid[8]
        r3c = r * r * r * c
        s, s_dot = inner_cotangents(mid, e_sum())
        pair = jnp.concatenate([s, s_dot], 0)
        acts = jnp.concatenate([act_dot, act], 0)
        for slot_z, z in enumerate((0, 2, 1, 3)):
            for slot_x, x_ in enumerate((0, 2, 1, 3)):
                block = 4 * z + x_
                cols = slice(128 * block, 128 * block + 128)
                x = x_ref[:, cols].astype(F32)
                h, t = x[:ROWS], x[ROWS:]
                normed = jnp.concatenate(
                    [(r * t - r3c * h).astype(BF16), (r * h).astype(BF16)], 0
                )
                down = mm_tn(normed, pair).astype(BF16)
                up = mm_tn(cot_ref[:, cols], acts).astype(BF16)
                for refs_, slot, inner, value in (
                    (outs[0], slot_z, slot_x, down),
                    (outs[1], slot_x, slot_z, up),
                ):
                    if slot < 3:
                        refs_[slot][inner, i] = value
                    else:
                        refs_[3 + inner // 2][inner % 2, i] = value


def step_kernel(*refs):
    for i in range(2):
        ahead, behind, first, second = refs[4 * i : 4 * i + 4]
        ahead_out, behind_out = refs[8 + 2 * i : 10 + 2 * i]
        ahead_out[:2] = (ahead[:2].astype(F32) + first[...].astype(F32)).astype(BF16)
        ahead_out[2:] = ahead[2:]
        behind_out[:2] = behind[:2]
        behind_out[2:] = (behind[2:].astype(F32) + second[...].astype(F32)).astype(BF16)


def ring_kernel(*refs):
    groups, outs = (refs[3:6], refs[:3]), refs[6:]
    for slot in range(4):
        for group, parts in enumerate(groups):
            total = parts[0][slot].astype(F32)
            for part in parts[1:]:
                total += part[slot].astype(F32)
            outs[slot][2 * group : 2 * group + 2] = total.astype(BF16)


def layer_kernel(place_ref, *refs):
    downs, ups, outs = refs[:4], refs[4:8], refs[8:]
    for slot, far in enumerate((0, 1, 3, 2)):
        layer = (place_ref[2] + far) & 3
        for half, parts in enumerate((downs, ups)):
            total = parts[0][layer].astype(F32)
            for part in parts[1:]:
                total += part[layer].astype(F32)
            outs[slot][128 * half : 128 * half + 128] = total.astype(BF16)


def totals_kernel(b0, b1, b2, b3, gain_ref, vector_ref, share_ref, totals_ref):
    share = b0[...].astype(F32) + b1[...].astype(F32) + b2[...].astype(F32) + b3[...].astype(F32)
    gain = jnp.concatenate([gain_ref[...], gain_ref[...]], 1)
    share = jnp.concatenate([share[:128] * gain, share[128:]], 0)
    share_ref[...] = share
    vector = vector_ref[...].astype(F32)
    lane = lax.broadcasted_iota(jnp.int32, (1, 128), 1)
    totals = jnp.zeros((1, 128), F32)
    for i, product in enumerate((share * share, vector * share, vector * vector)):
        total = jnp.sum(jnp.sum(product, axis=0, keepdims=True), axis=1, keepdims=True)
        totals = jnp.where(lane == i, total, totals)
    totals_ref[...] = totals


def output_kernel(share_ref, totals_ref, down_ref, up_ref, quotient_ref):
    totals = jnp.sum(totals_ref[...], axis=0, keepdims=True)
    means = totals * (1.0 / (2.0 * LAYERS * D * RANK))
    scale = 1.0 / jnp.sqrt(means[:, 0:1] + EPS)
    down_ref[...] = (share_ref[:128] * scale).astype(BF16)
    up_ref[...] = (share_ref[128:] * scale).T.astype(BF16)
    quotient = means[:, 1:2] / (means[:, 2:3] + EPS) * (1.0 / TOKENS)
    quotient_ref[...] = jnp.broadcast_to(quotient, (1, 128))


VMEM = pl.BlockSpec(memory_space=pltpu.VMEM)
ANY = pl.BlockSpec(memory_space=pl.ANY)
SMEM = pl.BlockSpec(memory_space=pltpu.SMEM)


def shape(dims, dtype):
    return jax.ShapeDtypeStruct(dims, dtype)


def call(kernel, in_specs, outs, flops=1 << 20, moved=1 << 20, scratch=()):
    return pl.pallas_call(
        kernel,
        in_specs=in_specs,
        out_specs=[VMEM] * len(outs),
        out_shape=outs,
        scratch_shapes=list(scratch),
        compiler_params=pltpu.CompilerParams(vmem_limit_bytes=24 * 1024 * 1024),
        cost_estimate=pl.CostEstimate(flops=flops, bytes_accessed=moved, transcendentals=0),
    )


def received(blocks, axis):
    own, ahead, behind, across = blocks
    return [own, shift(ahead, axis, 1), shift(behind, axis, -1), shift(across, axis, 2)]


def ring_gather(block, axis):
    behind, ahead = shift(block, axis, 1), shift(block, axis, -1)
    cut = block.shape[0] // 2
    return [block, behind, ahead, shift(behind[:cut], axis, 1), shift(ahead[cut:], axis, -1)]


def slots_stacked(parts, group):
    own, behind, ahead, *across = parts
    layers = slice(2 * group, 2 * group + 2)
    return jnp.stack([own[layers], behind[layers], ahead[layers], across[group]])


def local(tokens, targets, norm_gain, down_weight, up_weight, down_vector, up_vector):
    place = jnp.stack([lax.axis_index(axis) for axis in ("z", "x", "y", "c")]).astype(jnp.int32)
    core = place[3]
    chunk, column = call(
        chunk_kernel,
        [ANY] * 5,
        [shape((4, 128, RANK), BF16), shape((128, 128), F32)],
        scratch=[
            pltpu.VMEM((1, 128), BF16),
            *[pltpu.VMEM((1, 128, RANK), BF16)] * 2,
            *[pltpu.VMEM((1, RANK, 128), BF16)] * 2,
            pltpu.SemaphoreType.DMA((5,)),
        ],
    )(norm_gain, down_weight, down_vector, up_weight, up_vector)
    pair = shape((LAYERS, 2, 128, RANK), BF16)
    a_own, b_own = call(order_kernel, [SMEM] + [VMEM] * 4, [pair, pair])(
        place, chunk, shift(chunk, "y", 1), shift(chunk, "y", -1), shift(chunk, "y", 2)
    )
    a_all, b_all = ring_gather(a_own, "z"), ring_gather(b_own, "x")
    kept, given = call(
        rows_kernel, [SMEM, VMEM, VMEM], [shape((2, 32, HALF), BF16)] * 2, moved=3 << 20
    )(place, tokens, targets)
    got = swap(given)
    rows = jnp.where(
        core == 0, jnp.concatenate([kept, got], 1), jnp.concatenate([got, kept], 1)
    )
    groups = []
    for group in range(2):
        a_group = slots_stacked(a_all, group)
        b_group = slots_stacked(b_all, group)
        if not group:
            a_group, b_group, rows = lax.optimization_barrier((a_group, b_group, rows))
        else:
            a_group, b_group, groups[0] = lax.optimization_barrier(
                (a_group, b_group, groups[0])
            )
        groups.append((ring_gather(a_group, "x"), ring_gather(b_group, "z")))

    h, goal = rows[0], rows[1]
    x = jnp.concatenate([h, jnp.zeros_like(h)], 0)

    def a_of(layer):
        return groups[layer // 2][0]

    def b_of(layer):
        return groups[layer // 2][1]

    wide = shape((2 * ROWS, HALF), BF16)
    sums = shape((ROWS, 640), F32)
    e_sums = shape((ROWS, 512), F32)
    work = 6 * 2 * ROWS * HALF * RANK

    def exchanged(part):
        return part, swap(part)

    states, fulls, cots, e_fulls = [x], [], {}, {}
    (part,) = call(first_kernel, [VMEM] * 6, [sums], work // 3, 3 << 20)(
        x, *a_of(0)
    )
    for layer in range(1, LAYERS):
        x, part, full = call(
            functools.partial(forward_kernel, layer),
            [VMEM] * 13,
            [wide, sums, sums],
            work,
            5 << 20,
        )(x, part, swap(part), *b_of(layer - 1), *a_of(layer))
        states.append(x)
        fulls.append(full)
    cot, part, full = call(
        seed_kernel,
        [VMEM] * 9,
        [wide, e_sums, sums],
        work,
        3 << 20,
    )(x, part, swap(part), goal, *b_of(LAYERS - 1))
    fulls.append(full)

    slot = shape((4, 2, 128, RANK), BF16)
    cut = shape((2, 2, 128, RANK), BF16)
    down_parts, up_parts = [], []
    def backward(layer, cot, e_own, e_got):
        return call(
            functools.partial(backward_kernel, layer),
            [VMEM] * 15,
            [wide, e_sums, e_sums],
            work,
            5 << 20,
        )(states[layer], cot, fulls[layer], e_own, e_got, *a_of(layer), *b_of(layer - 1))

    def hessians(layer, e_own, e_got):
        above = layer + 1
        return call(
            hessian_kernel,
            [VMEM] * 9,
            [slot, slot, slot, cut, cut] * 2,
            2 * work,
            6 << 20,
        )(
            *(states[layer], cots[layer], fulls[layer], e_own, e_got),
            *(states[above], cots[above], fulls[above], e_fulls[above]),
        )

    def first_step(blocks):
        return (
            shift(blocks[3], "z", 1),
            shift(blocks[4], "z", -1),
            shift(blocks[8], "x", 1),
            shift(blocks[9], "x", -1),
        )

    def added(blocks, got):
        return call(step_kernel, [VMEM] * 8, [slot] * 4, moved=5 << 20)(
            *(blocks[1], blocks[2], got[0], got[1]), *(blocks[6], blocks[7], got[2], got[3])
        )

    def second_step(blocks, sent):
        down_parts.extend([blocks[0], shift(sent[0], "z", 1), shift(sent[1], "z", -1)])
        up_parts.extend([blocks[5], shift(sent[2], "x", 1), shift(sent[3], "x", -1)])

    cots[3] = cot
    cot, part, e_fulls[3] = backward(3, cot, part, swap(part))
    cots[2] = cot
    e_own, e_got = part, swap(part)
    blocks = hessians(2, e_own, e_got)
    cot, blocks = lax.optimization_barrier((cot, blocks))
    got = first_step(blocks)
    cot, part, e_fulls[2] = backward(2, cot, e_own, e_got)
    cots[1] = cot
    e_own, e_got = part, swap(part)
    got, e_got = lax.optimization_barrier((got, e_got))
    sent = added(blocks, got)
    cot, sent = lax.optimization_barrier((cot, sent))
    second_step(blocks, sent)
    cot, part, e_fulls[1] = backward(1, cot, e_own, e_got)
    cots[0] = cot
    blocks = hessians(0, part, swap(part))
    blocks, down_parts, up_parts = lax.optimization_barrier((blocks, down_parts, up_parts))
    second_step(blocks, added(blocks, first_step(blocks)))

    four = shape((LAYERS, 128, RANK), BF16)
    downs = call(ring_kernel, [VMEM] * 6, [four] * 4, moved=5 << 20)(*down_parts)
    downs = received(downs, "x")
    ups = call(ring_kernel, [VMEM] * 6, [four] * 4, moved=5 << 20)(*up_parts)
    ups = received(ups, "z")
    blocks = call(
        layer_kernel, [SMEM] + [VMEM] * 8, [shape((256, RANK), BF16)] * 4, moved=2 << 20
    )(place, *downs, *ups)
    share, totals = call(
        totals_kernel,
        [VMEM] * 6,
        [shape((256, RANK), F32), shape((1, 128), F32)],
    )(*received(blocks, "y"), column, jnp.concatenate([down_vector[0], chunk[3]], 0))
    totals = jnp.broadcast_to(totals[None], (128, 1, 128))
    totals = lax.all_to_all(totals, ("y", "z", "x", "c"), 0, 0).reshape(128, 128)
    next_down, next_up, quotient = call(
        output_kernel,
        [VMEM] * 2,
        [shape((128, RANK), BF16), shape((RANK, 128), BF16), shape((1, 128), F32)],
    )(share, totals)
    return (next_down[None], next_up[None], quotient[0, 0])


def solution(mesh):
    fine = Mesh(mesh.devices.reshape(4, 4, 4, 2), ("y", "z", "x", "c"))
    fsdp = ("z", "x", "c")
    placed = (
        P(fsdp, None),
        P(fsdp, None),
        P("y", fsdp),
        P("y", fsdp, None),
        P("y", None, fsdp),
        P("y", fsdp, None),
        P("y", None, fsdp),
    )
    return jax.shard_map(
        local,
        mesh=fine,
        in_specs=placed,
        out_specs=(P("y", fsdp, None), P("y", None, fsdp), P()),
        check_vma=False,
    )
```

```python
import functools

import jax
import jax.numpy as jnp
from jax import lax
from jax.experimental import pallas as pl
from jax.experimental.pallas import tpu as pltpu
from jax.sharding import Mesh, PartitionSpec as P

EPS = 1e-06
D = 4096
RANK = 256
LAYERS = 4
TOKENS = 4096
ROWS = 64
HALF = 2048
F32 = jnp.float32
BF16 = jnp.bfloat16


def shift(value, axis, steps):
    return lax.ppermute(value, axis, [(i, (i + steps) % 4) for i in range(4)])


def swap(value):
    return lax.ppermute(value, "c", [(0, 1), (1, 0)])


def dot(left, right, dims):
    return lax.dot_general(left, right, (dims, ((), ())), preferred_element_type=F32)


def mm(left, right):
    return dot(left, right, ((1,), (0,)))


def mm_nt(left, right):
    return dot(left, right, ((1,), (1,)))


def mm_tn(left, right):
    return dot(left, right, ((0,), (0,)))


def middle(full):
    u, v = full[:, :256], full[:, 256:512]
    r = lax.rsqrt(full[:, 512:513] * (1.0 / D) + EPS)
    c = full[:, 639:640] * (1.0 / D)
    r3c = r * r * r * c
    pre = r * u
    pre_dot = r * v - r3c * u
    s = jax.nn.sigmoid(pre)
    slope = s * (1.0 + pre * (1.0 - s))
    slope2 = s * (1.0 - s) * (2.0 + pre * (1.0 - 2.0 * s))
    act = (pre * s).astype(BF16)
    act_dot = (slope * pre_dot).astype(BF16)
    return u, v, r, c, pre_dot, slope, slope2, act, act_dot


def inner_cotangents(mid, e_full):
    e, e_dot = e_full[:, :256], e_full[:, 256:]
    pre_dot, slope, slope2 = mid[4], mid[5], mid[6]
    s = (e * slope).astype(BF16)
    s_dot = (e_dot * slope + e * slope2 * pre_dot).astype(BF16)
    return s, s_dot


FARS = (0, 3, 1, 2)


def chunk_kernel(gain_hbm, down_hbm, vector_hbm, up_hbm, up_vector_hbm, *refs):
    chunk_ref, column_ref, gain_ref, down_ref, vector_ref, up_ref, up_vector_ref, sems = refs
    copies = [
        pltpu.make_async_copy(source, target, sems.at[i])
        for i, (source, target) in enumerate(
            zip((gain_hbm, down_hbm, vector_hbm, up_hbm, up_vector_hbm), refs[2:7])
        )
    ]
    for copy in copies:
        copy.start()
    for copy in copies:
        copy.wait()
    column = jnp.broadcast_to(gain_ref[...].astype(F32), (128, 128)).T
    column_ref[...] = column
    gain = jnp.concatenate([column, column], 1)
    chunk_ref[0] = (down_ref[0].astype(F32) * gain).astype(BF16)
    chunk_ref[1] = (vector_ref[0].astype(F32) * gain).astype(BF16)
    chunk_ref[2] = up_ref[0].astype(F32).T.astype(BF16)
    chunk_ref[3] = up_vector_ref[0].astype(F32).T.astype(BF16)


def order_kernel(place_ref, own, behind, ahead, across, a_ref, b_ref):
    for far, chunk in zip(FARS, (own, behind, ahead, across)):
        layer = (place_ref[2] + far) & 3
        a_ref[layer] = chunk[:2]
        b_ref[layer] = chunk[2:]


def rows_kernel(place_ref, tokens_ref, targets_ref, keep_ref, give_ref):
    rows = pl.ds(pl.multiple_of(place_ref[2] * 32, 32), 32)
    for i, ref in enumerate((tokens_ref, targets_ref)):
        for slot_z, far_z in enumerate(FARS):
            for slot_x, far_x in enumerate(FARS):
                block = ((place_ref[0] + far_z) & 3) * 4 + ((place_ref[1] + far_x) & 3)
                slot = 4 * slot_z + slot_x
                for out_ref, core in ((keep_ref, place_ref[3]), (give_ref, 1 - place_ref[3])):
                    start = pl.multiple_of((2 * block + core) * 128, 128)
                    out_ref[i, :, 128 * slot : 128 * slot + 128] = ref[rows, pl.ds(start, 128)]


def part_a(refs, layer, i, which):
    return jnp.concatenate(
        [ref[i, layer, which] for ref in refs[:3]] + [refs[3 + i // 2][i % 2, layer, which]], 0
    )


def part_b(refs, layer, i, which):
    if i < 3:
        return refs[i][:, layer, which].reshape(512, RANK)
    return jnp.concatenate([ref[:, layer, which].reshape(256, RANK) for ref in refs[3:]], 0)


def write_sums(part_ref, u, v, s1, s2):
    lane = lax.broadcasted_iota(jnp.int32, (ROWS, 128), 1)
    part_ref[:, :256] = u
    part_ref[:, 256:512] = v
    part_ref[:, 512:] = jnp.where(lane < 64, s1, s2)


def first_kernel(x_ref, *refs):
    a, part_ref = refs[:5], refs[5]
    u = jnp.zeros((ROWS, RANK), F32)
    v = jnp.zeros((ROWS, RANK), F32)
    s1 = jnp.zeros((ROWS, 1), F32)
    for i in range(4):
        h = x_ref[:ROWS, 512 * i : 512 * i + 512]
        hf = h.astype(F32)
        s1 += jnp.sum(hf * hf, axis=1, keepdims=True)
        u += mm(h, part_a(a, 0, i, 0))
        v += mm(h, part_a(a, 0, i, 1))
    write_sums(part_ref, u, v, s1, jnp.zeros((ROWS, 1), F32))


def forward_kernel(layer, x_ref, own_ref, got_ref, *refs):
    b, a = refs[:5], refs[5:10]
    xo_ref, part_ref, full_ref = refs[10:]
    last, layer = (layer - 1) % 2, layer % 2
    full = own_ref[...] + got_ref[...]
    full_ref[...] = full
    mid = middle(full)
    act, act_dot = mid[7], mid[8]
    pair = jnp.concatenate([act, act_dot], 0)
    both = jnp.zeros((2 * ROWS, RANK), F32)
    cross = jnp.zeros((ROWS, RANK), F32)
    s1 = jnp.zeros((ROWS, 1), F32)
    s2 = jnp.zeros((ROWS, 1), F32)
    for i in range(4):
        cols = slice(512 * i, 512 * i + 512)
        step = mm_nt(pair, part_b(b, last, i, 0))
        tail = mm_nt(act, part_b(b, last, i, 1))
        h = (x_ref[:ROWS, cols].astype(F32) + step[:ROWS]).astype(BF16)
        t = (x_ref[ROWS:, cols].astype(F32) + step[ROWS:] + tail).astype(BF16)
        xo_ref[:ROWS, cols] = h
        xo_ref[ROWS:, cols] = t
        hf, tf = h.astype(F32), t.astype(F32)
        s1 += jnp.sum(hf * hf, axis=1, keepdims=True)
        s2 += jnp.sum(hf * tf, axis=1, keepdims=True)
        both += mm(jnp.concatenate([h, t], 0), part_a(a, layer, i, 0))
        cross += mm(h, part_a(a, layer, i, 1))
    write_sums(part_ref, both[:ROWS], both[ROWS:] + cross, s1, s2)


def seed_kernel(x_ref, own_ref, got_ref, goal_ref, *refs):
    cot_ref, part_ref, full_ref = refs[5:]
    full = own_ref[...] + got_ref[...]
    full_ref[...] = full
    mid = middle(full)
    act, act_dot = mid[7], mid[8]
    pair = jnp.concatenate([act, act_dot], 0)
    both = jnp.zeros((2 * ROWS, RANK), F32)
    cross = jnp.zeros((ROWS, RANK), F32)
    for i in range(4):
        cols = slice(512 * i, 512 * i + 512)
        b, q = part_b(refs[:5], 1, i, 0), part_b(refs[:5], 1, i, 1)
        step = mm_nt(pair, b)
        tail = mm_nt(act, q)
        h = (x_ref[:ROWS, cols].astype(F32) + step[:ROWS]).astype(BF16)
        t = (x_ref[ROWS:, cols].astype(F32) + step[ROWS:] + tail).astype(BF16)
        d = (h.astype(F32) - goal_ref[:, cols].astype(F32)).astype(BF16)
        cot_ref[:ROWS, cols] = d
        cot_ref[ROWS:, cols] = t
        both += mm(jnp.concatenate([d, t], 0), b)
        cross += mm(d, q)
    part_ref[:, :256] = both[:ROWS]
    part_ref[:, 256:] = both[ROWS:] + cross


def backward_kernel(layer, x_ref, cot_ref, full_ref, e_own_ref, e_got_ref, *refs):
    a, b = refs[:5], refs[5:10]
    out_ref, part_ref, e_full_ref = refs[10:]
    below, layer = (layer - 1) % 2, layer % 2
    mid = middle(full_ref[...])
    u, v, r, c = mid[:4]
    e_full = e_own_ref[...] + e_got_ref[...]
    e_full_ref[...] = e_full
    s, s_dot = inner_cotangents(mid, e_full)
    pair = jnp.concatenate([s, s_dot], 0)
    sf, sdf = s.astype(F32), s_dot.astype(F32)
    mean = jnp.sum(sf * u, axis=1, keepdims=True) * (1.0 / D)
    mean_dot = jnp.sum(sf * v + sdf * u, axis=1, keepdims=True) * (1.0 / D)
    r3 = r * r * r
    r3c = r3 * c
    r3m = r3 * mean
    by_h = 3.0 * r3m * r * r * c - r3 * mean_dot
    both = jnp.zeros((2 * ROWS, RANK), F32)
    cross = jnp.zeros((ROWS, RANK), F32)
    for i in range(4):
        cols = slice(512 * i, 512 * i + 512)
        ms = mm_nt(pair, part_a(a, layer, i, 0))
        m = ms[:ROWS]
        m_dot = ms[ROWS:] + mm_nt(s, part_a(a, layer, i, 1))
        h, t = x_ref[:ROWS, cols].astype(F32), x_ref[ROWS:, cols].astype(F32)
        bar = r * m - r3m * h
        bar_dot = r * m_dot - r3c * m - r3m * t + by_h * h
        d = (cot_ref[:ROWS, cols].astype(F32) + bar).astype(BF16)
        d_dot = (cot_ref[ROWS:, cols].astype(F32) + bar_dot).astype(BF16)
        out_ref[:ROWS, cols] = d
        out_ref[ROWS:, cols] = d_dot
        both += mm(jnp.concatenate([d, d_dot], 0), part_b(b, below, i, 0))
        cross += mm(d, part_b(b, below, i, 1))
    part_ref[:, :256] = both[:ROWS]
    part_ref[:, 256:] = both[ROWS:] + cross


def hessian_kernel(*refs):
    (x0, cot0, full0, e_own, e_got, x1, cot1, full1, e_full) = refs[:9]
    outs = refs[9:13] + refs[13:14], refs[14:18] + refs[18:19]
    layers = (
        (x0, cot0, full0, lambda: e_own[...] + e_got[...]),
        (x1, cot1, full1, lambda: e_full[...]),
    )
    for i, (x_ref, cot_ref, full_ref, e_sum) in enumerate(layers):
        mid = middle(full_ref[...])
        r, c, act, act_dot = mid[2], mid[3], mid[7], mid[8]
        r3c = r * r * r * c
        s, s_dot = inner_cotangents(mid, e_sum())
        pair = jnp.concatenate([s, s_dot], 0)
        acts = jnp.concatenate([act_dot, act], 0)
        for slot_z, z in enumerate((0, 2, 1, 3)):
            for slot_x, x_ in enumerate((0, 2, 1, 3)):
                block = 4 * z + x_
                cols = slice(128 * block, 128 * block + 128)
                x = x_ref[:, cols].astype(F32)
                h, t = x[:ROWS], x[ROWS:]
                normed = jnp.concatenate(
                    [(r * t - r3c * h).astype(BF16), (r * h).astype(BF16)], 0
                )
                down = mm_tn(normed, pair).astype(BF16)
                up = mm_tn(cot_ref[:, cols], acts).astype(BF16)
                for refs_, slot, inner, value in (
                    (outs[0], slot_z, slot_x, down),
                    (outs[1], slot_x, slot_z, up),
                ):
                    if slot < 3:
                        refs_[slot][inner, i] = value
                    else:
                        refs_[3 + inner // 2][inner % 2, i] = value


def step_kernel(*refs):
    for i in range(2):
        ahead, behind, first, second = refs[4 * i : 4 * i + 4]
        ahead_out, behind_out = refs[8 + 2 * i : 10 + 2 * i]
        ahead_out[:2] = (ahead[:2].astype(F32) + first[...].astype(F32)).astype(BF16)
        ahead_out[2:] = ahead[2:]
        behind_out[:2] = behind[:2]
        behind_out[2:] = (behind[2:].astype(F32) + second[...].astype(F32)).astype(BF16)


def ring_kernel(*refs):
    groups, outs = (refs[3:6], refs[:3]), refs[6:]
    for slot in range(4):
        for group, parts in enumerate(groups):
            total = parts[0][slot].astype(F32)
            for part in parts[1:]:
                total += part[slot].astype(F32)
            outs[slot][2 * group : 2 * group + 2] = total.astype(BF16)


def layer_kernel(place_ref, *refs):
    downs, ups, outs = refs[:4], refs[4:8], refs[8:]
    for slot, far in enumerate((0, 1, 3, 2)):
        layer = (place_ref[2] + far) & 3
        for half, parts in enumerate((downs, ups)):
            total = parts[0][layer].astype(F32)
            for part in parts[1:]:
                total += part[layer].astype(F32)
            outs[slot][128 * half : 128 * half + 128] = total.astype(BF16)


def totals_kernel(b0, b1, b2, b3, gain_ref, vector_ref, share_ref, totals_ref):
    share = b0[...].astype(F32) + b1[...].astype(F32) + b2[...].astype(F32) + b3[...].astype(F32)
    gain = jnp.concatenate([gain_ref[...], gain_ref[...]], 1)
    share = jnp.concatenate([share[:128] * gain, share[128:]], 0)
    share_ref[...] = share
    vector = vector_ref[...].astype(F32)
    lane = lax.broadcasted_iota(jnp.int32, (1, 128), 1)
    totals = jnp.zeros((1, 128), F32)
    for i, product in enumerate((share * share, vector * share, vector * vector)):
        total = jnp.sum(jnp.sum(product, axis=0, keepdims=True), axis=1, keepdims=True)
        totals = jnp.where(lane == i, total, totals)
    totals_ref[...] = totals


def output_kernel(share_ref, totals_ref, down_ref, up_ref, quotient_ref):
    totals = jnp.sum(totals_ref[...], axis=0, keepdims=True)
    means = totals * (1.0 / (2.0 * LAYERS * D * RANK))
    scale = 1.0 / jnp.sqrt(means[:, 0:1] + EPS)
    down_ref[...] = (share_ref[:128] * scale).astype(BF16)
    up_ref[...] = (share_ref[128:] * scale).T.astype(BF16)
    quotient = means[:, 1:2] / (means[:, 2:3] + EPS) * (1.0 / TOKENS)
    quotient_ref[...] = jnp.broadcast_to(quotient, (1, 128))


VMEM = pl.BlockSpec(memory_space=pltpu.VMEM)
ANY = pl.BlockSpec(memory_space=pl.ANY)
SMEM = pl.BlockSpec(memory_space=pltpu.SMEM)


def shape(dims, dtype):
    return jax.ShapeDtypeStruct(dims, dtype)


def call(kernel, in_specs, outs, flops=1 << 20, moved=1 << 20, scratch=()):
    return pl.pallas_call(
        kernel,
        in_specs=in_specs,
        out_specs=[VMEM] * len(outs),
        out_shape=outs,
        scratch_shapes=list(scratch),
        compiler_params=pltpu.CompilerParams(vmem_limit_bytes=24 * 1024 * 1024),
        cost_estimate=pl.CostEstimate(flops=flops, bytes_accessed=moved, transcendentals=0),
    )


def received(blocks, axis):
    own, ahead, behind, across = blocks
    return [own, shift(ahead, axis, 1), shift(behind, axis, -1), shift(across, axis, 2)]


def ring_near(block, axis):
    return shift(block, axis, 1), shift(block, axis, -1)


def ring_far(behind, ahead, axis):
    cut = behind.shape[0] // 2
    return shift(behind[:cut], axis, 1), shift(ahead[cut:], axis, -1)


def ring_gather(block, axis):
    near = ring_near(block, axis)
    return [block, *near, *ring_far(*near, axis)]


def slots_stacked(parts, group):
    own, behind, ahead, *across = parts
    layers = slice(2 * group, 2 * group + 2)
    return jnp.stack([own[layers], behind[layers], ahead[layers], across[group]])


def local(tokens, targets, norm_gain, down_weight, up_weight, down_vector, up_vector):
    place = jnp.stack([lax.axis_index(axis) for axis in ("z", "x", "y", "c")]).astype(jnp.int32)
    core = place[3]
    chunk, column = call(
        chunk_kernel,
        [ANY] * 5,
        [shape((4, 128, RANK), BF16), shape((128, 128), F32)],
        scratch=[
            pltpu.VMEM((1, 128), BF16),
            *[pltpu.VMEM((1, 128, RANK), BF16)] * 2,
            *[pltpu.VMEM((1, RANK, 128), BF16)] * 2,
            pltpu.SemaphoreType.DMA((5,)),
        ],
    )(norm_gain, down_weight, down_vector, up_weight, up_vector)
    pair = shape((LAYERS, 2, 128, RANK), BF16)
    a_own, b_own = call(order_kernel, [SMEM] + [VMEM] * 4, [pair, pair])(
        place, chunk, shift(chunk, "y", 1), shift(chunk, "y", -1), shift(chunk, "y", 2)
    )
    a_all, b_all = ring_gather(a_own, "z"), ring_gather(b_own, "x")
    kept, given = call(
        rows_kernel, [SMEM, VMEM, VMEM], [shape((2, 32, HALF), BF16)] * 2, moved=3 << 20
    )(place, tokens, targets)
    got = swap(given)
    rows = jnp.where(
        core == 0, jnp.concatenate([kept, got], 1), jnp.concatenate([got, kept], 1)
    )
    a_group, b_group = slots_stacked(a_all, 0), slots_stacked(b_all, 0)
    a_group, b_group, rows = lax.optimization_barrier((a_group, b_group, rows))
    groups = [(ring_gather(a_group, "x"), ring_gather(b_group, "z"))]
    a_group, b_group = slots_stacked(a_all, 1), slots_stacked(b_all, 1)
    a_group, b_group, groups[0] = lax.optimization_barrier((a_group, b_group, groups[0]))
    a_near, b_near = ring_near(a_group, "x"), ring_near(b_group, "z")
    h, goal = rows[0], rows[1]
    x = jnp.concatenate([h, jnp.zeros_like(h)], 0)

    def a_of(layer):
        return groups[layer // 2][0]

    def b_of(layer):
        return groups[layer // 2][1]

    wide = shape((2 * ROWS, HALF), BF16)
    sums = shape((ROWS, 640), F32)
    e_sums = shape((ROWS, 512), F32)
    work = 6 * 2 * ROWS * HALF * RANK

    def exchanged(part):
        return part, swap(part)

    states, fulls, cots, e_fulls = [x], [], {}, {}
    (part,) = call(first_kernel, [VMEM] * 6, [sums], work // 3, 3 << 20)(
        x, *a_of(0)
    )
    for layer in range(1, LAYERS):
        x, part, full = call(
            functools.partial(forward_kernel, layer),
            [VMEM] * 13,
            [wide, sums, sums],
            work,
            5 << 20,
        )(x, part, swap(part), *b_of(layer - 1), *a_of(layer))
        states.append(x)
        fulls.append(full)
        if layer == 1:
            part, a_near, b_near = lax.optimization_barrier((part, a_near, b_near))
            groups.append(
                (
                    [a_group, *a_near, *ring_far(*a_near, "x")],
                    [b_group, *b_near, *ring_far(*b_near, "z")],
                )
            )
    cot, part, full = call(
        seed_kernel,
        [VMEM] * 9,
        [wide, e_sums, sums],
        work,
        3 << 20,
    )(x, part, swap(part), goal, *b_of(LAYERS - 1))
    fulls.append(full)

    slot = shape((4, 2, 128, RANK), BF16)
    cut = shape((2, 2, 128, RANK), BF16)
    down_parts, up_parts = [], []
    def backward(layer, cot, e_own, e_got):
        return call(
            functools.partial(backward_kernel, layer),
            [VMEM] * 15,
            [wide, e_sums, e_sums],
            work,
            5 << 20,
        )(states[layer], cot, fulls[layer], e_own, e_got, *a_of(layer), *b_of(layer - 1))

    def hessians(layer, e_own, e_got):
        above = layer + 1
        return call(
            hessian_kernel,
            [VMEM] * 9,
            [slot, slot, slot, cut, cut] * 2,
            2 * work,
            6 << 20,
        )(
            *(states[layer], cots[layer], fulls[layer], e_own, e_got),
            *(states[above], cots[above], fulls[above], e_fulls[above]),
        )

    def first_step(blocks):
        return (
            shift(blocks[3], "z", 1),
            shift(blocks[4], "z", -1),
            shift(blocks[8], "x", 1),
            shift(blocks[9], "x", -1),
        )

    def added(blocks, got):
        return call(step_kernel, [VMEM] * 8, [slot] * 4, moved=5 << 20)(
            *(blocks[1], blocks[2], got[0], got[1]), *(blocks[6], blocks[7], got[2], got[3])
        )

    def second_step(blocks, sent):
        down_parts.extend([blocks[0], shift(sent[0], "z", 1), shift(sent[1], "z", -1)])
        up_parts.extend([blocks[5], shift(sent[2], "x", 1), shift(sent[3], "x", -1)])

    cots[3] = cot
    cot, part, e_fulls[3] = backward(3, cot, part, swap(part))
    cots[2] = cot
    e_own, e_got = part, swap(part)
    blocks = hessians(2, e_own, e_got)
    cot, blocks = lax.optimization_barrier((cot, blocks))
    got = first_step(blocks)
    cot, part, e_fulls[2] = backward(2, cot, e_own, e_got)
    cots[1] = cot
    e_own, e_got = part, swap(part)
    got, e_got = lax.optimization_barrier((got, e_got))
    sent = added(blocks, got)
    cot, sent = lax.optimization_barrier((cot, sent))
    second_step(blocks, sent)
    cot, part, e_fulls[1] = backward(1, cot, e_own, e_got)
    cots[0] = cot
    blocks = hessians(0, part, swap(part))
    blocks, down_parts, up_parts = lax.optimization_barrier((blocks, down_parts, up_parts))
    second_step(blocks, added(blocks, first_step(blocks)))

    four = shape((LAYERS, 128, RANK), BF16)
    downs = call(ring_kernel, [VMEM] * 6, [four] * 4, moved=5 << 20)(*down_parts)
    downs = received(downs, "x")
    ups = call(ring_kernel, [VMEM] * 6, [four] * 4, moved=5 << 20)(*up_parts)
    ups = received(ups, "z")
    blocks = call(
        layer_kernel, [SMEM] + [VMEM] * 8, [shape((256, RANK), BF16)] * 4, moved=2 << 20
    )(place, *downs, *ups)
    share, totals = call(
        totals_kernel,
        [VMEM] * 6,
        [shape((256, RANK), F32), shape((1, 128), F32)],
    )(*received(blocks, "y"), column, jnp.concatenate([down_vector[0], chunk[3]], 0))
    totals = jnp.broadcast_to(totals[None], (128, 1, 128))
    totals = lax.all_to_all(totals, ("y", "z", "x", "c"), 0, 0).reshape(128, 128)
    next_down, next_up, quotient = call(
        output_kernel,
        [VMEM] * 2,
        [shape((128, RANK), BF16), shape((RANK, 128), BF16), shape((1, 128), F32)],
    )(share, totals)
    return (next_down[None], next_up[None], quotient[0, 0])


def solution(mesh):
    fine = Mesh(mesh.devices.reshape(4, 4, 4, 2), ("y", "z", "x", "c"))
    fsdp = ("z", "x", "c")
    placed = (
        P(fsdp, None),
        P(fsdp, None),
        P("y", fsdp),
        P("y", fsdp, None),
        P("y", None, fsdp),
        P("y", fsdp, None),
        P("y", None, fsdp),
    )
    return jax.shard_map(
        local,
        mesh=fine,
        in_specs=placed,
        out_specs=(P("y", fsdp, None), P("y", None, fsdp), P()),
        check_vma=False,
    )
```

```python
import functools

import jax
import jax.numpy as jnp
from jax import lax
from jax.experimental import pallas as pl
from jax.experimental.pallas import tpu as pltpu
from jax.sharding import Mesh, PartitionSpec as P

EPS = 1e-06
D = 4096
RANK = 256
LAYERS = 4
TOKENS = 4096
ROWS = 64
HALF = 2048
F32 = jnp.float32
BF16 = jnp.bfloat16


def shift(value, axis, steps):
    return lax.ppermute(value, axis, [(i, (i + steps) % 4) for i in range(4)])


def swap(value):
    return lax.ppermute(value, "c", [(0, 1), (1, 0)])


def dot(left, right, dims):
    return lax.dot_general(left, right, (dims, ((), ())), preferred_element_type=F32)


def mm(left, right):
    return dot(left, right, ((1,), (0,)))


def mm_nt(left, right):
    return dot(left, right, ((1,), (1,)))


def mm_tn(left, right):
    return dot(left, right, ((0,), (0,)))


def middle(full):
    u, v = full[:, :256], full[:, 256:512]
    r = lax.rsqrt(full[:, 512:513] * (1.0 / D) + EPS)
    c = full[:, 639:640] * (1.0 / D)
    r3c = r * r * r * c
    pre = r * u
    pre_dot = r * v - r3c * u
    s = jax.nn.sigmoid(pre)
    slope = s * (1.0 + pre * (1.0 - s))
    slope2 = s * (1.0 - s) * (2.0 + pre * (1.0 - 2.0 * s))
    act = (pre * s).astype(BF16)
    act_dot = (slope * pre_dot).astype(BF16)
    return u, v, r, c, pre_dot, slope, slope2, act, act_dot


def inner_cotangents(mid, e_full):
    e, e_dot = e_full[:, :256], e_full[:, 256:]
    pre_dot, slope, slope2 = mid[4], mid[5], mid[6]
    s = (e * slope).astype(BF16)
    s_dot = (e_dot * slope + e * slope2 * pre_dot).astype(BF16)
    return s, s_dot


FARS = (0, 3, 1, 2)


def chunk_kernel(gain_hbm, down_hbm, vector_hbm, up_hbm, up_vector_hbm, *refs):
    chunk_ref, column_ref, gain_ref, down_ref, vector_ref, up_ref, up_vector_ref, sems = refs
    copies = [
        pltpu.make_async_copy(source, target, sems.at[i])
        for i, (source, target) in enumerate(
            zip((gain_hbm, down_hbm, vector_hbm, up_hbm, up_vector_hbm), refs[2:7])
        )
    ]
    for copy in copies:
        copy.start()
    for copy in copies:
        copy.wait()
    column = jnp.broadcast_to(gain_ref[...].astype(F32), (128, 128)).T
    column_ref[...] = column
    gain = jnp.concatenate([column, column], 1)
    chunk_ref[0] = (down_ref[0].astype(F32) * gain).astype(BF16)
    chunk_ref[1] = (vector_ref[0].astype(F32) * gain).astype(BF16)
    chunk_ref[2] = up_ref[0].astype(F32).T.astype(BF16)
    chunk_ref[3] = up_vector_ref[0].astype(F32).T.astype(BF16)


def order_kernel(place_ref, own, behind, ahead, across, a_ref, b_ref):
    for far, chunk in zip(FARS, (own, behind, ahead, across)):
        layer = (place_ref[2] + far) & 3
        a_ref[layer] = chunk[:2]
        b_ref[layer] = chunk[2:]


def rows_kernel(place_ref, tokens_ref, targets_ref, keep_ref, give_ref):
    rows = pl.ds(pl.multiple_of(place_ref[2] * 32, 32), 32)
    for i, ref in enumerate((tokens_ref, targets_ref)):
        for slot_z, far_z in enumerate(FARS):
            for slot_x, far_x in enumerate(FARS):
                block = ((place_ref[0] + far_z) & 3) * 4 + ((place_ref[1] + far_x) & 3)
                slot = 4 * slot_z + slot_x
                for out_ref, core in ((keep_ref, place_ref[3]), (give_ref, 1 - place_ref[3])):
                    start = pl.multiple_of((2 * block + core) * 128, 128)
                    out_ref[i, :, 128 * slot : 128 * slot + 128] = ref[rows, pl.ds(start, 128)]


def part_a(refs, layer, i, which):
    return jnp.concatenate(
        [ref[i, layer, which] for ref in refs[:3]] + [refs[3 + i // 2][i % 2, layer, which]], 0
    )


def part_b(refs, layer, i, which):
    if i < 3:
        return refs[i][:, layer, which].reshape(512, RANK)
    return jnp.concatenate([ref[:, layer, which].reshape(256, RANK) for ref in refs[3:]], 0)


def write_sums(part_ref, u, v, s1, s2):
    lane = lax.broadcasted_iota(jnp.int32, (ROWS, 128), 1)
    part_ref[:, :256] = u
    part_ref[:, 256:512] = v
    part_ref[:, 512:] = jnp.where(lane < 64, s1, s2)


def first_kernel(x_ref, *refs):
    a, part_ref = refs[:5], refs[5]
    u = jnp.zeros((ROWS, RANK), F32)
    v = jnp.zeros((ROWS, RANK), F32)
    s1 = jnp.zeros((ROWS, 1), F32)
    for i in range(4):
        h = x_ref[:ROWS, 512 * i : 512 * i + 512]
        hf = h.astype(F32)
        s1 += jnp.sum(hf * hf, axis=1, keepdims=True)
        u += mm(h, part_a(a, 0, i, 0))
        v += mm(h, part_a(a, 0, i, 1))
    write_sums(part_ref, u, v, s1, jnp.zeros((ROWS, 1), F32))


def forward_kernel(layer, x_ref, own_ref, got_ref, *refs):
    b, a = refs[:5], refs[5:10]
    xo_ref, part_ref, full_ref = refs[10:]
    last, layer = (layer - 1) % 2, layer % 2
    full = own_ref[...] + got_ref[...]
    full_ref[...] = full
    mid = middle(full)
    act, act_dot = mid[7], mid[8]
    pair = jnp.concatenate([act, act_dot], 0)
    both = jnp.zeros((2 * ROWS, RANK), F32)
    cross = jnp.zeros((ROWS, RANK), F32)
    s1 = jnp.zeros((ROWS, 1), F32)
    s2 = jnp.zeros((ROWS, 1), F32)
    for i in range(4):
        cols = slice(512 * i, 512 * i + 512)
        step = mm_nt(pair, part_b(b, last, i, 0))
        tail = mm_nt(act, part_b(b, last, i, 1))
        h = (x_ref[:ROWS, cols].astype(F32) + step[:ROWS]).astype(BF16)
        t = (x_ref[ROWS:, cols].astype(F32) + step[ROWS:] + tail).astype(BF16)
        xo_ref[:ROWS, cols] = h
        xo_ref[ROWS:, cols] = t
        hf, tf = h.astype(F32), t.astype(F32)
        s1 += jnp.sum(hf * hf, axis=1, keepdims=True)
        s2 += jnp.sum(hf * tf, axis=1, keepdims=True)
        both += mm(jnp.concatenate([h, t], 0), part_a(a, layer, i, 0))
        cross += mm(h, part_a(a, layer, i, 1))
    write_sums(part_ref, both[:ROWS], both[ROWS:] + cross, s1, s2)


def seed_kernel(x_ref, own_ref, got_ref, goal_ref, *refs):
    cot_ref, part_ref, full_ref = refs[5:]
    full = own_ref[...] + got_ref[...]
    full_ref[...] = full
    mid = middle(full)
    act, act_dot = mid[7], mid[8]
    pair = jnp.concatenate([act, act_dot], 0)
    both = jnp.zeros((2 * ROWS, RANK), F32)
    cross = jnp.zeros((ROWS, RANK), F32)
    for i in range(4):
        cols = slice(512 * i, 512 * i + 512)
        b, q = part_b(refs[:5], 1, i, 0), part_b(refs[:5], 1, i, 1)
        step = mm_nt(pair, b)
        tail = mm_nt(act, q)
        h = (x_ref[:ROWS, cols].astype(F32) + step[:ROWS]).astype(BF16)
        t = (x_ref[ROWS:, cols].astype(F32) + step[ROWS:] + tail).astype(BF16)
        d = (h.astype(F32) - goal_ref[:, cols].astype(F32)).astype(BF16)
        cot_ref[:ROWS, cols] = d
        cot_ref[ROWS:, cols] = t
        both += mm(jnp.concatenate([d, t], 0), b)
        cross += mm(d, q)
    part_ref[:, :256] = both[:ROWS]
    part_ref[:, 256:] = both[ROWS:] + cross


def backward_kernel(layer, x_ref, cot_ref, full_ref, e_own_ref, e_got_ref, *refs):
    a, b = refs[:5], refs[5:10]
    out_ref, part_ref, e_full_ref = refs[10:]
    below, layer = (layer - 1) % 2, layer % 2
    mid = middle(full_ref[...])
    u, v, r, c = mid[:4]
    e_full = e_own_ref[...] + e_got_ref[...]
    e_full_ref[...] = e_full
    s, s_dot = inner_cotangents(mid, e_full)
    pair = jnp.concatenate([s, s_dot], 0)
    sf, sdf = s.astype(F32), s_dot.astype(F32)
    mean = jnp.sum(sf * u, axis=1, keepdims=True) * (1.0 / D)
    mean_dot = jnp.sum(sf * v + sdf * u, axis=1, keepdims=True) * (1.0 / D)
    r3 = r * r * r
    r3c = r3 * c
    r3m = r3 * mean
    by_h = 3.0 * r3m * r * r * c - r3 * mean_dot
    both = jnp.zeros((2 * ROWS, RANK), F32)
    cross = jnp.zeros((ROWS, RANK), F32)
    for i in range(4):
        cols = slice(512 * i, 512 * i + 512)
        ms = mm_nt(pair, part_a(a, layer, i, 0))
        m = ms[:ROWS]
        m_dot = ms[ROWS:] + mm_nt(s, part_a(a, layer, i, 1))
        h, t = x_ref[:ROWS, cols].astype(F32), x_ref[ROWS:, cols].astype(F32)
        bar = r * m - r3m * h
        bar_dot = r * m_dot - r3c * m - r3m * t + by_h * h
        d = (cot_ref[:ROWS, cols].astype(F32) + bar).astype(BF16)
        d_dot = (cot_ref[ROWS:, cols].astype(F32) + bar_dot).astype(BF16)
        out_ref[:ROWS, cols] = d
        out_ref[ROWS:, cols] = d_dot
        both += mm(jnp.concatenate([d, d_dot], 0), part_b(b, below, i, 0))
        cross += mm(d, part_b(b, below, i, 1))
    part_ref[:, :256] = both[:ROWS]
    part_ref[:, 256:] = both[ROWS:] + cross


def hessian_layers(refs):
    e_own, e_got = refs[15:17]
    for layer in range(LAYERS):
        if layer == 0:
            x_ref, cot_ref, full_ref = refs[12:15]
            e_full = e_own[...] + e_got[...]
        else:
            x_ref, cot_ref, full_ref, e_ref = refs[4 * layer - 4 : 4 * layer]
            e_full = e_ref[...]
        mid = middle(full_ref[...])
        r, c, act, act_dot = mid[2], mid[3], mid[7], mid[8]
        pair = jnp.concatenate(inner_cotangents(mid, e_full), 0)
        acts = jnp.concatenate([act_dot, act], 0)
        yield layer, x_ref, cot_ref, r, r * r * r * c, pair, acts


def columns(slot_z, slot_x):
    order = (0, 2, 1, 3)
    block = 4 * order[slot_z] + order[slot_x]
    return slice(128 * block, 128 * block + 128)


def down_block(x_ref, cols, r, r3c, pair):
    x = x_ref[:, cols].astype(F32)
    h, t = x[:ROWS], x[ROWS:]
    normed = jnp.concatenate([(r * t - r3c * h).astype(BF16), (r * h).astype(BF16)], 0)
    return mm_tn(normed, pair).astype(BF16)


def far_kernel(*refs):
    outs = refs[17:]
    for layer, x_ref, cot_ref, r, r3c, pair, acts in hessian_layers(refs):
        for inner in range(4):
            cols = columns(3, inner)
            outs[inner // 2][inner % 2, layer] = down_block(x_ref, cols, r, r3c, pair)
            up = mm_tn(cot_ref[:, columns(inner, 3)], acts)
            outs[2 + inner // 2][inner % 2, layer] = up.astype(BF16)


def near_kernel(*refs):
    outs = refs[17:]
    for layer, x_ref, cot_ref, r, r3c, pair, acts in hessian_layers(refs):
        for slot in range(3):
            for inner in range(4):
                cols = columns(slot, inner)
                outs[slot][inner, layer] = down_block(x_ref, cols, r, r3c, pair)
                up = mm_tn(cot_ref[:, columns(inner, slot)], acts)
                outs[3 + slot][inner, layer] = up.astype(BF16)


def step_kernel(*refs):
    for i in range(2):
        ahead, behind, first, second = refs[4 * i : 4 * i + 4]
        ahead_out, behind_out = refs[8 + 2 * i : 10 + 2 * i]
        ahead_out[:2] = (ahead[:2].astype(F32) + first[...].astype(F32)).astype(BF16)
        ahead_out[2:] = ahead[2:]
        behind_out[:2] = behind[:2]
        behind_out[2:] = (behind[2:].astype(F32) + second[...].astype(F32)).astype(BF16)


def ring_kernel(own, behind, ahead, *outs):
    for slot in range(4):
        total = own[slot].astype(F32) + behind[slot].astype(F32) + ahead[slot].astype(F32)
        outs[slot][...] = total.astype(BF16)


def layer_kernel(place_ref, *refs):
    downs, ups, outs = refs[:4], refs[4:8], refs[8:]
    for slot, far in enumerate((0, 1, 3, 2)):
        layer = (place_ref[2] + far) & 3
        for half, parts in enumerate((downs, ups)):
            total = parts[0][layer].astype(F32)
            for part in parts[1:]:
                total += part[layer].astype(F32)
            outs[slot][128 * half : 128 * half + 128] = total.astype(BF16)


def totals_kernel(b0, b1, b2, b3, gain_ref, vector_ref, share_ref, totals_ref):
    share = b0[...].astype(F32) + b1[...].astype(F32) + b2[...].astype(F32) + b3[...].astype(F32)
    gain = jnp.concatenate([gain_ref[...], gain_ref[...]], 1)
    share = jnp.concatenate([share[:128] * gain, share[128:]], 0)
    share_ref[...] = share
    vector = vector_ref[...].astype(F32)
    lane = lax.broadcasted_iota(jnp.int32, (1, 128), 1)
    totals = jnp.zeros((1, 128), F32)
    for i, product in enumerate((share * share, vector * share, vector * vector)):
        total = jnp.sum(jnp.sum(product, axis=0, keepdims=True), axis=1, keepdims=True)
        totals = jnp.where(lane == i, total, totals)
    totals_ref[...] = totals


def output_kernel(share_ref, totals_ref, down_ref, up_ref, quotient_ref):
    totals = jnp.sum(totals_ref[...], axis=0, keepdims=True)
    means = totals * (1.0 / (2.0 * LAYERS * D * RANK))
    scale = 1.0 / jnp.sqrt(means[:, 0:1] + EPS)
    down_ref[...] = (share_ref[:128] * scale).astype(BF16)
    up_ref[...] = (share_ref[128:] * scale).T.astype(BF16)
    quotient = means[:, 1:2] / (means[:, 2:3] + EPS) * (1.0 / TOKENS)
    quotient_ref[...] = jnp.broadcast_to(quotient, (1, 128))


VMEM = pl.BlockSpec(memory_space=pltpu.VMEM)
ANY = pl.BlockSpec(memory_space=pl.ANY)
SMEM = pl.BlockSpec(memory_space=pltpu.SMEM)


def shape(dims, dtype):
    return jax.ShapeDtypeStruct(dims, dtype)


def call(kernel, in_specs, outs, flops=1 << 20, moved=1 << 20, scratch=()):
    return pl.pallas_call(
        kernel,
        in_specs=in_specs,
        out_specs=[VMEM] * len(outs),
        out_shape=outs,
        scratch_shapes=list(scratch),
        compiler_params=pltpu.CompilerParams(vmem_limit_bytes=24 * 1024 * 1024),
        cost_estimate=pl.CostEstimate(flops=flops, bytes_accessed=moved, transcendentals=0),
    )


def received(blocks, axis):
    own, ahead, behind, across = blocks
    return [own, shift(ahead, axis, 1), shift(behind, axis, -1), shift(across, axis, 2)]


def ring_near(block, axis):
    return shift(block, axis, 1), shift(block, axis, -1)


def ring_far(behind, ahead, axis):
    cut = behind.shape[0] // 2
    return shift(behind[:cut], axis, 1), shift(ahead[cut:], axis, -1)


def ring_gather(block, axis):
    near = ring_near(block, axis)
    return [block, *near, *ring_far(*near, axis)]


def slots_stacked(parts, group):
    own, behind, ahead, *across = parts
    layers = slice(2 * group, 2 * group + 2)
    return jnp.stack([own[layers], behind[layers], ahead[layers], across[group]])


def local(tokens, targets, norm_gain, down_weight, up_weight, down_vector, up_vector):
    place = jnp.stack([lax.axis_index(axis) for axis in ("z", "x", "y", "c")]).astype(jnp.int32)
    core = place[3]
    chunk, column = call(
        chunk_kernel,
        [ANY] * 5,
        [shape((4, 128, RANK), BF16), shape((128, 128), F32)],
        scratch=[
            pltpu.VMEM((1, 128), BF16),
            *[pltpu.VMEM((1, 128, RANK), BF16)] * 2,
            *[pltpu.VMEM((1, RANK, 128), BF16)] * 2,
            pltpu.SemaphoreType.DMA((5,)),
        ],
    )(norm_gain, down_weight, down_vector, up_weight, up_vector)
    pair = shape((LAYERS, 2, 128, RANK), BF16)
    a_own, b_own = call(order_kernel, [SMEM] + [VMEM] * 4, [pair, pair])(
        place, chunk, shift(chunk, "y", 1), shift(chunk, "y", -1), shift(chunk, "y", 2)
    )
    a_all, b_all = ring_gather(a_own, "z"), ring_gather(b_own, "x")
    kept, given = call(
        rows_kernel, [SMEM, VMEM, VMEM], [shape((2, 32, HALF), BF16)] * 2, moved=3 << 20
    )(place, tokens, targets)
    got = swap(given)
    rows = jnp.where(
        core == 0, jnp.concatenate([kept, got], 1), jnp.concatenate([got, kept], 1)
    )
    a_group, b_group = slots_stacked(a_all, 0), slots_stacked(b_all, 0)
    a_group, b_group, rows = lax.optimization_barrier((a_group, b_group, rows))
    groups = [(ring_gather(a_group, "x"), ring_gather(b_group, "z"))]
    a_group, b_group = slots_stacked(a_all, 1), slots_stacked(b_all, 1)
    a_group, b_group, groups[0] = lax.optimization_barrier((a_group, b_group, groups[0]))
    a_near, b_near = ring_near(a_group, "x"), ring_near(b_group, "z")
    h, goal = rows[0], rows[1]
    x = jnp.concatenate([h, jnp.zeros_like(h)], 0)

    def a_of(layer):
        return groups[layer // 2][0]

    def b_of(layer):
        return groups[layer // 2][1]

    wide = shape((2 * ROWS, HALF), BF16)
    sums = shape((ROWS, 640), F32)
    e_sums = shape((ROWS, 512), F32)
    work = 6 * 2 * ROWS * HALF * RANK

    def exchanged(part):
        return part, swap(part)

    states, fulls, cots, e_fulls = [x], [], {}, {}
    (part,) = call(first_kernel, [VMEM] * 6, [sums], work // 3, 3 << 20)(
        x, *a_of(0)
    )
    for layer in range(1, LAYERS):
        x, part, full = call(
            functools.partial(forward_kernel, layer),
            [VMEM] * 13,
            [wide, sums, sums],
            work,
            5 << 20,
        )(x, part, swap(part), *b_of(layer - 1), *a_of(layer))
        states.append(x)
        fulls.append(full)
        if layer == 1:
            part, a_near, b_near = lax.optimization_barrier((part, a_near, b_near))
            groups.append(
                (
                    [a_group, *a_near, *ring_far(*a_near, "x")],
                    [b_group, *b_near, *ring_far(*b_near, "z")],
                )
            )
    cot, part, full = call(
        seed_kernel,
        [VMEM] * 9,
        [wide, e_sums, sums],
        work,
        3 << 20,
    )(x, part, swap(part), goal, *b_of(LAYERS - 1))
    fulls.append(full)

    def backward(layer, cot, e_own, e_got):
        return call(
            functools.partial(backward_kernel, layer),
            [VMEM] * 15,
            [wide, e_sums, e_sums],
            work,
            5 << 20,
        )(states[layer], cot, fulls[layer], e_own, e_got, *a_of(layer), *b_of(layer - 1))

    operands = []
    for layer in (3, 2, 1):
        cots[layer] = cot
        cot, part, e_fulls[layer] = backward(layer, cot, part, swap(part))
    for layer in (1, 2, 3):
        operands += [states[layer], cots[layer], fulls[layer], e_fulls[layer]]
    operands += [states[0], cot, fulls[0], part, swap(part)]

    slot = shape((4, LAYERS, 128, RANK), BF16)
    cut = shape((2, LAYERS, 128, RANK), BF16)
    four = shape((LAYERS, 128, RANK), BF16)
    far = call(far_kernel, [VMEM] * 17, [cut] * 4, work, 6 << 20)(*operands)
    far = (
        shift(far[0], "z", 1),
        shift(far[1], "z", -1),
        shift(far[2], "x", 1),
        shift(far[3], "x", -1),
    )
    near = call(near_kernel, [VMEM] * 17, [slot] * 6, 3 * work, 10 << 20)(*operands)
    sent = call(step_kernel, [VMEM] * 8, [slot] * 4, moved=10 << 20)(
        *(near[1], near[2], far[0], far[1]), *(near[4], near[5], far[2], far[3])
    )
    down_parts = near[0], shift(sent[0], "z", 1), shift(sent[1], "z", -1)
    up_parts = near[3], shift(sent[2], "x", 1), shift(sent[3], "x", -1)
    downs = call(ring_kernel, [VMEM] * 3, [four] * 4, moved=4 << 20)(*down_parts)
    downs = received(downs, "x")
    ups = call(ring_kernel, [VMEM] * 3, [four] * 4, moved=4 << 20)(*up_parts)
    ups = received(ups, "z")
    blocks = call(
        layer_kernel, [SMEM] + [VMEM] * 8, [shape((256, RANK), BF16)] * 4, moved=2 << 20
    )(place, *downs, *ups)
    share, totals = call(
        totals_kernel,
        [VMEM] * 6,
        [shape((256, RANK), F32), shape((1, 128), F32)],
    )(*received(blocks, "y"), column, jnp.concatenate([down_vector[0], chunk[3]], 0))
    totals = jnp.broadcast_to(totals[None], (128, 1, 128))
    totals = lax.all_to_all(totals, ("y", "z", "x", "c"), 0, 0).reshape(128, 128)
    next_down, next_up, quotient = call(
        output_kernel,
        [VMEM] * 2,
        [shape((128, RANK), BF16), shape((RANK, 128), BF16), shape((1, 128), F32)],
    )(share, totals)
    return (next_down[None], next_up[None], quotient[0, 0])


def solution(mesh):
    fine = Mesh(mesh.devices.reshape(4, 4, 4, 2), ("y", "z", "x", "c"))
    fsdp = ("z", "x", "c")
    placed = (
        P(fsdp, None),
        P(fsdp, None),
        P("y", fsdp),
        P("y", fsdp, None),
        P("y", None, fsdp),
        P("y", fsdp, None),
        P("y", None, fsdp),
    )
    return jax.shard_map(
        local,
        mesh=fine,
        in_specs=placed,
        out_specs=(P("y", fsdp, None), P("y", None, fsdp), P()),
        check_vma=False,
    )
```

```python
import functools

import jax
import jax.numpy as jnp
from jax import lax
from jax.experimental import pallas as pl
from jax.experimental.pallas import tpu as pltpu
from jax.sharding import Mesh, PartitionSpec as P

EPS = 1e-06
D = 4096
RANK = 256
LAYERS = 4
TOKENS = 4096
ROWS = 64
HALF = 2048
F32 = jnp.float32
BF16 = jnp.bfloat16


def shift(value, axis, steps):
    return lax.ppermute(value, axis, [(i, (i + steps) % 4) for i in range(4)])


def swap(value):
    return lax.ppermute(value, "c", [(0, 1), (1, 0)])


def dot(left, right, dims):
    return lax.dot_general(left, right, (dims, ((), ())), preferred_element_type=F32)


def mm(left, right):
    return dot(left, right, ((1,), (0,)))


def mm_nt(left, right):
    return dot(left, right, ((1,), (1,)))


def mm_tn(left, right):
    return dot(left, right, ((0,), (0,)))


def middle(full):
    u, v = full[:, :256], full[:, 256:512]
    r = lax.rsqrt(full[:, 512:513] * (1.0 / D) + EPS)
    c = full[:, 639:640] * (1.0 / D)
    r3c = r * r * r * c
    pre = r * u
    pre_dot = r * v - r3c * u
    s = jax.nn.sigmoid(pre)
    slope = s * (1.0 + pre * (1.0 - s))
    slope2 = s * (1.0 - s) * (2.0 + pre * (1.0 - 2.0 * s))
    act = (pre * s).astype(BF16)
    act_dot = (slope * pre_dot).astype(BF16)
    return u, v, r, c, pre_dot, slope, slope2, act, act_dot


def inner_cotangents(mid, e_full):
    e, e_dot = e_full[:, :256], e_full[:, 256:]
    pre_dot, slope, slope2 = mid[4], mid[5], mid[6]
    s = (e * slope).astype(BF16)
    s_dot = (e_dot * slope + e * slope2 * pre_dot).astype(BF16)
    return s, s_dot


FARS = (0, 3, 1, 2)


def chunk_kernel(gain_hbm, down_hbm, vector_hbm, up_hbm, up_vector_hbm, *refs):
    chunk_ref, column_ref, gain_ref, down_ref, vector_ref, up_ref, up_vector_ref, sems = refs
    copies = [
        pltpu.make_async_copy(source, target, sems.at[i])
        for i, (source, target) in enumerate(
            zip((gain_hbm, down_hbm, vector_hbm, up_hbm, up_vector_hbm), refs[2:7])
        )
    ]
    for copy in copies:
        copy.start()
    for copy in copies:
        copy.wait()
    column = jnp.broadcast_to(gain_ref[...].astype(F32), (128, 128)).T
    column_ref[...] = column
    gain = jnp.concatenate([column, column], 1)
    chunk_ref[0] = (down_ref[0].astype(F32) * gain).astype(BF16)
    chunk_ref[1] = (vector_ref[0].astype(F32) * gain).astype(BF16)
    chunk_ref[2] = up_ref[0].astype(F32).T.astype(BF16)
    chunk_ref[3] = up_vector_ref[0].astype(F32).T.astype(BF16)


def order_kernel(place_ref, own, behind, ahead, across, a_ref, b_ref):
    for far, chunk in zip(FARS, (own, behind, ahead, across)):
        layer = (place_ref[2] + far) & 3
        a_ref[layer] = chunk[:2]
        b_ref[layer] = chunk[2:]


def rows_kernel(place_ref, tokens_ref, targets_ref, keep_ref, give_ref):
    rows = pl.ds(pl.multiple_of(place_ref[2] * 32, 32), 32)
    for i, ref in enumerate((tokens_ref, targets_ref)):
        for slot_z, far_z in enumerate(FARS):
            for slot_x, far_x in enumerate(FARS):
                block = ((place_ref[0] + far_z) & 3) * 4 + ((place_ref[1] + far_x) & 3)
                slot = 4 * slot_z + slot_x
                for out_ref, core in ((keep_ref, place_ref[3]), (give_ref, 1 - place_ref[3])):
                    start = pl.multiple_of((2 * block + core) * 128, 128)
                    out_ref[i, :, 128 * slot : 128 * slot + 128] = ref[rows, pl.ds(start, 128)]


def part_a(refs, layer, i, which):
    return jnp.concatenate(
        [ref[i, layer, which] for ref in refs[:3]] + [refs[3 + i // 2][i % 2, layer, which]], 0
    )


def part_b(refs, layer, i, which):
    if i < 3:
        return refs[i][:, layer, which].reshape(512, RANK)
    return jnp.concatenate([ref[:, layer, which].reshape(256, RANK) for ref in refs[3:]], 0)


def write_sums(part_ref, u, v, s1, s2):
    lane = lax.broadcasted_iota(jnp.int32, (ROWS, 128), 1)
    part_ref[:, :256] = u
    part_ref[:, 256:512] = v
    part_ref[:, 512:] = jnp.where(lane < 64, s1, s2)


def first_kernel(x_ref, *refs):
    a, part_ref = refs[:5], refs[5]
    u = jnp.zeros((ROWS, RANK), F32)
    v = jnp.zeros((ROWS, RANK), F32)
    s1 = jnp.zeros((ROWS, 1), F32)
    for i in range(4):
        h = x_ref[:ROWS, 512 * i : 512 * i + 512]
        hf = h.astype(F32)
        s1 += jnp.sum(hf * hf, axis=1, keepdims=True)
        u += mm(h, part_a(a, 0, i, 0))
        v += mm(h, part_a(a, 0, i, 1))
    write_sums(part_ref, u, v, s1, jnp.zeros((ROWS, 1), F32))


def forward_kernel(layer, x_ref, own_ref, got_ref, *refs):
    b, a = refs[:5], refs[5:10]
    xo_ref, part_ref, full_ref = refs[10:]
    last = layer - 1
    full = own_ref[...] + got_ref[...]
    full_ref[...] = full
    mid = middle(full)
    act, act_dot = mid[7], mid[8]
    pair = jnp.concatenate([act, act_dot], 0)
    both = jnp.zeros((2 * ROWS, RANK), F32)
    cross = jnp.zeros((ROWS, RANK), F32)
    s1 = jnp.zeros((ROWS, 1), F32)
    s2 = jnp.zeros((ROWS, 1), F32)
    for i in range(4):
        cols = slice(512 * i, 512 * i + 512)
        step = mm_nt(pair, part_b(b, last, i, 0))
        tail = mm_nt(act, part_b(b, last, i, 1))
        h = (x_ref[:ROWS, cols].astype(F32) + step[:ROWS]).astype(BF16)
        t = (x_ref[ROWS:, cols].astype(F32) + step[ROWS:] + tail).astype(BF16)
        xo_ref[:ROWS, cols] = h
        xo_ref[ROWS:, cols] = t
        hf, tf = h.astype(F32), t.astype(F32)
        s1 += jnp.sum(hf * hf, axis=1, keepdims=True)
        s2 += jnp.sum(hf * tf, axis=1, keepdims=True)
        both += mm(jnp.concatenate([h, t], 0), part_a(a, layer, i, 0))
        cross += mm(h, part_a(a, layer, i, 1))
    write_sums(part_ref, both[:ROWS], both[ROWS:] + cross, s1, s2)


def seed_kernel(x_ref, own_ref, got_ref, goal_ref, *refs):
    cot_ref, part_ref, full_ref = refs[5:]
    full = own_ref[...] + got_ref[...]
    full_ref[...] = full
    mid = middle(full)
    act, act_dot = mid[7], mid[8]
    pair = jnp.concatenate([act, act_dot], 0)
    both = jnp.zeros((2 * ROWS, RANK), F32)
    cross = jnp.zeros((ROWS, RANK), F32)
    for i in range(4):
        cols = slice(512 * i, 512 * i + 512)
        b, q = part_b(refs[:5], LAYERS - 1, i, 0), part_b(refs[:5], LAYERS - 1, i, 1)
        step = mm_nt(pair, b)
        tail = mm_nt(act, q)
        h = (x_ref[:ROWS, cols].astype(F32) + step[:ROWS]).astype(BF16)
        t = (x_ref[ROWS:, cols].astype(F32) + step[ROWS:] + tail).astype(BF16)
        d = (h.astype(F32) - goal_ref[:, cols].astype(F32)).astype(BF16)
        cot_ref[:ROWS, cols] = d
        cot_ref[ROWS:, cols] = t
        both += mm(jnp.concatenate([d, t], 0), b)
        cross += mm(d, q)
    part_ref[:, :256] = both[:ROWS]
    part_ref[:, 256:] = both[ROWS:] + cross


def backward_kernel(layer, x_ref, cot_ref, full_ref, e_own_ref, e_got_ref, *refs):
    a, b = refs[:5], refs[5:10]
    out_ref, part_ref, e_full_ref = refs[10:]
    below = layer - 1
    mid = middle(full_ref[...])
    u, v, r, c = mid[:4]
    e_full = e_own_ref[...] + e_got_ref[...]
    e_full_ref[...] = e_full
    s, s_dot = inner_cotangents(mid, e_full)
    pair = jnp.concatenate([s, s_dot], 0)
    sf, sdf = s.astype(F32), s_dot.astype(F32)
    mean = jnp.sum(sf * u, axis=1, keepdims=True) * (1.0 / D)
    mean_dot = jnp.sum(sf * v + sdf * u, axis=1, keepdims=True) * (1.0 / D)
    r3 = r * r * r
    r3c = r3 * c
    r3m = r3 * mean
    by_h = 3.0 * r3m * r * r * c - r3 * mean_dot
    both = jnp.zeros((2 * ROWS, RANK), F32)
    cross = jnp.zeros((ROWS, RANK), F32)
    for i in range(4):
        cols = slice(512 * i, 512 * i + 512)
        ms = mm_nt(pair, part_a(a, layer, i, 0))
        m = ms[:ROWS]
        m_dot = ms[ROWS:] + mm_nt(s, part_a(a, layer, i, 1))
        h, t = x_ref[:ROWS, cols].astype(F32), x_ref[ROWS:, cols].astype(F32)
        bar = r * m - r3m * h
        bar_dot = r * m_dot - r3c * m - r3m * t + by_h * h
        d = (cot_ref[:ROWS, cols].astype(F32) + bar).astype(BF16)
        d_dot = (cot_ref[ROWS:, cols].astype(F32) + bar_dot).astype(BF16)
        out_ref[:ROWS, cols] = d
        out_ref[ROWS:, cols] = d_dot
        both += mm(jnp.concatenate([d, d_dot], 0), part_b(b, below, i, 0))
        cross += mm(d, part_b(b, below, i, 1))
    part_ref[:, :256] = both[:ROWS]
    part_ref[:, 256:] = both[ROWS:] + cross


def hessian_layers(refs):
    e_own, e_got = refs[15:17]
    for layer in range(LAYERS):
        if layer == 0:
            x_ref, cot_ref, full_ref = refs[12:15]
            e_full = e_own[...] + e_got[...]
        else:
            x_ref, cot_ref, full_ref, e_ref = refs[4 * layer - 4 : 4 * layer]
            e_full = e_ref[...]
        mid = middle(full_ref[...])
        r, c, act, act_dot = mid[2], mid[3], mid[7], mid[8]
        pair = jnp.concatenate(inner_cotangents(mid, e_full), 0)
        acts = jnp.concatenate([act_dot, act], 0)
        yield layer, x_ref, cot_ref, r, r * r * r * c, pair, acts


def columns(slot_z, slot_x):
    order = (0, 2, 1, 3)
    block = 4 * order[slot_z] + order[slot_x]
    return slice(128 * block, 128 * block + 128)


def down_block(x_ref, cols, r, r3c, pair):
    x = x_ref[:, cols].astype(F32)
    h, t = x[:ROWS], x[ROWS:]
    normed = jnp.concatenate([(r * t - r3c * h).astype(BF16), (r * h).astype(BF16)], 0)
    return mm_tn(normed, pair).astype(BF16)


def far_kernel(*refs):
    outs = refs[17:]
    for layer, x_ref, cot_ref, r, r3c, pair, acts in hessian_layers(refs):
        for inner in range(4):
            cols = columns(3, inner)
            outs[inner // 2][inner % 2, layer] = down_block(x_ref, cols, r, r3c, pair)
            up = mm_tn(cot_ref[:, columns(inner, 3)], acts)
            outs[2 + inner // 2][inner % 2, layer] = up.astype(BF16)


def near_kernel(*refs):
    outs = refs[17:]
    for layer, x_ref, cot_ref, r, r3c, pair, acts in hessian_layers(refs):
        for slot in range(3):
            for inner in range(4):
                cols = columns(slot, inner)
                outs[slot][inner, layer] = down_block(x_ref, cols, r, r3c, pair)
                up = mm_tn(cot_ref[:, columns(inner, slot)], acts)
                outs[3 + slot][inner, layer] = up.astype(BF16)


def step_kernel(*refs):
    for i in range(2):
        ahead, behind, first, second = refs[4 * i : 4 * i + 4]
        ahead_out, behind_out = refs[8 + 2 * i : 10 + 2 * i]
        ahead_out[:2] = (ahead[:2].astype(F32) + first[...].astype(F32)).astype(BF16)
        ahead_out[2:] = ahead[2:]
        behind_out[:2] = behind[:2]
        behind_out[2:] = (behind[2:].astype(F32) + second[...].astype(F32)).astype(BF16)


def ring_kernel(own, behind, ahead, *outs):
    for slot in range(4):
        total = own[slot].astype(F32) + behind[slot].astype(F32) + ahead[slot].astype(F32)
        outs[slot][...] = total.astype(BF16)


def layer_kernel(place_ref, *refs):
    downs, ups, outs = refs[:4], refs[4:8], refs[8:]
    for slot, far in enumerate((0, 1, 3, 2)):
        layer = (place_ref[2] + far) & 3
        for half, parts in enumerate((downs, ups)):
            total = parts[0][layer].astype(F32)
            for part in parts[1:]:
                total += part[layer].astype(F32)
            outs[slot][128 * half : 128 * half + 128] = total.astype(BF16)


def totals_kernel(b0, b1, b2, b3, gain_ref, vector_ref, share_ref, totals_ref):
    share = b0[...].astype(F32) + b1[...].astype(F32) + b2[...].astype(F32) + b3[...].astype(F32)
    gain = jnp.concatenate([gain_ref[...], gain_ref[...]], 1)
    share = jnp.concatenate([share[:128] * gain, share[128:]], 0)
    share_ref[...] = share
    vector = vector_ref[...].astype(F32)
    lane = lax.broadcasted_iota(jnp.int32, (1, 128), 1)
    totals = jnp.zeros((1, 128), F32)
    for i, product in enumerate((share * share, vector * share, vector * vector)):
        total = jnp.sum(jnp.sum(product, axis=0, keepdims=True), axis=1, keepdims=True)
        totals = jnp.where(lane == i, total, totals)
    totals_ref[...] = totals


def output_kernel(share_ref, totals_ref, down_ref, up_ref, quotient_ref):
    totals = jnp.sum(totals_ref[...], axis=0, keepdims=True)
    means = totals * (1.0 / (2.0 * LAYERS * D * RANK))
    scale = 1.0 / jnp.sqrt(means[:, 0:1] + EPS)
    down_ref[...] = (share_ref[:128] * scale).astype(BF16)
    up_ref[...] = (share_ref[128:] * scale).T.astype(BF16)
    quotient = means[:, 1:2] / (means[:, 2:3] + EPS) * (1.0 / TOKENS)
    quotient_ref[...] = jnp.broadcast_to(quotient, (1, 128))


VMEM = pl.BlockSpec(memory_space=pltpu.VMEM)
ANY = pl.BlockSpec(memory_space=pl.ANY)
SMEM = pl.BlockSpec(memory_space=pltpu.SMEM)


def shape(dims, dtype):
    return jax.ShapeDtypeStruct(dims, dtype)


def call(kernel, in_specs, outs, flops=1 << 20, moved=1 << 20, scratch=(), grant=24):
    return pl.pallas_call(
        kernel,
        in_specs=in_specs,
        out_specs=[VMEM] * len(outs),
        out_shape=outs,
        scratch_shapes=list(scratch),
        compiler_params=pltpu.CompilerParams(vmem_limit_bytes=grant << 20),
        cost_estimate=pl.CostEstimate(flops=flops, bytes_accessed=moved, transcendentals=0),
    )


def received(blocks, axis):
    own, ahead, behind, across = blocks
    return [own, shift(ahead, axis, 1), shift(behind, axis, -1), shift(across, axis, 2)]


def ring_near(block, axis):
    return shift(block, axis, 1), shift(block, axis, -1)


def ring_far(behind, ahead, axis):
    cut = behind.shape[0] // 2
    return shift(behind[:cut], axis, 1), shift(ahead[cut:], axis, -1)


def ring_gather(block, axis):
    near = ring_near(block, axis)
    return [block, *near, *ring_far(*near, axis)]


def slots_stacked(parts):
    own, behind, ahead, *across = parts
    return jnp.stack([own, behind, ahead, jnp.concatenate(across, 0)])


def local(tokens, targets, norm_gain, down_weight, up_weight, down_vector, up_vector):
    place = jnp.stack([lax.axis_index(axis) for axis in ("z", "x", "y", "c")]).astype(jnp.int32)
    core = place[3]
    chunk, column = call(
        chunk_kernel,
        [ANY] * 5,
        [shape((4, 128, RANK), BF16), shape((128, 128), F32)],
        scratch=[
            pltpu.VMEM((1, 128), BF16),
            *[pltpu.VMEM((1, 128, RANK), BF16)] * 2,
            *[pltpu.VMEM((1, RANK, 128), BF16)] * 2,
            pltpu.SemaphoreType.DMA((5,)),
        ],
        grant=60,
    )(norm_gain, down_weight, down_vector, up_weight, up_vector)
    pair = shape((LAYERS, 2, 128, RANK), BF16)
    a_own, b_own = call(order_kernel, [SMEM] + [VMEM] * 4, [pair, pair])(
        place, chunk, shift(chunk, "y", 1), shift(chunk, "y", -1), shift(chunk, "y", 2)
    )
    a_all, b_all = ring_gather(a_own, "z"), ring_gather(b_own, "x")
    kept, given = call(
        rows_kernel, [SMEM, VMEM, VMEM], [shape((2, 32, HALF), BF16)] * 2, moved=3 << 20
    )(place, tokens, targets)
    got = swap(given)
    rows = jnp.where(
        core == 0, jnp.concatenate([kept, got], 1), jnp.concatenate([got, kept], 1)
    )
    a_all, b_all = slots_stacked(a_all), slots_stacked(b_all)
    a_all, b_all, rows = lax.optimization_barrier((a_all, b_all, rows))
    a_all, b_all = ring_gather(a_all, "x"), ring_gather(b_all, "z")
    h, goal = rows[0], rows[1]
    x = jnp.concatenate([h, jnp.zeros_like(h)], 0)

    wide = shape((2 * ROWS, HALF), BF16)
    sums = shape((ROWS, 640), F32)
    e_sums = shape((ROWS, 512), F32)
    work = 6 * 2 * ROWS * HALF * RANK

    def exchanged(part):
        return part, swap(part)

    states, fulls, cots, e_fulls = [x], [], {}, {}
    (part,) = call(first_kernel, [VMEM] * 6, [sums], work // 3, 3 << 20)(
        x, *a_all
    )
    for layer in range(1, LAYERS):
        x, part, full = call(
            functools.partial(forward_kernel, layer),
            [VMEM] * 13,
            [wide, sums, sums],
            work,
            5 << 20,
        )(x, part, swap(part), *b_all, *a_all)
        states.append(x)
        fulls.append(full)
    cot, part, full = call(
        seed_kernel,
        [VMEM] * 9,
        [wide, e_sums, sums],
        work,
        3 << 20,
    )(x, part, swap(part), goal, *b_all)
    fulls.append(full)

    def backward(layer, cot, e_own, e_got):
        return call(
            functools.partial(backward_kernel, layer),
            [VMEM] * 15,
            [wide, e_sums, e_sums],
            work,
            5 << 20,
        )(states[layer], cot, fulls[layer], e_own, e_got, *a_all, *b_all)

    operands = []
    for layer in (3, 2, 1):
        cots[layer] = cot
        cot, part, e_fulls[layer] = backward(layer, cot, part, swap(part))
    for layer in (1, 2, 3):
        operands += [states[layer], cots[layer], fulls[layer], e_fulls[layer]]
    operands += [states[0], cot, fulls[0], part, swap(part)]

    slot = shape((4, LAYERS, 128, RANK), BF16)
    cut = shape((2, LAYERS, 128, RANK), BF16)
    four = shape((LAYERS, 128, RANK), BF16)
    far = call(far_kernel, [VMEM] * 17, [cut] * 4, work, 6 << 20)(*operands)
    far = (
        shift(far[0], "z", 1),
        shift(far[1], "z", -1),
        shift(far[2], "x", 1),
        shift(far[3], "x", -1),
    )
    near = call(near_kernel, [VMEM] * 17, [slot] * 6, 3 * work, 10 << 20)(*operands)
    sent = call(step_kernel, [VMEM] * 8, [slot] * 4, moved=10 << 20)(
        *(near[1], near[2], far[0], far[1]), *(near[4], near[5], far[2], far[3])
    )
    down_parts = near[0], shift(sent[0], "z", 1), shift(sent[1], "z", -1)
    up_parts = near[3], shift(sent[2], "x", 1), shift(sent[3], "x", -1)
    downs = call(ring_kernel, [VMEM] * 3, [four] * 4, moved=4 << 20)(*down_parts)
    downs = received(downs, "x")
    ups = call(ring_kernel, [VMEM] * 3, [four] * 4, moved=4 << 20)(*up_parts)
    ups = received(ups, "z")
    blocks = call(
        layer_kernel, [SMEM] + [VMEM] * 8, [shape((256, RANK), BF16)] * 4, moved=2 << 20
    )(place, *downs, *ups)
    share, totals = call(
        totals_kernel,
        [VMEM] * 6,
        [shape((256, RANK), F32), shape((1, 128), F32)],
    )(*received(blocks, "y"), column, jnp.concatenate([down_vector[0], chunk[3]], 0))
    totals = jnp.broadcast_to(totals[None], (128, 1, 128))
    totals = lax.all_to_all(totals, ("y", "z", "x", "c"), 0, 0).reshape(128, 128)
    next_down, next_up, quotient = call(
        output_kernel,
        [VMEM] * 2,
        [shape((128, RANK), BF16), shape((RANK, 128), BF16), shape((1, 128), F32)],
    )(share, totals)
    return (next_down[None], next_up[None], quotient[0, 0])


def solution(mesh):
    fine = Mesh(mesh.devices.reshape(4, 4, 4, 2), ("y", "z", "x", "c"))
    fsdp = ("z", "x", "c")
    placed = (
        P(fsdp, None),
        P(fsdp, None),
        P("y", fsdp),
        P("y", fsdp, None),
        P("y", None, fsdp),
        P("y", fsdp, None),
        P("y", None, fsdp),
    )
    return jax.shard_map(
        local,
        mesh=fine,
        in_specs=placed,
        out_specs=(P("y", fsdp, None), P("y", None, fsdp), P()),
        check_vma=False,
    )
```

```python
import functools

import jax
import jax.numpy as jnp
from jax import lax
from jax.experimental import pallas as pl
from jax.experimental.pallas import tpu as pltpu
from jax.sharding import Mesh, PartitionSpec as P

EPS = 1e-06
D = 4096
RANK = 256
LAYERS = 4
TOKENS = 4096
ROWS = 64
HALF = 2048
F32 = jnp.float32
BF16 = jnp.bfloat16


def shift(value, axis, steps):
    return lax.ppermute(value, axis, [(i, (i + steps) % 4) for i in range(4)])


def swap(value):
    return lax.ppermute(value, "c", [(0, 1), (1, 0)])


def dot(left, right, dims):
    return lax.dot_general(left, right, (dims, ((), ())), preferred_element_type=F32)


def mm(left, right):
    return dot(left, right, ((1,), (0,)))


def mm_nt(left, right):
    return dot(left, right, ((1,), (1,)))


def mm_tn(left, right):
    return dot(left, right, ((0,), (0,)))


def middle(full):
    u, v = full[:, :256], full[:, 256:512]
    r = lax.rsqrt(full[:, 512:513] * (1.0 / D) + EPS)
    c = full[:, 639:640] * (1.0 / D)
    r3c = r * r * r * c
    pre = r * u
    pre_dot = r * v - r3c * u
    s = jax.nn.sigmoid(pre)
    slope = s * (1.0 + pre * (1.0 - s))
    slope2 = s * (1.0 - s) * (2.0 + pre * (1.0 - 2.0 * s))
    act = (pre * s).astype(BF16)
    act_dot = (slope * pre_dot).astype(BF16)
    return u, v, r, c, pre_dot, slope, slope2, act, act_dot


def inner_cotangents(mid, e_full):
    e, e_dot = e_full[:, :256], e_full[:, 256:]
    pre_dot, slope, slope2 = mid[4], mid[5], mid[6]
    s = (e * slope).astype(BF16)
    s_dot = (e_dot * slope + e * slope2 * pre_dot).astype(BF16)
    return s, s_dot


FARS = (0, 3, 1, 2)


def chunk_kernel(gain_hbm, down_hbm, vector_hbm, up_hbm, up_vector_hbm, *refs):
    chunk_ref, column_ref, gain_ref, down_ref, vector_ref, up_ref, up_vector_ref, sems = refs
    copies = [
        pltpu.make_async_copy(source, target, sems.at[i])
        for i, (source, target) in enumerate(
            zip((gain_hbm, down_hbm, vector_hbm, up_hbm, up_vector_hbm), refs[2:7])
        )
    ]
    for copy in copies:
        copy.start()
    for copy in copies:
        copy.wait()
    column = jnp.broadcast_to(gain_ref[...].astype(F32), (128, 128)).T
    column_ref[...] = column
    gain = jnp.concatenate([column, column], 1)
    chunk_ref[0] = (down_ref[0].astype(F32) * gain).astype(BF16)
    chunk_ref[1] = (vector_ref[0].astype(F32) * gain).astype(BF16)
    chunk_ref[2] = up_ref[0].astype(F32).T.astype(BF16)
    chunk_ref[3] = up_vector_ref[0].astype(F32).T.astype(BF16)


def order_kernel(place_ref, own, behind, ahead, across, a_ref, b_ref):
    for far, chunk in zip(FARS, (own, behind, ahead, across)):
        layer = (place_ref[2] + far) & 3
        a_ref[layer] = chunk[:2]
        b_ref[layer] = chunk[2:]


def rows_kernel(place_ref, tokens_ref, targets_ref, keep_ref, give_ref):
    rows = pl.ds(pl.multiple_of(place_ref[2] * 32, 32), 32)
    for i, ref in enumerate((tokens_ref, targets_ref)):
        for slot_z, far_z in enumerate(FARS):
            for slot_x, far_x in enumerate(FARS):
                block = ((place_ref[0] + far_z) & 3) * 4 + ((place_ref[1] + far_x) & 3)
                slot = 4 * slot_z + slot_x
                for out_ref, core in ((keep_ref, place_ref[3]), (give_ref, 1 - place_ref[3])):
                    start = pl.multiple_of((2 * block + core) * 128, 128)
                    out_ref[i, :, 128 * slot : 128 * slot + 128] = ref[rows, pl.ds(start, 128)]


def part_a(refs, layer, i, which):
    return jnp.concatenate(
        [ref[i, layer, which] for ref in refs[:3]] + [refs[3 + i // 2][i % 2, layer, which]], 0
    )


def part_b(refs, layer, i, which):
    if i < 3:
        return refs[i][:, layer, which].reshape(512, RANK)
    return jnp.concatenate([ref[:, layer, which].reshape(256, RANK) for ref in refs[3:]], 0)


def write_sums(part_ref, u, v, s1, s2):
    lane = lax.broadcasted_iota(jnp.int32, (ROWS, 128), 1)
    part_ref[:, :256] = u
    part_ref[:, 256:512] = v
    part_ref[:, 512:] = jnp.where(lane < 64, s1, s2)


def first_kernel(x_ref, *refs):
    a, part_ref = refs[:5], refs[5]
    u = jnp.zeros((ROWS, RANK), F32)
    v = jnp.zeros((ROWS, RANK), F32)
    s1 = jnp.zeros((ROWS, 1), F32)
    for i in range(4):
        h = x_ref[:ROWS, 512 * i : 512 * i + 512]
        hf = h.astype(F32)
        s1 += jnp.sum(hf * hf, axis=1, keepdims=True)
        u += mm(h, part_a(a, 0, i, 0))
        v += mm(h, part_a(a, 0, i, 1))
    write_sums(part_ref, u, v, s1, jnp.zeros((ROWS, 1), F32))


def forward_kernel(layer, x_ref, own_ref, got_ref, *refs):
    b, a = refs[:5], refs[5:10]
    xo_ref, part_ref, full_ref = refs[10:]
    last = layer - 1
    full = own_ref[...] + got_ref[...]
    full_ref[...] = full
    mid = middle(full)
    act, act_dot = mid[7], mid[8]
    pair = jnp.concatenate([act, act_dot], 0)
    both = jnp.zeros((2 * ROWS, RANK), F32)
    cross = jnp.zeros((ROWS, RANK), F32)
    s1 = jnp.zeros((ROWS, 1), F32)
    s2 = jnp.zeros((ROWS, 1), F32)
    for i in range(4):
        cols = slice(512 * i, 512 * i + 512)
        step = mm_nt(pair, part_b(b, last, i, 0))
        tail = mm_nt(act, part_b(b, last, i, 1))
        h = (x_ref[:ROWS, cols].astype(F32) + step[:ROWS]).astype(BF16)
        t = (x_ref[ROWS:, cols].astype(F32) + step[ROWS:] + tail).astype(BF16)
        xo_ref[:ROWS, cols] = h
        xo_ref[ROWS:, cols] = t
        hf, tf = h.astype(F32), t.astype(F32)
        s1 += jnp.sum(hf * hf, axis=1, keepdims=True)
        s2 += jnp.sum(hf * tf, axis=1, keepdims=True)
        both += mm(jnp.concatenate([h, t], 0), part_a(a, layer, i, 0))
        cross += mm(h, part_a(a, layer, i, 1))
    write_sums(part_ref, both[:ROWS], both[ROWS:] + cross, s1, s2)


def seed_kernel(x_ref, own_ref, got_ref, goal_ref, *refs):
    cot_ref, part_ref, full_ref = refs[5:]
    full = own_ref[...] + got_ref[...]
    full_ref[...] = full
    mid = middle(full)
    act, act_dot = mid[7], mid[8]
    pair = jnp.concatenate([act, act_dot], 0)
    both = jnp.zeros((2 * ROWS, RANK), F32)
    cross = jnp.zeros((ROWS, RANK), F32)
    for i in range(4):
        cols = slice(512 * i, 512 * i + 512)
        b, q = part_b(refs[:5], LAYERS - 1, i, 0), part_b(refs[:5], LAYERS - 1, i, 1)
        step = mm_nt(pair, b)
        tail = mm_nt(act, q)
        h = (x_ref[:ROWS, cols].astype(F32) + step[:ROWS]).astype(BF16)
        t = (x_ref[ROWS:, cols].astype(F32) + step[ROWS:] + tail).astype(BF16)
        d = (h.astype(F32) - goal_ref[:, cols].astype(F32)).astype(BF16)
        cot_ref[:ROWS, cols] = d
        cot_ref[ROWS:, cols] = t
        both += mm(jnp.concatenate([d, t], 0), b)
        cross += mm(d, q)
    part_ref[:, :256] = both[:ROWS]
    part_ref[:, 256:] = both[ROWS:] + cross


def backward_kernel(layer, x_ref, cot_ref, full_ref, e_own_ref, e_got_ref, *refs):
    a, b = refs[:5], refs[5:10]
    out_ref, part_ref, e_full_ref = refs[10:]
    below = layer - 1
    mid = middle(full_ref[...])
    u, v, r, c = mid[:4]
    e_full = e_own_ref[...] + e_got_ref[...]
    e_full_ref[...] = e_full
    s, s_dot = inner_cotangents(mid, e_full)
    pair = jnp.concatenate([s, s_dot], 0)
    sf, sdf = s.astype(F32), s_dot.astype(F32)
    mean = jnp.sum(sf * u, axis=1, keepdims=True) * (1.0 / D)
    mean_dot = jnp.sum(sf * v + sdf * u, axis=1, keepdims=True) * (1.0 / D)
    r3 = r * r * r
    r3c = r3 * c
    r3m = r3 * mean
    by_h = 3.0 * r3m * r * r * c - r3 * mean_dot
    both = jnp.zeros((2 * ROWS, RANK), F32)
    cross = jnp.zeros((ROWS, RANK), F32)
    for i in range(4):
        cols = slice(512 * i, 512 * i + 512)
        ms = mm_nt(pair, part_a(a, layer, i, 0))
        m = ms[:ROWS]
        m_dot = ms[ROWS:] + mm_nt(s, part_a(a, layer, i, 1))
        h, t = x_ref[:ROWS, cols].astype(F32), x_ref[ROWS:, cols].astype(F32)
        bar = r * m - r3m * h
        bar_dot = r * m_dot - r3c * m - r3m * t + by_h * h
        d = (cot_ref[:ROWS, cols].astype(F32) + bar).astype(BF16)
        d_dot = (cot_ref[ROWS:, cols].astype(F32) + bar_dot).astype(BF16)
        out_ref[:ROWS, cols] = d
        out_ref[ROWS:, cols] = d_dot
        both += mm(jnp.concatenate([d, d_dot], 0), part_b(b, below, i, 0))
        cross += mm(d, part_b(b, below, i, 1))
    part_ref[:, :256] = both[:ROWS]
    part_ref[:, 256:] = both[ROWS:] + cross


def hessian_layers(refs):
    e_own, e_got = refs[15:17]
    for layer in range(LAYERS):
        if layer == 0:
            x_ref, cot_ref, full_ref = refs[12:15]
            e_full = e_own[...] + e_got[...]
        else:
            x_ref, cot_ref, full_ref, e_ref = refs[4 * layer - 4 : 4 * layer]
            e_full = e_ref[...]
        mid = middle(full_ref[...])
        r, c, act, act_dot = mid[2], mid[3], mid[7], mid[8]
        pair = jnp.concatenate(inner_cotangents(mid, e_full), 0)
        acts = jnp.concatenate([act_dot, act], 0)
        yield layer, x_ref, cot_ref, r, r * r * r * c, pair, acts


def columns(slot_z, slot_x):
    order = (0, 2, 1, 3)
    block = 4 * order[slot_z] + order[slot_x]
    return slice(128 * block, 128 * block + 128)


def down_block(x_ref, cols, r, r3c, pair):
    x = x_ref[:, cols].astype(F32)
    h, t = x[:ROWS], x[ROWS:]
    normed = jnp.concatenate([(r * t - r3c * h).astype(BF16), (r * h).astype(BF16)], 0)
    return mm_tn(normed, pair).astype(BF16)


def far_kernel(*refs):
    outs = refs[17:]
    for layer, x_ref, cot_ref, r, r3c, pair, acts in hessian_layers(refs):
        for inner in range(4):
            cols = columns(3, inner)
            outs[inner // 2][inner % 2, layer] = down_block(x_ref, cols, r, r3c, pair)
            up = mm_tn(cot_ref[:, columns(inner, 3)], acts)
            outs[2 + inner // 2][inner % 2, layer] = up.astype(BF16)


def near_kernel(*refs):
    outs = refs[17:]
    for layer, x_ref, cot_ref, r, r3c, pair, acts in hessian_layers(refs):
        for slot in range(3):
            for inner in range(4):
                cols = columns(slot, inner)
                outs[slot][inner, layer] = down_block(x_ref, cols, r, r3c, pair)
                up = mm_tn(cot_ref[:, columns(inner, slot)], acts)
                outs[3 + slot][inner, layer] = up.astype(BF16)


def step_kernel(*refs):
    for i in range(2):
        ahead, behind, first, second = refs[4 * i : 4 * i + 4]
        ahead_out, behind_out = refs[8 + 2 * i : 10 + 2 * i]
        ahead_out[:2] = (ahead[:2].astype(F32) + first[...].astype(F32)).astype(BF16)
        ahead_out[2:] = ahead[2:]
        behind_out[:2] = behind[:2]
        behind_out[2:] = (behind[2:].astype(F32) + second[...].astype(F32)).astype(BF16)


def ring_kernel(own, behind, ahead, *outs):
    for slot in range(4):
        total = own[slot].astype(F32) + behind[slot].astype(F32) + ahead[slot].astype(F32)
        outs[slot][...] = total.astype(BF16)


def layer_kernel(place_ref, *refs):
    downs, ups, outs = refs[:4], refs[4:8], refs[8:]
    for slot, far in enumerate((0, 1, 3, 2)):
        layer = (place_ref[2] + far) & 3
        for half, parts in enumerate((downs, ups)):
            total = parts[0][layer].astype(F32)
            for part in parts[1:]:
                total += part[layer].astype(F32)
            outs[slot][128 * half : 128 * half + 128] = total.astype(BF16)


def totals_kernel(b0, b1, b2, b3, gain_ref, vector_ref, share_ref, totals_ref):
    share = b0[...].astype(F32) + b1[...].astype(F32) + b2[...].astype(F32) + b3[...].astype(F32)
    gain = jnp.concatenate([gain_ref[...], gain_ref[...]], 1)
    share = jnp.concatenate([share[:128] * gain, share[128:]], 0)
    share_ref[...] = share
    vector = vector_ref[...].astype(F32)
    lane = lax.broadcasted_iota(jnp.int32, (1, 128), 1)
    totals = jnp.zeros((1, 128), F32)
    for i, product in enumerate((share * share, vector * share, vector * vector)):
        total = jnp.sum(jnp.sum(product, axis=0, keepdims=True), axis=1, keepdims=True)
        totals = jnp.where(lane == i, total, totals)
    totals_ref[...] = totals


def output_kernel(share_ref, totals_ref, down_ref, up_ref, quotient_ref):
    totals = jnp.sum(totals_ref[...], axis=0, keepdims=True)
    means = totals * (1.0 / (2.0 * LAYERS * D * RANK))
    scale = 1.0 / jnp.sqrt(means[:, 0:1] + EPS)
    down_ref[...] = (share_ref[:128] * scale).astype(BF16)
    up_ref[...] = (share_ref[128:] * scale).T.astype(BF16)
    quotient = means[:, 1:2] / (means[:, 2:3] + EPS) * (1.0 / TOKENS)
    quotient_ref[...] = jnp.broadcast_to(quotient, (1, 128))


VMEM = pl.BlockSpec(memory_space=pltpu.VMEM)
ANY = pl.BlockSpec(memory_space=pl.ANY)
SMEM = pl.BlockSpec(memory_space=pltpu.SMEM)


def shape(dims, dtype):
    return jax.ShapeDtypeStruct(dims, dtype)


def call(kernel, in_specs, outs, flops=1 << 20, moved=1 << 20, scratch=(), grant=24):
    return pl.pallas_call(
        kernel,
        in_specs=in_specs,
        out_specs=[VMEM] * len(outs),
        out_shape=outs,
        scratch_shapes=list(scratch),
        compiler_params=pltpu.CompilerParams(vmem_limit_bytes=grant << 20),
        cost_estimate=pl.CostEstimate(flops=flops, bytes_accessed=moved, transcendentals=0),
    )


def received(blocks, axis):
    own, ahead, behind, across = blocks
    return [own, shift(ahead, axis, 1), shift(behind, axis, -1), shift(across, axis, 2)]


def ring_near(block, axis):
    return shift(block, axis, 1), shift(block, axis, -1)


def ring_far(behind, ahead, axis):
    cut = behind.shape[0] // 2
    return shift(behind[:cut], axis, 1), shift(ahead[cut:], axis, -1)


def ring_gather(block, axis):
    near = ring_near(block, axis)
    return [block, *near, *ring_far(*near, axis)]


def slots_stacked(parts):
    own, behind, ahead, *across = parts
    return jnp.stack([own, behind, ahead, jnp.concatenate(across, 0)])


def local(tokens, targets, norm_gain, down_weight, up_weight, down_vector, up_vector):
    place = jnp.stack([lax.axis_index(axis) for axis in ("z", "x", "y", "c")]).astype(jnp.int32)
    core = place[3]
    chunk, column = call(
        chunk_kernel,
        [ANY] * 5,
        [shape((4, 128, RANK), BF16), shape((128, 128), F32)],
        scratch=[
            pltpu.VMEM((1, 128), BF16),
            *[pltpu.VMEM((1, 128, RANK), BF16)] * 2,
            *[pltpu.VMEM((1, RANK, 128), BF16)] * 2,
            pltpu.SemaphoreType.DMA((5,)),
        ],
        grant=60,
    )(norm_gain, down_weight, down_vector, up_weight, up_vector)
    pair = shape((LAYERS, 2, 128, RANK), BF16)
    a_own, b_own = call(order_kernel, [SMEM] + [VMEM] * 4, [pair, pair])(
        place, chunk, shift(chunk, "y", 1), shift(chunk, "y", -1), shift(chunk, "y", 2)
    )
    a_all, b_all = ring_gather(a_own, "z"), ring_gather(b_own, "x")
    kept, given = call(
        rows_kernel, [SMEM, VMEM, VMEM], [shape((2, 32, HALF), BF16)] * 2, moved=3 << 20
    )(place, tokens, targets)
    got = swap(given)
    rows = jnp.where(
        core == 0, jnp.concatenate([kept, got], 1), jnp.concatenate([got, kept], 1)
    )
    a_all, b_all = slots_stacked(a_all), slots_stacked(b_all)
    b_all, rows = lax.optimization_barrier((b_all, rows))
    a_all, b_all = ring_gather(a_all, "x"), ring_gather(b_all, "z")
    h, goal = rows[0], rows[1]
    x = jnp.concatenate([h, jnp.zeros_like(h)], 0)

    wide = shape((2 * ROWS, HALF), BF16)
    sums = shape((ROWS, 640), F32)
    e_sums = shape((ROWS, 512), F32)
    work = 6 * 2 * ROWS * HALF * RANK

    def exchanged(part):
        return part, swap(part)

    states, fulls, cots, e_fulls = [x], [], {}, {}
    (part,) = call(first_kernel, [VMEM] * 6, [sums], work // 3, 3 << 20)(
        x, *a_all
    )
    for layer in range(1, LAYERS):
        x, part, full = call(
            functools.partial(forward_kernel, layer),
            [VMEM] * 13,
            [wide, sums, sums],
            work,
            5 << 20,
        )(x, part, swap(part), *b_all, *a_all)
        states.append(x)
        fulls.append(full)
    cot, part, full = call(
        seed_kernel,
        [VMEM] * 9,
        [wide, e_sums, sums],
        work,
        3 << 20,
    )(x, part, swap(part), goal, *b_all)
    fulls.append(full)

    def backward(layer, cot, e_own, e_got):
        return call(
            functools.partial(backward_kernel, layer),
            [VMEM] * 15,
            [wide, e_sums, e_sums],
            work,
            5 << 20,
        )(states[layer], cot, fulls[layer], e_own, e_got, *a_all, *b_all)

    operands = []
    for layer in (3, 2, 1):
        cots[layer] = cot
        cot, part, e_fulls[layer] = backward(layer, cot, part, swap(part))
    for layer in (1, 2, 3):
        operands += [states[layer], cots[layer], fulls[layer], e_fulls[layer]]
    operands += [states[0], cot, fulls[0], part, swap(part)]

    slot = shape((4, LAYERS, 128, RANK), BF16)
    cut = shape((2, LAYERS, 128, RANK), BF16)
    four = shape((LAYERS, 128, RANK), BF16)
    far = call(far_kernel, [VMEM] * 17, [cut] * 4, work, 6 << 20)(*operands)
    far = (
        shift(far[0], "z", 1),
        shift(far[1], "z", -1),
        shift(far[2], "x", 1),
        shift(far[3], "x", -1),
    )
    near = call(near_kernel, [VMEM] * 17, [slot] * 6, 3 * work, 10 << 20)(*operands)
    sent = call(step_kernel, [VMEM] * 8, [slot] * 4, moved=10 << 20)(
        *(near[1], near[2], far[0], far[1]), *(near[4], near[5], far[2], far[3])
    )
    down_parts = near[0], shift(sent[0], "z", 1), shift(sent[1], "z", -1)
    up_parts = near[3], shift(sent[2], "x", 1), shift(sent[3], "x", -1)
    downs = call(ring_kernel, [VMEM] * 3, [four] * 4, moved=4 << 20)(*down_parts)
    downs = received(downs, "x")
    ups = call(ring_kernel, [VMEM] * 3, [four] * 4, moved=4 << 20)(*up_parts)
    ups = received(ups, "z")
    blocks = call(
        layer_kernel, [SMEM] + [VMEM] * 8, [shape((256, RANK), BF16)] * 4, moved=2 << 20
    )(place, *downs, *ups)
    share, totals = call(
        totals_kernel,
        [VMEM] * 6,
        [shape((256, RANK), F32), shape((1, 128), F32)],
    )(*received(blocks, "y"), column, jnp.concatenate([down_vector[0], chunk[3]], 0))
    totals = jnp.broadcast_to(totals[None], (128, 1, 128))
    totals = lax.all_to_all(totals, ("y", "z", "x", "c"), 0, 0).reshape(128, 128)
    next_down, next_up, quotient = call(
        output_kernel,
        [VMEM] * 2,
        [shape((128, RANK), BF16), shape((RANK, 128), BF16), shape((1, 128), F32)],
    )(share, totals)
    return (next_down[None], next_up[None], quotient[0, 0])


def solution(mesh):
    fine = Mesh(mesh.devices.reshape(4, 4, 4, 2), ("y", "z", "x", "c"))
    fsdp = ("z", "x", "c")
    placed = (
        P(fsdp, None),
        P(fsdp, None),
        P("y", fsdp),
        P("y", fsdp, None),
        P("y", None, fsdp),
        P("y", fsdp, None),
        P("y", None, fsdp),
    )
    return jax.shard_map(
        local,
        mesh=fine,
        in_specs=placed,
        out_specs=(P("y", fsdp, None), P("y", None, fsdp), P()),
        check_vma=False,
    )
```

```python
import functools

import jax
import jax.numpy as jnp
from jax import lax
from jax.experimental import pallas as pl
from jax.experimental.pallas import tpu as pltpu
from jax.sharding import Mesh, PartitionSpec as P

EPS = 1e-06
D = 4096
RANK = 256
LAYERS = 4
TOKENS = 4096
ROWS = 64
HALF = 2048
F32 = jnp.float32
BF16 = jnp.bfloat16


def shift(value, axis, steps):
    return lax.ppermute(value, axis, [(i, (i + steps) % 4) for i in range(4)])


def swap(value):
    return lax.ppermute(value, "c", [(0, 1), (1, 0)])


def dot(left, right, dims):
    return lax.dot_general(left, right, (dims, ((), ())), preferred_element_type=F32)


def mm(left, right):
    return dot(left, right, ((1,), (0,)))


def mm_nt(left, right):
    return dot(left, right, ((1,), (1,)))


def mm_tn(left, right):
    return dot(left, right, ((0,), (0,)))


def middle(full):
    u, v = full[:, :256], full[:, 256:512]
    r = lax.rsqrt(full[:, 512:513] * (1.0 / D) + EPS)
    c = full[:, 639:640] * (1.0 / D)
    r3c = r * r * r * c
    pre = r * u
    pre_dot = r * v - r3c * u
    s = jax.nn.sigmoid(pre)
    slope = s * (1.0 + pre * (1.0 - s))
    slope2 = s * (1.0 - s) * (2.0 + pre * (1.0 - 2.0 * s))
    act = (pre * s).astype(BF16)
    act_dot = (slope * pre_dot).astype(BF16)
    return u, v, r, c, pre_dot, slope, slope2, act, act_dot


def inner_cotangents(mid, e_full):
    e, e_dot = e_full[:, :256], e_full[:, 256:]
    pre_dot, slope, slope2 = mid[4], mid[5], mid[6]
    s = (e * slope).astype(BF16)
    s_dot = (e_dot * slope + e * slope2 * pre_dot).astype(BF16)
    return s, s_dot


FARS = (0, 3, 1, 2)


def chunk_kernel(gain_hbm, down_hbm, vector_hbm, up_hbm, up_vector_hbm, *refs):
    chunk_ref, column_ref, gain_ref, down_ref, vector_ref, up_ref, up_vector_ref, sems = refs
    copies = [
        pltpu.make_async_copy(source, target, sems.at[i])
        for i, (source, target) in enumerate(
            zip((gain_hbm, down_hbm, vector_hbm, up_hbm, up_vector_hbm), refs[2:7])
        )
    ]
    for copy in copies:
        copy.start()
    for copy in copies:
        copy.wait()
    column = jnp.broadcast_to(gain_ref[...].astype(F32), (128, 128)).T
    column_ref[...] = column
    gain = jnp.concatenate([column, column], 1)
    chunk_ref[0] = (down_ref[0].astype(F32) * gain).astype(BF16)
    chunk_ref[1] = (vector_ref[0].astype(F32) * gain).astype(BF16)
    chunk_ref[2] = up_ref[0].astype(F32).T.astype(BF16)
    chunk_ref[3] = up_vector_ref[0].astype(F32).T.astype(BF16)


def order_kernel(place_ref, own, behind, ahead, across, a_ref, b_ref):
    for far, chunk in zip(FARS, (own, behind, ahead, across)):
        layer = (place_ref[2] + far) & 3
        a_ref[layer] = chunk[:2]
        b_ref[layer] = chunk[2:]


def halves_kernel(behind, ahead, behind_out, ahead_out):
    behind_out[...] = behind[:2]
    ahead_out[...] = ahead[2:]


def slots_kernel(own, behind, ahead, across_low, across_high, out_ref):
    out_ref[0] = own[...]
    out_ref[1] = behind[...]
    out_ref[2] = ahead[...]
    out_ref[3, :2] = across_low[...]
    out_ref[3, 2:] = across_high[...]


def rows_kernel(place_ref, tokens_ref, targets_ref, keep_ref, give_ref):
    rows = pl.ds(pl.multiple_of(place_ref[2] * 32, 32), 32)
    for i, ref in enumerate((tokens_ref, targets_ref)):
        for slot_z, far_z in enumerate(FARS):
            for slot_x, far_x in enumerate(FARS):
                block = ((place_ref[0] + far_z) & 3) * 4 + ((place_ref[1] + far_x) & 3)
                slot = 4 * slot_z + slot_x
                for out_ref, core in ((keep_ref, place_ref[3]), (give_ref, 1 - place_ref[3])):
                    start = pl.multiple_of((2 * block + core) * 128, 128)
                    out_ref[i, :, 128 * slot : 128 * slot + 128] = ref[rows, pl.ds(start, 128)]


def part_a(refs, layer, i, which):
    return jnp.concatenate(
        [ref[i, layer, which] for ref in refs[:3]] + [refs[3 + i // 2][i % 2, layer, which]], 0
    )


def part_b(refs, layer, i, which):
    if i < 3:
        return refs[i][:, layer, which].reshape(512, RANK)
    return jnp.concatenate([ref[:, layer, which].reshape(256, RANK) for ref in refs[3:]], 0)


def write_sums(part_ref, u, v, s1, s2):
    lane = lax.broadcasted_iota(jnp.int32, (ROWS, 128), 1)
    part_ref[:, :256] = u
    part_ref[:, 256:512] = v
    part_ref[:, 512:] = jnp.where(lane < 64, s1, s2)


def first_kernel(x_ref, *refs):
    a, part_ref = refs[:5], refs[5]
    u = jnp.zeros((ROWS, RANK), F32)
    v = jnp.zeros((ROWS, RANK), F32)
    s1 = jnp.zeros((ROWS, 1), F32)
    for i in range(4):
        h = x_ref[:ROWS, 512 * i : 512 * i + 512]
        hf = h.astype(F32)
        s1 += jnp.sum(hf * hf, axis=1, keepdims=True)
        u += mm(h, part_a(a, 0, i, 0))
        v += mm(h, part_a(a, 0, i, 1))
    write_sums(part_ref, u, v, s1, jnp.zeros((ROWS, 1), F32))


def forward_kernel(layer, x_ref, own_ref, got_ref, *refs):
    b, a = refs[:5], refs[5:10]
    xo_ref, part_ref, full_ref = refs[10:]
    last = layer - 1
    full = own_ref[...] + got_ref[...]
    full_ref[...] = full
    mid = middle(full)
    act, act_dot = mid[7], mid[8]
    pair = jnp.concatenate([act, act_dot], 0)
    both = jnp.zeros((2 * ROWS, RANK), F32)
    cross = jnp.zeros((ROWS, RANK), F32)
    s1 = jnp.zeros((ROWS, 1), F32)
    s2 = jnp.zeros((ROWS, 1), F32)
    for i in range(4):
        cols = slice(512 * i, 512 * i + 512)
        step = mm_nt(pair, part_b(b, last, i, 0))
        tail = mm_nt(act, part_b(b, last, i, 1))
        h = (x_ref[:ROWS, cols].astype(F32) + step[:ROWS]).astype(BF16)
        t = (x_ref[ROWS:, cols].astype(F32) + step[ROWS:] + tail).astype(BF16)
        xo_ref[:ROWS, cols] = h
        xo_ref[ROWS:, cols] = t
        hf, tf = h.astype(F32), t.astype(F32)
        s1 += jnp.sum(hf * hf, axis=1, keepdims=True)
        s2 += jnp.sum(hf * tf, axis=1, keepdims=True)
        both += mm(jnp.concatenate([h, t], 0), part_a(a, layer, i, 0))
        cross += mm(h, part_a(a, layer, i, 1))
    write_sums(part_ref, both[:ROWS], both[ROWS:] + cross, s1, s2)


def seed_kernel(x_ref, own_ref, got_ref, goal_ref, *refs):
    cot_ref, part_ref, full_ref = refs[5:]
    full = own_ref[...] + got_ref[...]
    full_ref[...] = full
    mid = middle(full)
    act, act_dot = mid[7], mid[8]
    pair = jnp.concatenate([act, act_dot], 0)
    both = jnp.zeros((2 * ROWS, RANK), F32)
    cross = jnp.zeros((ROWS, RANK), F32)
    for i in range(4):
        cols = slice(512 * i, 512 * i + 512)
        b, q = part_b(refs[:5], LAYERS - 1, i, 0), part_b(refs[:5], LAYERS - 1, i, 1)
        step = mm_nt(pair, b)
        tail = mm_nt(act, q)
        h = (x_ref[:ROWS, cols].astype(F32) + step[:ROWS]).astype(BF16)
        t = (x_ref[ROWS:, cols].astype(F32) + step[ROWS:] + tail).astype(BF16)
        d = (h.astype(F32) - goal_ref[:, cols].astype(F32)).astype(BF16)
        cot_ref[:ROWS, cols] = d
        cot_ref[ROWS:, cols] = t
        both += mm(jnp.concatenate([d, t], 0), b)
        cross += mm(d, q)
    part_ref[:, :256] = both[:ROWS]
    part_ref[:, 256:] = both[ROWS:] + cross


def backward_kernel(layer, x_ref, cot_ref, full_ref, e_own_ref, e_got_ref, *refs):
    a, b = refs[:5], refs[5:10]
    out_ref, part_ref, e_full_ref = refs[10:]
    below = layer - 1
    mid = middle(full_ref[...])
    u, v, r, c = mid[:4]
    e_full = e_own_ref[...] + e_got_ref[...]
    e_full_ref[...] = e_full
    s, s_dot = inner_cotangents(mid, e_full)
    pair = jnp.concatenate([s, s_dot], 0)
    sf, sdf = s.astype(F32), s_dot.astype(F32)
    mean = jnp.sum(sf * u, axis=1, keepdims=True) * (1.0 / D)
    mean_dot = jnp.sum(sf * v + sdf * u, axis=1, keepdims=True) * (1.0 / D)
    r3 = r * r * r
    r3c = r3 * c
    r3m = r3 * mean
    by_h = 3.0 * r3m * r * r * c - r3 * mean_dot
    both = jnp.zeros((2 * ROWS, RANK), F32)
    cross = jnp.zeros((ROWS, RANK), F32)
    for i in range(4):
        cols = slice(512 * i, 512 * i + 512)
        ms = mm_nt(pair, part_a(a, layer, i, 0))
        m = ms[:ROWS]
        m_dot = ms[ROWS:] + mm_nt(s, part_a(a, layer, i, 1))
        h, t = x_ref[:ROWS, cols].astype(F32), x_ref[ROWS:, cols].astype(F32)
        bar = r * m - r3m * h
        bar_dot = r * m_dot - r3c * m - r3m * t + by_h * h
        d = (cot_ref[:ROWS, cols].astype(F32) + bar).astype(BF16)
        d_dot = (cot_ref[ROWS:, cols].astype(F32) + bar_dot).astype(BF16)
        out_ref[:ROWS, cols] = d
        out_ref[ROWS:, cols] = d_dot
        both += mm(jnp.concatenate([d, d_dot], 0), part_b(b, below, i, 0))
        cross += mm(d, part_b(b, below, i, 1))
    part_ref[:, :256] = both[:ROWS]
    part_ref[:, 256:] = both[ROWS:] + cross


def hessian_layers(refs):
    e_own, e_got = refs[15:17]
    for layer in range(LAYERS):
        if layer == 0:
            x_ref, cot_ref, full_ref = refs[12:15]
            e_full = e_own[...] + e_got[...]
        else:
            x_ref, cot_ref, full_ref, e_ref = refs[4 * layer - 4 : 4 * layer]
            e_full = e_ref[...]
        mid = middle(full_ref[...])
        r, c, act, act_dot = mid[2], mid[3], mid[7], mid[8]
        pair = jnp.concatenate(inner_cotangents(mid, e_full), 0)
        acts = jnp.concatenate([act_dot, act], 0)
        yield layer, x_ref, cot_ref, r, r * r * r * c, pair, acts


def columns(slot_z, slot_x):
    order = (0, 2, 1, 3)
    block = 4 * order[slot_z] + order[slot_x]
    return slice(128 * block, 128 * block + 128)


def down_block(x_ref, cols, r, r3c, pair):
    x = x_ref[:, cols].astype(F32)
    h, t = x[:ROWS], x[ROWS:]
    normed = jnp.concatenate([(r * t - r3c * h).astype(BF16), (r * h).astype(BF16)], 0)
    return mm_tn(normed, pair).astype(BF16)


def far_kernel(*refs):
    outs = refs[17:]
    for layer, x_ref, cot_ref, r, r3c, pair, acts in hessian_layers(refs):
        for inner in range(4):
            cols = columns(3, inner)
            outs[inner // 2][inner % 2, layer] = down_block(x_ref, cols, r, r3c, pair)
            up = mm_tn(cot_ref[:, columns(inner, 3)], acts)
            outs[2 + inner // 2][inner % 2, layer] = up.astype(BF16)


def near_kernel(*refs):
    outs = refs[17:]
    for layer, x_ref, cot_ref, r, r3c, pair, acts in hessian_layers(refs):
        for slot in range(3):
            for inner in range(4):
                cols = columns(slot, inner)
                outs[slot][inner, layer] = down_block(x_ref, cols, r, r3c, pair)
                up = mm_tn(cot_ref[:, columns(inner, slot)], acts)
                outs[3 + slot][inner, layer] = up.astype(BF16)


def step_kernel(*refs):
    for i in range(2):
        ahead, behind, first, second = refs[4 * i : 4 * i + 4]
        ahead_out, behind_out = refs[8 + 2 * i : 10 + 2 * i]
        ahead_out[:2] = (ahead[:2].astype(F32) + first[...].astype(F32)).astype(BF16)
        ahead_out[2:] = ahead[2:]
        behind_out[:2] = behind[:2]
        behind_out[2:] = (behind[2:].astype(F32) + second[...].astype(F32)).astype(BF16)


def ring_kernel(own, behind, ahead, *outs):
    for slot in range(4):
        total = own[slot].astype(F32) + behind[slot].astype(F32) + ahead[slot].astype(F32)
        outs[slot][...] = total.astype(BF16)


def layer_kernel(place_ref, *refs):
    downs, ups, outs = refs[:4], refs[4:8], refs[8:]
    for slot, far in enumerate((0, 1, 3, 2)):
        layer = (place_ref[2] + far) & 3
        for half, parts in enumerate((downs, ups)):
            total = parts[0][layer].astype(F32)
            for part in parts[1:]:
                total += part[layer].astype(F32)
            outs[slot][128 * half : 128 * half + 128] = total.astype(BF16)


def totals_kernel(b0, b1, b2, b3, gain_ref, vector_ref, share_ref, totals_ref):
    share = b0[...].astype(F32) + b1[...].astype(F32) + b2[...].astype(F32) + b3[...].astype(F32)
    gain = jnp.concatenate([gain_ref[...], gain_ref[...]], 1)
    share = jnp.concatenate([share[:128] * gain, share[128:]], 0)
    share_ref[...] = share
    vector = vector_ref[...].astype(F32)
    lane = lax.broadcasted_iota(jnp.int32, (1, 128), 1)
    totals = jnp.zeros((1, 128), F32)
    for i, product in enumerate((share * share, vector * share, vector * vector)):
        total = jnp.sum(jnp.sum(product, axis=0, keepdims=True), axis=1, keepdims=True)
        totals = jnp.where(lane == i, total, totals)
    totals_ref[...] = totals


def output_kernel(share_ref, totals_ref, down_ref, up_ref, quotient_ref):
    totals = jnp.sum(totals_ref[...], axis=0, keepdims=True)
    means = totals * (1.0 / (2.0 * LAYERS * D * RANK))
    scale = 1.0 / jnp.sqrt(means[:, 0:1] + EPS)
    down_ref[...] = (share_ref[:128] * scale).astype(BF16)
    up_ref[...] = (share_ref[128:] * scale).T.astype(BF16)
    quotient = means[:, 1:2] / (means[:, 2:3] + EPS) * (1.0 / TOKENS)
    quotient_ref[...] = jnp.broadcast_to(quotient, (1, 128))


VMEM = pl.BlockSpec(memory_space=pltpu.VMEM)
ANY = pl.BlockSpec(memory_space=pl.ANY)
SMEM = pl.BlockSpec(memory_space=pltpu.SMEM)


def shape(dims, dtype):
    return jax.ShapeDtypeStruct(dims, dtype)


def call(kernel, in_specs, outs, flops=1 << 20, moved=1 << 20, scratch=(), grant=24):
    return pl.pallas_call(
        kernel,
        in_specs=in_specs,
        out_specs=[VMEM] * len(outs),
        out_shape=outs,
        scratch_shapes=list(scratch),
        compiler_params=pltpu.CompilerParams(vmem_limit_bytes=grant << 20),
        cost_estimate=pl.CostEstimate(flops=flops, bytes_accessed=moved, transcendentals=0),
    )


def received(blocks, axis):
    own, ahead, behind, across = blocks
    return [own, shift(ahead, axis, 1), shift(behind, axis, -1), shift(across, axis, 2)]


def ring_near(block, axis):
    return shift(block, axis, 1), shift(block, axis, -1)


def ring_far(behind, ahead, axis):
    cut = behind.shape[0] // 2
    return shift(behind[:cut], axis, 1), shift(ahead[cut:], axis, -1)


def ring_gather(block, axis):
    near = ring_near(block, axis)
    return [block, *near, *ring_far(*near, axis)]


def local(tokens, targets, norm_gain, down_weight, up_weight, down_vector, up_vector):
    place = jnp.stack([lax.axis_index(axis) for axis in ("z", "x", "y", "c")]).astype(jnp.int32)
    core = place[3]
    chunk, column = call(
        chunk_kernel,
        [ANY] * 5,
        [shape((4, 128, RANK), BF16), shape((128, 128), F32)],
        scratch=[
            pltpu.VMEM((1, 128), BF16),
            *[pltpu.VMEM((1, 128, RANK), BF16)] * 2,
            *[pltpu.VMEM((1, RANK, 128), BF16)] * 2,
            pltpu.SemaphoreType.DMA((5,)),
        ],
        grant=60,
    )(norm_gain, down_weight, down_vector, up_weight, up_vector)
    pair = shape((LAYERS, 2, 128, RANK), BF16)
    a_own, b_own = call(order_kernel, [SMEM] + [VMEM] * 4, [pair, pair])(
        place, chunk, shift(chunk, "y", 1), shift(chunk, "y", -1), shift(chunk, "y", 2)
    )

    def first_ring(own, axis):
        near = shift(own, axis, 1), shift(own, axis, -1)
        half = shape((2, 2, 128, RANK), BF16)
        behind, ahead = call(halves_kernel, [VMEM] * 2, [half] * 2)(*near)
        parts = own, *near, shift(behind, axis, 1), shift(ahead, axis, -1)
        (stacked,) = call(slots_kernel, [VMEM] * 5, [shape((4, *own.shape), BF16)])(*parts)
        return stacked

    a_all, b_all = first_ring(a_own, "z"), first_ring(b_own, "x")
    kept, given = call(
        rows_kernel, [SMEM, VMEM, VMEM], [shape((2, 32, HALF), BF16)] * 2, moved=3 << 20
    )(place, tokens, targets)
    got = swap(given)
    rows = jnp.where(
        core == 0, jnp.concatenate([kept, got], 1), jnp.concatenate([got, kept], 1)
    )
    a_all, b_all, rows = lax.optimization_barrier((a_all, b_all, rows))
    a_all, b_all = ring_gather(a_all, "x"), ring_gather(b_all, "z")
    h, goal = rows[0], rows[1]
    x = jnp.concatenate([h, jnp.zeros_like(h)], 0)

    wide = shape((2 * ROWS, HALF), BF16)
    sums = shape((ROWS, 640), F32)
    e_sums = shape((ROWS, 512), F32)
    work = 6 * 2 * ROWS * HALF * RANK

    def exchanged(part):
        return part, swap(part)

    states, fulls, cots, e_fulls = [x], [], {}, {}
    (part,) = call(first_kernel, [VMEM] * 6, [sums], work // 3, 3 << 20)(
        x, *a_all
    )
    for layer in range(1, LAYERS):
        x, part, full = call(
            functools.partial(forward_kernel, layer),
            [VMEM] * 13,
            [wide, sums, sums],
            work,
            5 << 20,
        )(x, part, swap(part), *b_all, *a_all)
        states.append(x)
        fulls.append(full)
    cot, part, full = call(
        seed_kernel,
        [VMEM] * 9,
        [wide, e_sums, sums],
        work,
        3 << 20,
    )(x, part, swap(part), goal, *b_all)
    fulls.append(full)

    def backward(layer, cot, e_own, e_got):
        return call(
            functools.partial(backward_kernel, layer),
            [VMEM] * 15,
            [wide, e_sums, e_sums],
            work,
            5 << 20,
        )(states[layer], cot, fulls[layer], e_own, e_got, *a_all, *b_all)

    operands = []
    for layer in (3, 2, 1):
        cots[layer] = cot
        cot, part, e_fulls[layer] = backward(layer, cot, part, swap(part))
    for layer in (1, 2, 3):
        operands += [states[layer], cots[layer], fulls[layer], e_fulls[layer]]
    operands += [states[0], cot, fulls[0], part, swap(part)]

    slot = shape((4, LAYERS, 128, RANK), BF16)
    cut = shape((2, LAYERS, 128, RANK), BF16)
    four = shape((LAYERS, 128, RANK), BF16)
    far = call(far_kernel, [VMEM] * 17, [cut] * 4, work, 6 << 20)(*operands)
    far = (
        shift(far[0], "z", 1),
        shift(far[1], "z", -1),
        shift(far[2], "x", 1),
        shift(far[3], "x", -1),
    )
    near = call(near_kernel, [VMEM] * 17, [slot] * 6, 3 * work, 10 << 20)(*operands)
    sent = call(step_kernel, [VMEM] * 8, [slot] * 4, moved=10 << 20)(
        *(near[1], near[2], far[0], far[1]), *(near[4], near[5], far[2], far[3])
    )
    down_parts = near[0], shift(sent[0], "z", 1), shift(sent[1], "z", -1)
    up_parts = near[3], shift(sent[2], "x", 1), shift(sent[3], "x", -1)
    downs = call(ring_kernel, [VMEM] * 3, [four] * 4, moved=4 << 20)(*down_parts)
    downs = received(downs, "x")
    ups = call(ring_kernel, [VMEM] * 3, [four] * 4, moved=4 << 20)(*up_parts)
    ups = received(ups, "z")
    blocks = call(
        layer_kernel, [SMEM] + [VMEM] * 8, [shape((256, RANK), BF16)] * 4, moved=2 << 20
    )(place, *downs, *ups)
    share, totals = call(
        totals_kernel,
        [VMEM] * 6,
        [shape((256, RANK), F32), shape((1, 128), F32)],
    )(*received(blocks, "y"), column, jnp.concatenate([down_vector[0], chunk[3]], 0))
    totals = jnp.broadcast_to(totals[None], (128, 1, 128))
    totals = lax.all_to_all(totals, ("y", "z", "x", "c"), 0, 0).reshape(128, 128)
    next_down, next_up, quotient = call(
        output_kernel,
        [VMEM] * 2,
        [shape((128, RANK), BF16), shape((RANK, 128), BF16), shape((1, 128), F32)],
    )(share, totals)
    return (next_down[None], next_up[None], quotient[0, 0])


def solution(mesh):
    fine = Mesh(mesh.devices.reshape(4, 4, 4, 2), ("y", "z", "x", "c"))
    fsdp = ("z", "x", "c")
    placed = (
        P(fsdp, None),
        P(fsdp, None),
        P("y", fsdp),
        P("y", fsdp, None),
        P("y", None, fsdp),
        P("y", fsdp, None),
        P("y", None, fsdp),
    )
    return jax.shard_map(
        local,
        mesh=fine,
        in_specs=placed,
        out_specs=(P("y", fsdp, None), P("y", None, fsdp), P()),
        check_vma=False,
    )
```

```python
import functools

import jax
import jax.numpy as jnp
from jax import lax
from jax.experimental import pallas as pl
from jax.experimental.pallas import tpu as pltpu
from jax.sharding import Mesh, PartitionSpec as P

EPS = 1e-06
D = 4096
RANK = 256
LAYERS = 4
TOKENS = 4096
ROWS = 64
HALF = 2048
F32 = jnp.float32
BF16 = jnp.bfloat16


def shift(value, axis, steps):
    return lax.ppermute(value, axis, [(i, (i + steps) % 4) for i in range(4)])


def swap(value):
    return lax.ppermute(value, "c", [(0, 1), (1, 0)])


def dot(left, right, dims):
    return lax.dot_general(left, right, (dims, ((), ())), preferred_element_type=F32)


def mm(left, right):
    return dot(left, right, ((1,), (0,)))


def mm_nt(left, right):
    return dot(left, right, ((1,), (1,)))


def mm_tn(left, right):
    return dot(left, right, ((0,), (0,)))


def middle(full):
    u, v = full[:, :256], full[:, 256:512]
    r = lax.rsqrt(full[:, 512:513] * (1.0 / D) + EPS)
    c = full[:, 639:640] * (1.0 / D)
    r3c = r * r * r * c
    pre = r * u
    pre_dot = r * v - r3c * u
    s = jax.nn.sigmoid(pre)
    slope = s * (1.0 + pre * (1.0 - s))
    slope2 = s * (1.0 - s) * (2.0 + pre * (1.0 - 2.0 * s))
    act = (pre * s).astype(BF16)
    act_dot = (slope * pre_dot).astype(BF16)
    return u, v, r, c, pre_dot, slope, slope2, act, act_dot


def inner_cotangents(mid, e_full):
    e, e_dot = e_full[:, :256], e_full[:, 256:]
    pre_dot, slope, slope2 = mid[4], mid[5], mid[6]
    s = (e * slope).astype(BF16)
    s_dot = (e_dot * slope + e * slope2 * pre_dot).astype(BF16)
    return s, s_dot


FARS = (0, 3, 1, 2)


def chunk_kernel(gain_ref, down_hbm, vector_hbm, up_hbm, up_vector_hbm, *refs):
    chunk_ref, column_ref, down_ref, vector_ref, up_ref, up_vector_ref, sems = refs
    copies = [
        pltpu.make_async_copy(source, target, sems.at[i])
        for i, (source, target) in enumerate(
            zip((down_hbm, vector_hbm, up_hbm, up_vector_hbm), refs[2:6])
        )
    ]
    for copy in copies:
        copy.start()
    for copy in copies:
        copy.wait()
    column = jnp.broadcast_to(gain_ref[...].astype(F32), (128, 128)).T
    column_ref[...] = column
    gain = jnp.concatenate([column, column], 1)
    chunk_ref[0] = (down_ref[0].astype(F32) * gain).astype(BF16)
    chunk_ref[1] = (vector_ref[0].astype(F32) * gain).astype(BF16)
    chunk_ref[2] = up_ref[0].astype(F32).T.astype(BF16)
    chunk_ref[3] = up_vector_ref[0].astype(F32).T.astype(BF16)


def order_kernel(place_ref, own, behind, ahead, across, a_ref, b_ref):
    for far, chunk in zip(FARS, (own, behind, ahead, across)):
        layer = (place_ref[2] + far) & 3
        a_ref[layer] = chunk[:2]
        b_ref[layer] = chunk[2:]


def halves_kernel(behind, ahead, behind_out, ahead_out):
    behind_out[...] = behind[:2]
    ahead_out[...] = ahead[2:]


def slots_kernel(own, behind, ahead, across_low, across_high, out_ref):
    out_ref[0] = own[...]
    out_ref[1] = behind[...]
    out_ref[2] = ahead[...]
    out_ref[3, :2] = across_low[...]
    out_ref[3, 2:] = across_high[...]


def rows_kernel(place_ref, tokens_ref, targets_ref, keep_ref, give_ref):
    rows = pl.ds(pl.multiple_of(place_ref[2] * 32, 32), 32)
    for i, ref in enumerate((tokens_ref, targets_ref)):
        for slot_z, far_z in enumerate(FARS):
            for slot_x, far_x in enumerate(FARS):
                block = ((place_ref[0] + far_z) & 3) * 4 + ((place_ref[1] + far_x) & 3)
                slot = 4 * slot_z + slot_x
                for out_ref, core in ((keep_ref, place_ref[3]), (give_ref, 1 - place_ref[3])):
                    start = pl.multiple_of((2 * block + core) * 128, 128)
                    out_ref[i, :, 128 * slot : 128 * slot + 128] = ref[rows, pl.ds(start, 128)]


def part_a(refs, layer, i, which):
    return jnp.concatenate(
        [ref[i, layer, which] for ref in refs[:3]] + [refs[3 + i // 2][i % 2, layer, which]], 0
    )


def part_b(refs, layer, i, which):
    if i < 3:
        return refs[i][:, layer, which].reshape(512, RANK)
    return jnp.concatenate([ref[:, layer, which].reshape(256, RANK) for ref in refs[3:]], 0)


def write_sums(part_ref, u, v, s1, s2):
    lane = lax.broadcasted_iota(jnp.int32, (ROWS, 128), 1)
    part_ref[:, :256] = u
    part_ref[:, 256:512] = v
    part_ref[:, 512:] = jnp.where(lane < 64, s1, s2)


def first_kernel(x_ref, *refs):
    a, part_ref = refs[:5], refs[5]
    u = jnp.zeros((ROWS, RANK), F32)
    v = jnp.zeros((ROWS, RANK), F32)
    s1 = jnp.zeros((ROWS, 1), F32)
    for i in range(4):
        h = x_ref[:ROWS, 512 * i : 512 * i + 512]
        hf = h.astype(F32)
        s1 += jnp.sum(hf * hf, axis=1, keepdims=True)
        u += mm(h, part_a(a, 0, i, 0))
        v += mm(h, part_a(a, 0, i, 1))
    write_sums(part_ref, u, v, s1, jnp.zeros((ROWS, 1), F32))


def forward_kernel(layer, x_ref, own_ref, got_ref, *refs):
    b, a = refs[:5], refs[5:10]
    xo_ref, part_ref, full_ref = refs[10:]
    last = layer - 1
    full = own_ref[...] + got_ref[...]
    full_ref[...] = full
    mid = middle(full)
    act, act_dot = mid[7], mid[8]
    pair = jnp.concatenate([act, act_dot], 0)
    both = jnp.zeros((2 * ROWS, RANK), F32)
    cross = jnp.zeros((ROWS, RANK), F32)
    s1 = jnp.zeros((ROWS, 1), F32)
    s2 = jnp.zeros((ROWS, 1), F32)
    for i in range(4):
        cols = slice(512 * i, 512 * i + 512)
        step = mm_nt(pair, part_b(b, last, i, 0))
        tail = mm_nt(act, part_b(b, last, i, 1))
        h = (x_ref[:ROWS, cols].astype(F32) + step[:ROWS]).astype(BF16)
        t = (x_ref[ROWS:, cols].astype(F32) + step[ROWS:] + tail).astype(BF16)
        xo_ref[:ROWS, cols] = h
        xo_ref[ROWS:, cols] = t
        hf, tf = h.astype(F32), t.astype(F32)
        s1 += jnp.sum(hf * hf, axis=1, keepdims=True)
        s2 += jnp.sum(hf * tf, axis=1, keepdims=True)
        both += mm(jnp.concatenate([h, t], 0), part_a(a, layer, i, 0))
        cross += mm(h, part_a(a, layer, i, 1))
    write_sums(part_ref, both[:ROWS], both[ROWS:] + cross, s1, s2)


def seed_kernel(x_ref, own_ref, got_ref, goal_ref, *refs):
    cot_ref, part_ref, full_ref = refs[5:]
    full = own_ref[...] + got_ref[...]
    full_ref[...] = full
    mid = middle(full)
    act, act_dot = mid[7], mid[8]
    pair = jnp.concatenate([act, act_dot], 0)
    both = jnp.zeros((2 * ROWS, RANK), F32)
    cross = jnp.zeros((ROWS, RANK), F32)
    for i in range(4):
        cols = slice(512 * i, 512 * i + 512)
        b, q = part_b(refs[:5], LAYERS - 1, i, 0), part_b(refs[:5], LAYERS - 1, i, 1)
        step = mm_nt(pair, b)
        tail = mm_nt(act, q)
        h = (x_ref[:ROWS, cols].astype(F32) + step[:ROWS]).astype(BF16)
        t = (x_ref[ROWS:, cols].astype(F32) + step[ROWS:] + tail).astype(BF16)
        d = (h.astype(F32) - goal_ref[:, cols].astype(F32)).astype(BF16)
        cot_ref[:ROWS, cols] = d
        cot_ref[ROWS:, cols] = t
        both += mm(jnp.concatenate([d, t], 0), b)
        cross += mm(d, q)
    part_ref[:, :256] = both[:ROWS]
    part_ref[:, 256:] = both[ROWS:] + cross


def backward_kernel(layer, x_ref, cot_ref, full_ref, e_own_ref, e_got_ref, *refs):
    a, b = refs[:5], refs[5:10]
    out_ref, part_ref, e_full_ref = refs[10:]
    below = layer - 1
    mid = middle(full_ref[...])
    u, v, r, c = mid[:4]
    e_full = e_own_ref[...] + e_got_ref[...]
    e_full_ref[...] = e_full
    s, s_dot = inner_cotangents(mid, e_full)
    pair = jnp.concatenate([s, s_dot], 0)
    sf, sdf = s.astype(F32), s_dot.astype(F32)
    mean = jnp.sum(sf * u, axis=1, keepdims=True) * (1.0 / D)
    mean_dot = jnp.sum(sf * v + sdf * u, axis=1, keepdims=True) * (1.0 / D)
    r3 = r * r * r
    r3c = r3 * c
    r3m = r3 * mean
    by_h = 3.0 * r3m * r * r * c - r3 * mean_dot
    both = jnp.zeros((2 * ROWS, RANK), F32)
    cross = jnp.zeros((ROWS, RANK), F32)
    for i in range(4):
        cols = slice(512 * i, 512 * i + 512)
        ms = mm_nt(pair, part_a(a, layer, i, 0))
        m = ms[:ROWS]
        m_dot = ms[ROWS:] + mm_nt(s, part_a(a, layer, i, 1))
        h, t = x_ref[:ROWS, cols].astype(F32), x_ref[ROWS:, cols].astype(F32)
        bar = r * m - r3m * h
        bar_dot = r * m_dot - r3c * m - r3m * t + by_h * h
        d = (cot_ref[:ROWS, cols].astype(F32) + bar).astype(BF16)
        d_dot = (cot_ref[ROWS:, cols].astype(F32) + bar_dot).astype(BF16)
        out_ref[:ROWS, cols] = d
        out_ref[ROWS:, cols] = d_dot
        both += mm(jnp.concatenate([d, d_dot], 0), part_b(b, below, i, 0))
        cross += mm(d, part_b(b, below, i, 1))
    part_ref[:, :256] = both[:ROWS]
    part_ref[:, 256:] = both[ROWS:] + cross


def hessian_layers(refs):
    e_own, e_got = refs[15:17]
    for layer in range(LAYERS):
        if layer == 0:
            x_ref, cot_ref, full_ref = refs[12:15]
            e_full = e_own[...] + e_got[...]
        else:
            x_ref, cot_ref, full_ref, e_ref = refs[4 * layer - 4 : 4 * layer]
            e_full = e_ref[...]
        mid = middle(full_ref[...])
        r, c, act, act_dot = mid[2], mid[3], mid[7], mid[8]
        pair = jnp.concatenate(inner_cotangents(mid, e_full), 0)
        acts = jnp.concatenate([act_dot, act], 0)
        yield layer, x_ref, cot_ref, r, r * r * r * c, pair, acts


def columns(slot_z, slot_x):
    order = (0, 2, 1, 3)
    block = 4 * order[slot_z] + order[slot_x]
    return slice(128 * block, 128 * block + 128)


def down_block(x_ref, cols, r, r3c, pair):
    x = x_ref[:, cols].astype(F32)
    h, t = x[:ROWS], x[ROWS:]
    normed = jnp.concatenate([(r * t - r3c * h).astype(BF16), (r * h).astype(BF16)], 0)
    return mm_tn(normed, pair).astype(BF16)


def far_kernel(*refs):
    outs = refs[17:]
    for layer, x_ref, cot_ref, r, r3c, pair, acts in hessian_layers(refs):
        for inner in range(4):
            cols = columns(3, inner)
            outs[inner // 2][inner % 2, layer] = down_block(x_ref, cols, r, r3c, pair)
            up = mm_tn(cot_ref[:, columns(inner, 3)], acts)
            outs[2 + inner // 2][inner % 2, layer] = up.astype(BF16)


def near_kernel(*refs):
    outs = refs[17:]
    for layer, x_ref, cot_ref, r, r3c, pair, acts in hessian_layers(refs):
        for slot in range(3):
            for inner in range(4):
                cols = columns(slot, inner)
                outs[slot][inner, layer] = down_block(x_ref, cols, r, r3c, pair)
                up = mm_tn(cot_ref[:, columns(inner, slot)], acts)
                outs[3 + slot][inner, layer] = up.astype(BF16)


def step_kernel(*refs):
    for i in range(2):
        ahead, behind, first, second = refs[4 * i : 4 * i + 4]
        ahead_out, behind_out = refs[8 + 2 * i : 10 + 2 * i]
        ahead_out[:2] = (ahead[:2].astype(F32) + first[...].astype(F32)).astype(BF16)
        ahead_out[2:] = ahead[2:]
        behind_out[:2] = behind[:2]
        behind_out[2:] = (behind[2:].astype(F32) + second[...].astype(F32)).astype(BF16)


def ring_kernel(own, behind, ahead, *outs):
    for slot in range(4):
        total = own[slot].astype(F32) + behind[slot].astype(F32) + ahead[slot].astype(F32)
        outs[slot][...] = total.astype(BF16)


def layer_kernel(place_ref, *refs):
    downs, ups, outs = refs[:4], refs[4:8], refs[8:]
    for slot, far in enumerate((0, 1, 3, 2)):
        layer = (place_ref[2] + far) & 3
        for half, parts in enumerate((downs, ups)):
            total = parts[0][layer].astype(F32)
            for part in parts[1:]:
                total += part[layer].astype(F32)
            outs[slot][128 * half : 128 * half + 128] = total.astype(BF16)


def totals_kernel(b0, b1, b2, b3, gain_ref, vector_ref, share_ref, totals_ref):
    share = b0[...].astype(F32) + b1[...].astype(F32) + b2[...].astype(F32) + b3[...].astype(F32)
    gain = jnp.concatenate([gain_ref[...], gain_ref[...]], 1)
    share = jnp.concatenate([share[:128] * gain, share[128:]], 0)
    share_ref[...] = share
    vector = vector_ref[...].astype(F32)
    lane = lax.broadcasted_iota(jnp.int32, (1, 128), 1)
    totals = jnp.zeros((1, 128), F32)
    for i, product in enumerate((share * share, vector * share, vector * vector)):
        total = jnp.sum(jnp.sum(product, axis=0, keepdims=True), axis=1, keepdims=True)
        totals = jnp.where(lane == i, total, totals)
    totals_ref[...] = totals


def output_kernel(share_ref, totals_ref, down_ref, up_ref, quotient_ref):
    totals = jnp.sum(totals_ref[...], axis=0, keepdims=True)
    means = totals * (1.0 / (2.0 * LAYERS * D * RANK))
    scale = 1.0 / jnp.sqrt(means[:, 0:1] + EPS)
    down_ref[...] = (share_ref[:128] * scale).astype(BF16)
    up_ref[...] = (share_ref[128:] * scale).T.astype(BF16)
    quotient = means[:, 1:2] / (means[:, 2:3] + EPS) * (1.0 / TOKENS)
    quotient_ref[...] = jnp.broadcast_to(quotient, (1, 128))


VMEM = pl.BlockSpec(memory_space=pltpu.VMEM)
ANY = pl.BlockSpec(memory_space=pl.ANY)
SMEM = pl.BlockSpec(memory_space=pltpu.SMEM)


def shape(dims, dtype):
    return jax.ShapeDtypeStruct(dims, dtype)


def call(kernel, in_specs, outs, flops=1 << 20, moved=1 << 20, scratch=(), grant=24):
    return pl.pallas_call(
        kernel,
        in_specs=in_specs,
        out_specs=[VMEM] * len(outs),
        out_shape=outs,
        scratch_shapes=list(scratch),
        compiler_params=pltpu.CompilerParams(vmem_limit_bytes=grant << 20),
        cost_estimate=pl.CostEstimate(flops=flops, bytes_accessed=moved, transcendentals=0),
    )


def received(blocks, axis):
    own, ahead, behind, across = blocks
    return [own, shift(ahead, axis, 1), shift(behind, axis, -1), shift(across, axis, 2)]


def ring_near(block, axis):
    return shift(block, axis, 1), shift(block, axis, -1)


def ring_far(behind, ahead, axis):
    cut = behind.shape[0] // 2
    return shift(behind[:cut], axis, 1), shift(ahead[cut:], axis, -1)


def ring_gather(block, axis):
    near = ring_near(block, axis)
    return [block, *near, *ring_far(*near, axis)]


def local(tokens, targets, norm_gain, down_weight, up_weight, down_vector, up_vector):
    place = jnp.stack([lax.axis_index(axis) for axis in ("z", "x", "y", "c")]).astype(jnp.int32)
    core = place[3]
    chunk, column = call(
        chunk_kernel,
        [VMEM] + [ANY] * 4,
        [shape((4, 128, RANK), BF16), shape((128, 128), F32)],
        scratch=[
            *[pltpu.VMEM((1, 128, RANK), BF16)] * 2,
            *[pltpu.VMEM((1, RANK, 128), BF16)] * 2,
            pltpu.SemaphoreType.DMA((4,)),
        ],
        grant=60,
    )(norm_gain, down_weight, down_vector, up_weight, up_vector)
    pair = shape((LAYERS, 2, 128, RANK), BF16)
    a_own, b_own = call(order_kernel, [SMEM] + [VMEM] * 4, [pair, pair])(
        place, chunk, shift(chunk, "y", 1), shift(chunk, "y", -1), shift(chunk, "y", 2)
    )

    def first_ring(own, axis):
        near = shift(own, axis, 1), shift(own, axis, -1)
        half = shape((2, 2, 128, RANK), BF16)
        behind, ahead = call(halves_kernel, [VMEM] * 2, [half] * 2)(*near)
        parts = own, *near, shift(behind, axis, 1), shift(ahead, axis, -1)
        (stacked,) = call(slots_kernel, [VMEM] * 5, [shape((4, *own.shape), BF16)])(*parts)
        return stacked

    a_all, b_all = first_ring(a_own, "z"), first_ring(b_own, "x")
    kept, given = call(
        rows_kernel, [SMEM, VMEM, VMEM], [shape((2, 32, HALF), BF16)] * 2, moved=3 << 20
    )(place, tokens, targets)
    got = swap(given)
    rows = jnp.where(
        core == 0, jnp.concatenate([kept, got], 1), jnp.concatenate([got, kept], 1)
    )
    a_all, b_all, rows = lax.optimization_barrier((a_all, b_all, rows))
    a_all, b_all = ring_gather(a_all, "x"), ring_gather(b_all, "z")
    h, goal = rows[0], rows[1]
    x = jnp.concatenate([h, jnp.zeros_like(h)], 0)

    wide = shape((2 * ROWS, HALF), BF16)
    sums = shape((ROWS, 640), F32)
    e_sums = shape((ROWS, 512), F32)
    work = 6 * 2 * ROWS * HALF * RANK

    def exchanged(part):
        return part, swap(part)

    states, fulls, cots, e_fulls = [x], [], {}, {}
    (part,) = call(first_kernel, [VMEM] * 6, [sums], work // 3, 3 << 20)(
        x, *a_all
    )
    for layer in range(1, LAYERS):
        x, part, full = call(
            functools.partial(forward_kernel, layer),
            [VMEM] * 13,
            [wide, sums, sums],
            work,
            5 << 20,
        )(x, part, swap(part), *b_all, *a_all)
        states.append(x)
        fulls.append(full)
    cot, part, full = call(
        seed_kernel,
        [VMEM] * 9,
        [wide, e_sums, sums],
        work,
        3 << 20,
    )(x, part, swap(part), goal, *b_all)
    fulls.append(full)

    def backward(layer, cot, e_own, e_got):
        return call(
            functools.partial(backward_kernel, layer),
            [VMEM] * 15,
            [wide, e_sums, e_sums],
            work,
            5 << 20,
        )(states[layer], cot, fulls[layer], e_own, e_got, *a_all, *b_all)

    operands = []
    for layer in (3, 2, 1):
        cots[layer] = cot
        cot, part, e_fulls[layer] = backward(layer, cot, part, swap(part))
    for layer in (1, 2, 3):
        operands += [states[layer], cots[layer], fulls[layer], e_fulls[layer]]
    operands += [states[0], cot, fulls[0], part, swap(part)]

    slot = shape((4, LAYERS, 128, RANK), BF16)
    cut = shape((2, LAYERS, 128, RANK), BF16)
    four = shape((LAYERS, 128, RANK), BF16)
    far = call(far_kernel, [VMEM] * 17, [cut] * 4, work, 6 << 20)(*operands)
    far = (
        shift(far[0], "z", 1),
        shift(far[1], "z", -1),
        shift(far[2], "x", 1),
        shift(far[3], "x", -1),
    )
    near = call(near_kernel, [VMEM] * 17, [slot] * 6, 3 * work, 10 << 20)(*operands)
    sent = call(step_kernel, [VMEM] * 8, [slot] * 4, moved=10 << 20)(
        *(near[1], near[2], far[0], far[1]), *(near[4], near[5], far[2], far[3])
    )
    down_parts = near[0], shift(sent[0], "z", 1), shift(sent[1], "z", -1)
    up_parts = near[3], shift(sent[2], "x", 1), shift(sent[3], "x", -1)
    downs = call(ring_kernel, [VMEM] * 3, [four] * 4, moved=4 << 20)(*down_parts)
    downs = received(downs, "x")
    ups = call(ring_kernel, [VMEM] * 3, [four] * 4, moved=4 << 20)(*up_parts)
    ups = received(ups, "z")
    blocks = call(
        layer_kernel, [SMEM] + [VMEM] * 8, [shape((256, RANK), BF16)] * 4, moved=2 << 20
    )(place, *downs, *ups)
    share, totals = call(
        totals_kernel,
        [VMEM] * 6,
        [shape((256, RANK), F32), shape((1, 128), F32)],
    )(*received(blocks, "y"), column, jnp.concatenate([down_vector[0], chunk[3]], 0))
    totals = jnp.broadcast_to(totals[None], (128, 1, 128))
    totals = lax.all_to_all(totals, ("y", "z", "x", "c"), 0, 0).reshape(128, 128)
    next_down, next_up, quotient = call(
        output_kernel,
        [VMEM] * 2,
        [shape((128, RANK), BF16), shape((RANK, 128), BF16), shape((1, 128), F32)],
    )(share, totals)
    return (next_down[None], next_up[None], quotient[0, 0])


def solution(mesh):
    fine = Mesh(mesh.devices.reshape(4, 4, 4, 2), ("y", "z", "x", "c"))
    fsdp = ("z", "x", "c")
    placed = (
        P(fsdp, None),
        P(fsdp, None),
        P("y", fsdp),
        P("y", fsdp, None),
        P("y", None, fsdp),
        P("y", fsdp, None),
        P("y", None, fsdp),
    )
    return jax.shard_map(
        local,
        mesh=fine,
        in_specs=placed,
        out_specs=(P("y", fsdp, None), P("y", None, fsdp), P()),
        check_vma=False,
    )
```

```python
import functools

import jax
import jax.numpy as jnp
from jax import lax
from jax.experimental import pallas as pl
from jax.experimental.pallas import tpu as pltpu
from jax.sharding import Mesh, PartitionSpec as P

EPS = 1e-06
D = 4096
RANK = 256
LAYERS = 4
TOKENS = 4096
ROWS = 64
HALF = 2048
F32 = jnp.float32
BF16 = jnp.bfloat16


def shift(value, axis, steps):
    return lax.ppermute(value, axis, [(i, (i + steps) % 4) for i in range(4)])


def swap(value):
    return lax.ppermute(value, "c", [(0, 1), (1, 0)])


def dot(left, right, dims):
    return lax.dot_general(left, right, (dims, ((), ())), preferred_element_type=F32)


def mm(left, right):
    return dot(left, right, ((1,), (0,)))


def mm_nt(left, right):
    return dot(left, right, ((1,), (1,)))


def mm_tn(left, right):
    return dot(left, right, ((0,), (0,)))


def middle(full):
    u, v = full[:, :256], full[:, 256:512]
    r = lax.rsqrt(full[:, 512:513] * (1.0 / D) + EPS)
    c = full[:, 639:640] * (1.0 / D)
    r3c = r * r * r * c
    pre = r * u
    pre_dot = r * v - r3c * u
    s = jax.nn.sigmoid(pre)
    slope = s * (1.0 + pre * (1.0 - s))
    slope2 = s * (1.0 - s) * (2.0 + pre * (1.0 - 2.0 * s))
    act = (pre * s).astype(BF16)
    act_dot = (slope * pre_dot).astype(BF16)
    return u, v, r, c, pre_dot, slope, slope2, act, act_dot


def inner_cotangents(mid, e_full):
    e, e_dot = e_full[:, :256], e_full[:, 256:]
    pre_dot, slope, slope2 = mid[4], mid[5], mid[6]
    s = (e * slope).astype(BF16)
    s_dot = (e_dot * slope + e * slope2 * pre_dot).astype(BF16)
    return s, s_dot


FARS = (0, 3, 1, 2)


def chunk_kernel(gain_ref, down_hbm, vector_hbm, up_hbm, up_vector_hbm, *refs):
    chunk_ref, column_ref, down_ref, vector_ref, up_ref, up_vector_ref, sems = refs
    copies = [
        pltpu.make_async_copy(source, target, sems.at[i])
        for i, (source, target) in enumerate(
            zip((down_hbm, vector_hbm, up_hbm, up_vector_hbm), refs[2:6])
        )
    ]
    for copy in copies:
        copy.start()
    for copy in copies:
        copy.wait()
    column = jnp.broadcast_to(gain_ref[...].astype(F32), (128, 128)).T
    column_ref[...] = column
    gain = jnp.concatenate([column, column], 1)
    chunk_ref[0] = (down_ref[0].astype(F32) * gain).astype(BF16)
    chunk_ref[1] = (vector_ref[0].astype(F32) * gain).astype(BF16)
    chunk_ref[2] = up_ref[0].astype(F32).T.astype(BF16)
    chunk_ref[3] = up_vector_ref[0].astype(F32).T.astype(BF16)


def order_kernel(place_ref, own, behind, ahead, across, a_ref, b_ref):
    for far, chunk in zip(FARS, (own, behind, ahead, across)):
        layer = (place_ref[2] + far) & 3
        a_ref[layer] = chunk[:2]
        b_ref[layer] = chunk[2:]


def halves_kernel(behind, ahead, behind_out, ahead_out):
    behind_out[...] = behind[:2]
    ahead_out[...] = ahead[2:]


def slots_kernel(own, behind, ahead, across_low, across_high, out_ref):
    out_ref[0] = own[...]
    out_ref[1] = behind[...]
    out_ref[2] = ahead[...]
    out_ref[3, :2] = across_low[...]
    out_ref[3, 2:] = across_high[...]


def rows_kernel(place_ref, tokens_ref, targets_ref, keep_ref, give_ref):
    rows = pl.ds(pl.multiple_of(place_ref[2] * 32, 32), 32)
    for i, ref in enumerate((tokens_ref, targets_ref)):
        for slot_z, far_z in enumerate(FARS):
            for slot_x, far_x in enumerate(FARS):
                block = ((place_ref[0] + far_z) & 3) * 4 + ((place_ref[1] + far_x) & 3)
                slot = 4 * slot_z + slot_x
                for out_ref, core in ((keep_ref, place_ref[3]), (give_ref, 1 - place_ref[3])):
                    start = pl.multiple_of((2 * block + core) * 128, 128)
                    out_ref[i, :, 128 * slot : 128 * slot + 128] = ref[rows, pl.ds(start, 128)]


def part_a(refs, layer, i, which):
    return jnp.concatenate(
        [ref[i, layer, which] for ref in refs[:3]] + [refs[3 + i // 2][i % 2, layer, which]], 0
    )


def part_b(refs, layer, i, which):
    if i < 3:
        return refs[i][:, layer, which].reshape(512, RANK)
    return jnp.concatenate([ref[:, layer, which].reshape(256, RANK) for ref in refs[3:]], 0)


def write_sums(part_ref, u, v, s1, s2):
    lane = lax.broadcasted_iota(jnp.int32, (ROWS, 128), 1)
    part_ref[:, :256] = u
    part_ref[:, 256:512] = v
    part_ref[:, 512:] = jnp.where(lane < 64, s1, s2)


def first_kernel(x_ref, *refs):
    a, part_ref = refs[:5], refs[5]
    u = jnp.zeros((ROWS, RANK), F32)
    v = jnp.zeros((ROWS, RANK), F32)
    s1 = jnp.zeros((ROWS, 1), F32)
    for i in range(4):
        h = x_ref[:ROWS, 512 * i : 512 * i + 512]
        hf = h.astype(F32)
        s1 += jnp.sum(hf * hf, axis=1, keepdims=True)
        u += mm(h, part_a(a, 0, i, 0))
        v += mm(h, part_a(a, 0, i, 1))
    write_sums(part_ref, u, v, s1, jnp.zeros((ROWS, 1), F32))


def forward_kernel(layer, x_ref, own_ref, got_ref, *refs):
    b, a = refs[:5], refs[5:10]
    xo_ref, part_ref, full_ref = refs[10:]
    last = layer - 1
    full = own_ref[...] + got_ref[...]
    full_ref[...] = full
    mid = middle(full)
    act, act_dot = mid[7], mid[8]
    pair = jnp.concatenate([act, act_dot], 0)
    both = jnp.zeros((2 * ROWS, RANK), F32)
    cross = jnp.zeros((ROWS, RANK), F32)
    s1 = jnp.zeros((ROWS, 1), F32)
    s2 = jnp.zeros((ROWS, 1), F32)
    for i in range(4):
        cols = slice(512 * i, 512 * i + 512)
        step = mm_nt(pair, part_b(b, last, i, 0))
        tail = mm_nt(act, part_b(b, last, i, 1))
        h = (x_ref[:ROWS, cols].astype(F32) + step[:ROWS]).astype(BF16)
        t = (x_ref[ROWS:, cols].astype(F32) + step[ROWS:] + tail).astype(BF16)
        xo_ref[:ROWS, cols] = h
        xo_ref[ROWS:, cols] = t
        hf, tf = h.astype(F32), t.astype(F32)
        s1 += jnp.sum(hf * hf, axis=1, keepdims=True)
        s2 += jnp.sum(hf * tf, axis=1, keepdims=True)
        both += mm(jnp.concatenate([h, t], 0), part_a(a, layer, i, 0))
        cross += mm(h, part_a(a, layer, i, 1))
    write_sums(part_ref, both[:ROWS], both[ROWS:] + cross, s1, s2)


def seed_kernel(x_ref, own_ref, got_ref, goal_ref, *refs):
    cot_ref, part_ref, full_ref = refs[5:]
    full = own_ref[...] + got_ref[...]
    full_ref[...] = full
    mid = middle(full)
    act, act_dot = mid[7], mid[8]
    pair = jnp.concatenate([act, act_dot], 0)
    both = jnp.zeros((2 * ROWS, RANK), F32)
    cross = jnp.zeros((ROWS, RANK), F32)
    for i in range(4):
        cols = slice(512 * i, 512 * i + 512)
        b, q = part_b(refs[:5], LAYERS - 1, i, 0), part_b(refs[:5], LAYERS - 1, i, 1)
        step = mm_nt(pair, b)
        tail = mm_nt(act, q)
        h = (x_ref[:ROWS, cols].astype(F32) + step[:ROWS]).astype(BF16)
        t = (x_ref[ROWS:, cols].astype(F32) + step[ROWS:] + tail).astype(BF16)
        d = (h.astype(F32) - goal_ref[:, cols].astype(F32)).astype(BF16)
        cot_ref[:ROWS, cols] = d
        cot_ref[ROWS:, cols] = t
        both += mm(jnp.concatenate([d, t], 0), b)
        cross += mm(d, q)
    part_ref[:, :256] = both[:ROWS]
    part_ref[:, 256:] = both[ROWS:] + cross


def backward_kernel(layer, x_ref, cot_ref, full_ref, e_own_ref, e_got_ref, *refs):
    a, b = refs[:5], refs[5:10]
    out_ref, part_ref, e_full_ref = refs[10:]
    below = layer - 1
    mid = middle(full_ref[...])
    u, v, r, c = mid[:4]
    e_full = e_own_ref[...] + e_got_ref[...]
    e_full_ref[...] = e_full
    s, s_dot = inner_cotangents(mid, e_full)
    pair = jnp.concatenate([s, s_dot], 0)
    sf, sdf = s.astype(F32), s_dot.astype(F32)
    mean = jnp.sum(sf * u, axis=1, keepdims=True) * (1.0 / D)
    mean_dot = jnp.sum(sf * v + sdf * u, axis=1, keepdims=True) * (1.0 / D)
    r3 = r * r * r
    r3c = r3 * c
    r3m = r3 * mean
    by_h = 3.0 * r3m * r * r * c - r3 * mean_dot
    both = jnp.zeros((2 * ROWS, RANK), F32)
    cross = jnp.zeros((ROWS, RANK), F32)
    for i in range(4):
        cols = slice(512 * i, 512 * i + 512)
        ms = mm_nt(pair, part_a(a, layer, i, 0))
        m = ms[:ROWS]
        m_dot = ms[ROWS:] + mm_nt(s, part_a(a, layer, i, 1))
        h, t = x_ref[:ROWS, cols].astype(F32), x_ref[ROWS:, cols].astype(F32)
        bar = r * m - r3m * h
        bar_dot = r * m_dot - r3c * m - r3m * t + by_h * h
        d = (cot_ref[:ROWS, cols].astype(F32) + bar).astype(BF16)
        d_dot = (cot_ref[ROWS:, cols].astype(F32) + bar_dot).astype(BF16)
        out_ref[:ROWS, cols] = d
        out_ref[ROWS:, cols] = d_dot
        both += mm(jnp.concatenate([d, d_dot], 0), part_b(b, below, i, 0))
        cross += mm(d, part_b(b, below, i, 1))
    part_ref[:, :256] = both[:ROWS]
    part_ref[:, 256:] = both[ROWS:] + cross


def hessian_layers(refs):
    e_own, e_got = refs[15:17]
    for layer in range(LAYERS):
        if layer == 0:
            x_ref, cot_ref, full_ref = refs[12:15]
            e_full = e_own[...] + e_got[...]
        else:
            x_ref, cot_ref, full_ref, e_ref = refs[4 * layer - 4 : 4 * layer]
            e_full = e_ref[...]
        mid = middle(full_ref[...])
        r, c, act, act_dot = mid[2], mid[3], mid[7], mid[8]
        pair = jnp.concatenate(inner_cotangents(mid, e_full), 0)
        acts = jnp.concatenate([act_dot, act], 0)
        yield layer, x_ref, cot_ref, r, r * r * r * c, pair, acts


def columns(slot_z, slot_x):
    order = (0, 2, 1, 3)
    block = 4 * order[slot_z] + order[slot_x]
    return slice(128 * block, 128 * block + 128)


def down_block(x_ref, cols, r, r3c, pair):
    x = x_ref[:, cols].astype(F32)
    h, t = x[:ROWS], x[ROWS:]
    normed = jnp.concatenate([(r * t - r3c * h).astype(BF16), (r * h).astype(BF16)], 0)
    return mm_tn(normed, pair).astype(BF16)


def far_kernel(*refs):
    outs = refs[17:]
    for layer, x_ref, cot_ref, r, r3c, pair, acts in hessian_layers(refs):
        for inner in range(4):
            cols = columns(3, inner)
            outs[inner // 2][inner % 2, layer] = down_block(x_ref, cols, r, r3c, pair)
            up = mm_tn(cot_ref[:, columns(inner, 3)], acts)
            outs[2 + inner // 2][inner % 2, layer] = up.astype(BF16)


def near_kernel(*refs):
    outs = refs[17:]
    for layer, x_ref, cot_ref, r, r3c, pair, acts in hessian_layers(refs):
        for slot in range(3):
            for inner in range(4):
                cols = columns(slot, inner)
                outs[slot][inner, layer] = down_block(x_ref, cols, r, r3c, pair)
                up = mm_tn(cot_ref[:, columns(inner, slot)], acts)
                outs[3 + slot][inner, layer] = up.astype(BF16)


def step_kernel(*refs):
    for i in range(2):
        ahead, behind, first, second = refs[4 * i : 4 * i + 4]
        ahead_out, behind_out = refs[8 + 2 * i : 10 + 2 * i]
        ahead_out[:2] = (ahead[:2].astype(F32) + first[...].astype(F32)).astype(BF16)
        ahead_out[2:] = ahead[2:]
        behind_out[:2] = behind[:2]
        behind_out[2:] = (behind[2:].astype(F32) + second[...].astype(F32)).astype(BF16)


def ring_kernel(own, behind, ahead, *outs):
    for slot in range(4):
        total = own[slot].astype(F32) + behind[slot].astype(F32) + ahead[slot].astype(F32)
        outs[slot][...] = total.astype(BF16)


def layer_kernel(place_ref, *refs):
    downs, ups, outs = refs[:4], refs[4:8], refs[8:]
    for slot, far in enumerate((0, 1, 3, 2)):
        layer = (place_ref[2] + far) & 3
        for half, parts in enumerate((downs, ups)):
            total = parts[0][layer].astype(F32)
            for part in parts[1:]:
                total += part[layer].astype(F32)
            outs[slot][128 * half : 128 * half + 128] = total.astype(BF16)


def totals_kernel(b0, b1, b2, b3, gain_ref, vector_ref, share_ref, totals_ref):
    share = b0[...].astype(F32) + b1[...].astype(F32) + b2[...].astype(F32) + b3[...].astype(F32)
    gain = jnp.concatenate([gain_ref[...], gain_ref[...]], 1)
    share = jnp.concatenate([share[:128] * gain, share[128:]], 0)
    share_ref[...] = share
    vector = vector_ref[...].astype(F32)
    lane = lax.broadcasted_iota(jnp.int32, (1, 128), 1)
    totals = jnp.zeros((1, 128), F32)
    for i, product in enumerate((share * share, vector * share, vector * vector)):
        total = jnp.sum(jnp.sum(product, axis=0, keepdims=True), axis=1, keepdims=True)
        totals = jnp.where(lane == i, total, totals)
    totals_ref[...] = totals


def output_kernel(share_ref, totals_ref, down_ref, up_ref, quotient_ref):
    totals = jnp.sum(totals_ref[...], axis=0, keepdims=True)
    means = totals * (1.0 / (2.0 * LAYERS * D * RANK))
    scale = 1.0 / jnp.sqrt(means[:, 0:1] + EPS)
    down_ref[...] = (share_ref[:128] * scale).astype(BF16)
    up_ref[...] = (share_ref[128:] * scale).T.astype(BF16)
    quotient = means[:, 1:2] / (means[:, 2:3] + EPS) * (1.0 / TOKENS)
    quotient_ref[...] = jnp.broadcast_to(quotient, (1, 128))


VMEM = pl.BlockSpec(memory_space=pltpu.VMEM)
ANY = pl.BlockSpec(memory_space=pl.ANY)
SMEM = pl.BlockSpec(memory_space=pltpu.SMEM)


def shape(dims, dtype):
    return jax.ShapeDtypeStruct(dims, dtype)


def call(kernel, in_specs, outs, flops=1 << 20, moved=1 << 20, scratch=(), grant=24):
    return pl.pallas_call(
        kernel,
        in_specs=in_specs,
        out_specs=[VMEM] * len(outs),
        out_shape=outs,
        scratch_shapes=list(scratch),
        compiler_params=pltpu.CompilerParams(vmem_limit_bytes=grant << 20),
        cost_estimate=pl.CostEstimate(flops=flops, bytes_accessed=moved, transcendentals=0),
    )


def received(blocks, axis):
    own, ahead, behind, across = blocks
    return [own, shift(ahead, axis, 1), shift(behind, axis, -1), shift(across, axis, 2)]


def ring_near(block, axis):
    return shift(block, axis, 1), shift(block, axis, -1)


def ring_far(behind, ahead, axis):
    cut = behind.shape[0] // 2
    return shift(behind[:cut], axis, 1), shift(ahead[cut:], axis, -1)


def ring_gather(block, axis):
    near = ring_near(block, axis)
    return [block, *near, *ring_far(*near, axis)]


def local(tokens, targets, norm_gain, down_weight, up_weight, down_vector, up_vector):
    place = jnp.stack([lax.axis_index(axis) for axis in ("z", "x", "y", "c")]).astype(jnp.int32)
    core = place[3]
    chunk, column = call(
        chunk_kernel,
        [VMEM] + [ANY] * 4,
        [shape((4, 128, RANK), BF16), shape((128, 128), F32)],
        scratch=[
            *[pltpu.VMEM((1, 128, RANK), BF16)] * 2,
            *[pltpu.VMEM((1, RANK, 128), BF16)] * 2,
            pltpu.SemaphoreType.DMA((4,)),
        ],
        grant=60,
    )(norm_gain, down_weight, down_vector, up_weight, up_vector)
    pair = shape((LAYERS, 2, 128, RANK), BF16)
    a_own, b_own = call(order_kernel, [SMEM] + [VMEM] * 4, [pair, pair])(
        place, chunk, shift(chunk, "y", 1), shift(chunk, "y", -1), shift(chunk, "y", 2)
    )

    def first_ring(own, axis):
        near = shift(own, axis, 1), shift(own, axis, -1)
        half = shape((2, 2, 128, RANK), BF16)
        behind, ahead = call(halves_kernel, [VMEM] * 2, [half] * 2)(*near)
        parts = own, *near, shift(behind, axis, 1), shift(ahead, axis, -1)
        (stacked,) = call(slots_kernel, [VMEM] * 5, [shape((4, *own.shape), BF16)])(*parts)
        return stacked

    a_all, b_all = first_ring(a_own, "z"), first_ring(b_own, "x")
    kept, given = call(
        rows_kernel, [SMEM, VMEM, VMEM], [shape((2, 32, HALF), BF16)] * 2, moved=3 << 20
    )(place, tokens, targets)
    got = swap(given)
    rows = jnp.where(
        core == 0, jnp.concatenate([kept, got], 1), jnp.concatenate([got, kept], 1)
    )
    a_all, b_all, rows = lax.optimization_barrier((a_all, b_all, rows))
    a_all, b_all = ring_gather(a_all, "x"), ring_gather(b_all, "z")
    a_all, b_all = lax.optimization_barrier((a_all, b_all))
    h, goal = rows[0], rows[1]
    x = jnp.concatenate([h, jnp.zeros_like(h)], 0)

    wide = shape((2 * ROWS, HALF), BF16)
    sums = shape((ROWS, 640), F32)
    e_sums = shape((ROWS, 512), F32)
    work = 6 * 2 * ROWS * HALF * RANK

    def exchanged(part):
        return part, swap(part)

    states, fulls, cots, e_fulls = [x], [], {}, {}
    (part,) = call(first_kernel, [VMEM] * 6, [sums], work // 3, 3 << 20)(
        x, *a_all
    )
    for layer in range(1, LAYERS):
        x, part, full = call(
            functools.partial(forward_kernel, layer),
            [VMEM] * 13,
            [wide, sums, sums],
            work,
            5 << 20,
        )(x, part, swap(part), *b_all, *a_all)
        states.append(x)
        fulls.append(full)
    cot, part, full = call(
        seed_kernel,
        [VMEM] * 9,
        [wide, e_sums, sums],
        work,
        3 << 20,
    )(x, part, swap(part), goal, *b_all)
    fulls.append(full)

    def backward(layer, cot, e_own, e_got):
        return call(
            functools.partial(backward_kernel, layer),
            [VMEM] * 15,
            [wide, e_sums, e_sums],
            work,
            5 << 20,
        )(states[layer], cot, fulls[layer], e_own, e_got, *a_all, *b_all)

    operands = []
    for layer in (3, 2, 1):
        cots[layer] = cot
        cot, part, e_fulls[layer] = backward(layer, cot, part, swap(part))
    for layer in (1, 2, 3):
        operands += [states[layer], cots[layer], fulls[layer], e_fulls[layer]]
    operands += [states[0], cot, fulls[0], part, swap(part)]

    slot = shape((4, LAYERS, 128, RANK), BF16)
    cut = shape((2, LAYERS, 128, RANK), BF16)
    four = shape((LAYERS, 128, RANK), BF16)
    far = call(far_kernel, [VMEM] * 17, [cut] * 4, work, 6 << 20)(*operands)
    far = (
        shift(far[0], "z", 1),
        shift(far[1], "z", -1),
        shift(far[2], "x", 1),
        shift(far[3], "x", -1),
    )
    near = call(near_kernel, [VMEM] * 17, [slot] * 6, 3 * work, 10 << 20)(*operands)
    sent = call(step_kernel, [VMEM] * 8, [slot] * 4, moved=10 << 20)(
        *(near[1], near[2], far[0], far[1]), *(near[4], near[5], far[2], far[3])
    )
    down_parts = near[0], shift(sent[0], "z", 1), shift(sent[1], "z", -1)
    up_parts = near[3], shift(sent[2], "x", 1), shift(sent[3], "x", -1)
    downs = call(ring_kernel, [VMEM] * 3, [four] * 4, moved=4 << 20)(*down_parts)
    downs = received(downs, "x")
    ups = call(ring_kernel, [VMEM] * 3, [four] * 4, moved=4 << 20)(*up_parts)
    ups = received(ups, "z")
    blocks = call(
        layer_kernel, [SMEM] + [VMEM] * 8, [shape((256, RANK), BF16)] * 4, moved=2 << 20
    )(place, *downs, *ups)
    share, totals = call(
        totals_kernel,
        [VMEM] * 6,
        [shape((256, RANK), F32), shape((1, 128), F32)],
    )(*received(blocks, "y"), column, jnp.concatenate([down_vector[0], chunk[3]], 0))
    totals = jnp.broadcast_to(totals[None], (128, 1, 128))
    totals = lax.all_to_all(totals, ("y", "z", "x", "c"), 0, 0).reshape(128, 128)
    next_down, next_up, quotient = call(
        output_kernel,
        [VMEM] * 2,
        [shape((128, RANK), BF16), shape((RANK, 128), BF16), shape((1, 128), F32)],
    )(share, totals)
    return (next_down[None], next_up[None], quotient[0, 0])


def solution(mesh):
    fine = Mesh(mesh.devices.reshape(4, 4, 4, 2), ("y", "z", "x", "c"))
    fsdp = ("z", "x", "c")
    placed = (
        P(fsdp, None),
        P(fsdp, None),
        P("y", fsdp),
        P("y", fsdp, None),
        P("y", None, fsdp),
        P("y", fsdp, None),
        P("y", None, fsdp),
    )
    return jax.shard_map(
        local,
        mesh=fine,
        in_specs=placed,
        out_specs=(P("y", fsdp, None), P("y", None, fsdp), P()),
        check_vma=False,
    )
```

```python
import functools

import jax
import jax.numpy as jnp
from jax import lax
from jax.experimental import pallas as pl
from jax.experimental.pallas import tpu as pltpu
from jax.sharding import Mesh, PartitionSpec as P

EPS = 1e-06
D = 4096
RANK = 256
LAYERS = 4
TOKENS = 4096
ROWS = 64
HALF = 2048
F32 = jnp.float32
BF16 = jnp.bfloat16


def shift(value, axis, steps):
    return lax.ppermute(value, axis, [(i, (i + steps) % 4) for i in range(4)])


def swap(value):
    return lax.ppermute(value, "c", [(0, 1), (1, 0)])


def dot(left, right, dims):
    return lax.dot_general(left, right, (dims, ((), ())), preferred_element_type=F32)


def mm(left, right):
    return dot(left, right, ((1,), (0,)))


def mm_nt(left, right):
    return dot(left, right, ((1,), (1,)))


def mm_tn(left, right):
    return dot(left, right, ((0,), (0,)))


def middle(full):
    u, v = full[:, :256], full[:, 256:512]
    r = lax.rsqrt(full[:, 512:513] * (1.0 / D) + EPS)
    c = full[:, 639:640] * (1.0 / D)
    r3c = r * r * r * c
    pre = r * u
    pre_dot = r * v - r3c * u
    s = jax.nn.sigmoid(pre)
    slope = s * (1.0 + pre * (1.0 - s))
    slope2 = s * (1.0 - s) * (2.0 + pre * (1.0 - 2.0 * s))
    act = (pre * s).astype(BF16)
    act_dot = (slope * pre_dot).astype(BF16)
    return u, v, r, c, pre_dot, slope, slope2, act, act_dot


def inner_cotangents(mid, e_full):
    e, e_dot = e_full[:, :256], e_full[:, 256:]
    pre_dot, slope, slope2 = mid[4], mid[5], mid[6]
    s = (e * slope).astype(BF16)
    s_dot = (e_dot * slope + e * slope2 * pre_dot).astype(BF16)
    return s, s_dot


FARS = (0, 3, 1, 2)


def chunk_kernel(gain_ref, down_hbm, vector_hbm, up_hbm, up_vector_hbm, *refs):
    chunk_ref, column_ref, down_ref, vector_ref, up_ref, up_vector_ref, sems = refs
    copies = [
        pltpu.make_async_copy(source, target, sems.at[i])
        for i, (source, target) in enumerate(
            zip((down_hbm, vector_hbm, up_hbm, up_vector_hbm), refs[2:6])
        )
    ]
    for copy in copies:
        copy.start()
    for copy in copies:
        copy.wait()
    column = jnp.broadcast_to(gain_ref[...].astype(F32), (128, 128)).T
    column_ref[...] = column
    gain = jnp.concatenate([column, column], 1)
    chunk_ref[0] = (down_ref[0].astype(F32) * gain).astype(BF16)
    chunk_ref[1] = (vector_ref[0].astype(F32) * gain).astype(BF16)
    chunk_ref[2] = up_ref[0].astype(F32).T.astype(BF16)
    chunk_ref[3] = up_vector_ref[0].astype(F32).T.astype(BF16)


def order_kernel(place_ref, own, behind, ahead, across, a_ref, b_ref):
    for far, chunk in zip(FARS, (own, behind, ahead, across)):
        layer = (place_ref[2] + far) & 3
        a_ref[layer] = chunk[:2]
        b_ref[layer] = chunk[2:]


def halves_kernel(behind, ahead, behind_out, ahead_out):
    behind_out[...] = behind[:2]
    ahead_out[...] = ahead[2:]


def slots_kernel(own, behind, ahead, across_low, across_high, out_ref):
    out_ref[0] = own[...]
    out_ref[1] = behind[...]
    out_ref[2] = ahead[...]
    out_ref[3, :2] = across_low[...]
    out_ref[3, 2:] = across_high[...]


def rows_kernel(place_ref, tokens_ref, targets_ref, keep_ref, give_ref):
    rows = pl.ds(pl.multiple_of(place_ref[2] * 32, 32), 32)
    for i, ref in enumerate((tokens_ref, targets_ref)):
        for slot_z, far_z in enumerate(FARS):
            for slot_x, far_x in enumerate(FARS):
                block = ((place_ref[0] + far_z) & 3) * 4 + ((place_ref[1] + far_x) & 3)
                slot = 4 * slot_z + slot_x
                for out_ref, core in ((keep_ref, place_ref[3]), (give_ref, 1 - place_ref[3])):
                    start = pl.multiple_of((2 * block + core) * 128, 128)
                    out_ref[i, :, 128 * slot : 128 * slot + 128] = ref[rows, pl.ds(start, 128)]


def part_a(refs, layer, i, which):
    return jnp.concatenate(
        [ref[i, layer, which] for ref in refs[:3]] + [refs[3 + i // 2][i % 2, layer, which]], 0
    )


def part_b(refs, layer, i, which):
    if i < 3:
        return refs[i][:, layer, which].reshape(512, RANK)
    return jnp.concatenate([ref[:, layer, which].reshape(256, RANK) for ref in refs[3:]], 0)


def write_sums(part_ref, u, v, s1, s2):
    lane = lax.broadcasted_iota(jnp.int32, (ROWS, 128), 1)
    part_ref[:, :256] = u
    part_ref[:, 256:512] = v
    part_ref[:, 512:] = jnp.where(lane < 64, s1, s2)


def first_kernel(x_ref, *refs):
    a, part_ref = refs[:5], refs[5]
    u = jnp.zeros((ROWS, RANK), F32)
    v = jnp.zeros((ROWS, RANK), F32)
    s1 = jnp.zeros((ROWS, 1), F32)
    for i in range(4):
        h = x_ref[:ROWS, 512 * i : 512 * i + 512]
        hf = h.astype(F32)
        s1 += jnp.sum(hf * hf, axis=1, keepdims=True)
        u += mm(h, part_a(a, 0, i, 0))
        v += mm(h, part_a(a, 0, i, 1))
    write_sums(part_ref, u, v, s1, jnp.zeros((ROWS, 1), F32))


def forward_kernel(layer, x_ref, own_ref, got_ref, *refs):
    b, a = refs[:5], refs[5:10]
    xo_ref, part_ref, full_ref = refs[10:]
    last = layer - 1
    full = own_ref[...] + got_ref[...]
    full_ref[...] = full
    mid = middle(full)
    act, act_dot = mid[7], mid[8]
    pair = jnp.concatenate([act, act_dot], 0)
    both = jnp.zeros((2 * ROWS, RANK), F32)
    cross = jnp.zeros((ROWS, RANK), F32)
    s1 = jnp.zeros((ROWS, 1), F32)
    s2 = jnp.zeros((ROWS, 1), F32)
    for i in range(4):
        cols = slice(512 * i, 512 * i + 512)
        step = mm_nt(pair, part_b(b, last, i, 0))
        tail = mm_nt(act, part_b(b, last, i, 1))
        h = (x_ref[:ROWS, cols].astype(F32) + step[:ROWS]).astype(BF16)
        t = (x_ref[ROWS:, cols].astype(F32) + step[ROWS:] + tail).astype(BF16)
        xo_ref[:ROWS, cols] = h
        xo_ref[ROWS:, cols] = t
        hf, tf = h.astype(F32), t.astype(F32)
        s1 += jnp.sum(hf * hf, axis=1, keepdims=True)
        s2 += jnp.sum(hf * tf, axis=1, keepdims=True)
        both += mm(jnp.concatenate([h, t], 0), part_a(a, layer, i, 0))
        cross += mm(h, part_a(a, layer, i, 1))
    write_sums(part_ref, both[:ROWS], both[ROWS:] + cross, s1, s2)


def seed_kernel(x_ref, own_ref, got_ref, goal_ref, *refs):
    cot_ref, part_ref, full_ref = refs[5:]
    full = own_ref[...] + got_ref[...]
    full_ref[...] = full
    mid = middle(full)
    act, act_dot = mid[7], mid[8]
    pair = jnp.concatenate([act, act_dot], 0)
    both = jnp.zeros((2 * ROWS, RANK), F32)
    cross = jnp.zeros((ROWS, RANK), F32)
    for i in range(4):
        cols = slice(512 * i, 512 * i + 512)
        b, q = part_b(refs[:5], LAYERS - 1, i, 0), part_b(refs[:5], LAYERS - 1, i, 1)
        step = mm_nt(pair, b)
        tail = mm_nt(act, q)
        h = (x_ref[:ROWS, cols].astype(F32) + step[:ROWS]).astype(BF16)
        t = (x_ref[ROWS:, cols].astype(F32) + step[ROWS:] + tail).astype(BF16)
        d = (h.astype(F32) - goal_ref[:, cols].astype(F32)).astype(BF16)
        cot_ref[:ROWS, cols] = d
        cot_ref[ROWS:, cols] = t
        both += mm(jnp.concatenate([d, t], 0), b)
        cross += mm(d, q)
    part_ref[:, :256] = both[:ROWS]
    part_ref[:, 256:] = both[ROWS:] + cross


def backward_kernel(layer, x_ref, cot_ref, full_ref, e_own_ref, e_got_ref, *refs):
    a, b = refs[:5], refs[5:10]
    out_ref, part_ref, e_full_ref = refs[10:]
    below = layer - 1
    mid = middle(full_ref[...])
    u, v, r, c = mid[:4]
    e_full = e_own_ref[...] + e_got_ref[...]
    e_full_ref[...] = e_full
    s, s_dot = inner_cotangents(mid, e_full)
    pair = jnp.concatenate([s, s_dot], 0)
    sf, sdf = s.astype(F32), s_dot.astype(F32)
    mean = jnp.sum(sf * u, axis=1, keepdims=True) * (1.0 / D)
    mean_dot = jnp.sum(sf * v + sdf * u, axis=1, keepdims=True) * (1.0 / D)
    r3 = r * r * r
    r3c = r3 * c
    r3m = r3 * mean
    by_h = 3.0 * r3m * r * r * c - r3 * mean_dot
    both = jnp.zeros((2 * ROWS, RANK), F32)
    cross = jnp.zeros((ROWS, RANK), F32)
    for i in range(4):
        cols = slice(512 * i, 512 * i + 512)
        ms = mm_nt(pair, part_a(a, layer, i, 0))
        m = ms[:ROWS]
        m_dot = ms[ROWS:] + mm_nt(s, part_a(a, layer, i, 1))
        h, t = x_ref[:ROWS, cols].astype(F32), x_ref[ROWS:, cols].astype(F32)
        bar = r * m - r3m * h
        bar_dot = r * m_dot - r3c * m - r3m * t + by_h * h
        d = (cot_ref[:ROWS, cols].astype(F32) + bar).astype(BF16)
        d_dot = (cot_ref[ROWS:, cols].astype(F32) + bar_dot).astype(BF16)
        out_ref[:ROWS, cols] = d
        out_ref[ROWS:, cols] = d_dot
        both += mm(jnp.concatenate([d, d_dot], 0), part_b(b, below, i, 0))
        cross += mm(d, part_b(b, below, i, 1))
    part_ref[:, :256] = both[:ROWS]
    part_ref[:, 256:] = both[ROWS:] + cross


def hessian_layers(refs):
    e_own, e_got = refs[15:17]
    for layer in range(LAYERS):
        if layer == 0:
            x_ref, cot_ref, full_ref = refs[12:15]
            e_full = e_own[...] + e_got[...]
        else:
            x_ref, cot_ref, full_ref, e_ref = refs[4 * layer - 4 : 4 * layer]
            e_full = e_ref[...]
        mid = middle(full_ref[...])
        r, c, act, act_dot = mid[2], mid[3], mid[7], mid[8]
        pair = jnp.concatenate(inner_cotangents(mid, e_full), 0)
        acts = jnp.concatenate([act_dot, act], 0)
        yield layer, x_ref, cot_ref, r, r * r * r * c, pair, acts


def columns(slot_z, slot_x):
    order = (0, 2, 1, 3)
    block = 4 * order[slot_z] + order[slot_x]
    return slice(128 * block, 128 * block + 128)


def down_block(x_ref, cols, r, r3c, pair):
    x = x_ref[:, cols].astype(F32)
    h, t = x[:ROWS], x[ROWS:]
    normed = jnp.concatenate([(r * t - r3c * h).astype(BF16), (r * h).astype(BF16)], 0)
    return mm_tn(normed, pair).astype(BF16)


def far_kernel(*refs):
    outs = refs[17:]
    for layer, x_ref, cot_ref, r, r3c, pair, acts in hessian_layers(refs):
        for inner in range(4):
            cols = columns(3, inner)
            outs[inner // 2][inner % 2, layer] = down_block(x_ref, cols, r, r3c, pair)
            up = mm_tn(cot_ref[:, columns(inner, 3)], acts)
            outs[2 + inner // 2][inner % 2, layer] = up.astype(BF16)


def near_kernel(*refs):
    outs = refs[17:]
    for layer, x_ref, cot_ref, r, r3c, pair, acts in hessian_layers(refs):
        for slot in range(3):
            for inner in range(4):
                cols = columns(slot, inner)
                outs[slot][inner, layer] = down_block(x_ref, cols, r, r3c, pair)
                up = mm_tn(cot_ref[:, columns(inner, slot)], acts)
                outs[3 + slot][inner, layer] = up.astype(BF16)


def step_kernel(*refs):
    for i in range(2):
        ahead, behind, first, second = refs[4 * i : 4 * i + 4]
        ahead_out, behind_out = refs[8 + 2 * i : 10 + 2 * i]
        ahead_out[:2] = (ahead[:2].astype(F32) + first[...].astype(F32)).astype(BF16)
        ahead_out[2:] = ahead[2:]
        behind_out[:2] = behind[:2]
        behind_out[2:] = (behind[2:].astype(F32) + second[...].astype(F32)).astype(BF16)


def ring_kernel(own, behind, ahead, *outs):
    for slot in range(4):
        total = own[slot].astype(F32) + behind[slot].astype(F32) + ahead[slot].astype(F32)
        outs[slot][...] = total.astype(BF16)


def layer_kernel(place_ref, *refs):
    downs, ups, outs = refs[:4], refs[4:8], refs[8:]
    for slot, far in enumerate((0, 1, 3, 2)):
        layer = (place_ref[2] + far) & 3
        for half, parts in enumerate((downs, ups)):
            total = parts[0][layer].astype(F32)
            for part in parts[1:]:
                total += part[layer].astype(F32)
            outs[slot][128 * half : 128 * half + 128] = total.astype(BF16)


def totals_kernel(b0, b1, b2, b3, gain_ref, vector_ref, share_ref, totals_ref):
    share = b0[...].astype(F32) + b1[...].astype(F32) + b2[...].astype(F32) + b3[...].astype(F32)
    gain = jnp.concatenate([gain_ref[...], gain_ref[...]], 1)
    share = jnp.concatenate([share[:128] * gain, share[128:]], 0)
    share_ref[...] = share
    vector = vector_ref[...].astype(F32)
    lane = lax.broadcasted_iota(jnp.int32, (1, 128), 1)
    totals = jnp.zeros((1, 128), F32)
    for i, product in enumerate((share * share, vector * share, vector * vector)):
        total = jnp.sum(jnp.sum(product, axis=0, keepdims=True), axis=1, keepdims=True)
        totals = jnp.where(lane == i, total, totals)
    totals_ref[...] = totals


def output_kernel(share_ref, totals_ref, down_ref, up_ref, quotient_ref):
    totals = jnp.sum(totals_ref[...], axis=0, keepdims=True)
    means = totals * (1.0 / (2.0 * LAYERS * D * RANK))
    scale = 1.0 / jnp.sqrt(means[:, 0:1] + EPS)
    down_ref[...] = (share_ref[:128] * scale).astype(BF16)
    up_ref[...] = (share_ref[128:] * scale).T.astype(BF16)
    quotient = means[:, 1:2] / (means[:, 2:3] + EPS) * (1.0 / TOKENS)
    quotient_ref[...] = jnp.broadcast_to(quotient, (1, 128))


VMEM = pl.BlockSpec(memory_space=pltpu.VMEM)
ANY = pl.BlockSpec(memory_space=pl.ANY)
SMEM = pl.BlockSpec(memory_space=pltpu.SMEM)


def shape(dims, dtype):
    return jax.ShapeDtypeStruct(dims, dtype)


def call(kernel, in_specs, outs, flops=1 << 20, moved=1 << 20, scratch=(), grant=24):
    return pl.pallas_call(
        kernel,
        in_specs=in_specs,
        out_specs=[VMEM] * len(outs),
        out_shape=outs,
        scratch_shapes=list(scratch),
        compiler_params=pltpu.CompilerParams(vmem_limit_bytes=grant << 20),
        cost_estimate=pl.CostEstimate(flops=flops, bytes_accessed=moved, transcendentals=0),
    )


def received(blocks, axis):
    own, ahead, behind, across = blocks
    return [own, shift(ahead, axis, 1), shift(behind, axis, -1), shift(across, axis, 2)]


def ring_far(behind, ahead, axis):
    cut = behind.shape[0] // 2
    return shift(behind[:cut], axis, 1), shift(ahead[cut:], axis, -1)


def local(tokens, targets, norm_gain, down_weight, up_weight, down_vector, up_vector):
    place = jnp.stack([lax.axis_index(axis) for axis in ("z", "x", "y", "c")]).astype(jnp.int32)
    core = place[3]
    chunk, column = call(
        chunk_kernel,
        [VMEM] + [ANY] * 4,
        [shape((4, 128, RANK), BF16), shape((128, 128), F32)],
        scratch=[
            *[pltpu.VMEM((1, 128, RANK), BF16)] * 2,
            *[pltpu.VMEM((1, RANK, 128), BF16)] * 2,
            pltpu.SemaphoreType.DMA((4,)),
        ],
        grant=60,
    )(norm_gain, down_weight, down_vector, up_weight, up_vector)
    pair = shape((LAYERS, 2, 128, RANK), BF16)
    a_own, b_own = call(order_kernel, [SMEM] + [VMEM] * 4, [pair, pair])(
        place, chunk, shift(chunk, "y", 1), shift(chunk, "y", -1), shift(chunk, "y", 2)
    )

    def first_ring(own, axis):
        near = shift(own, axis, 1), shift(own, axis, -1)
        half = shape((2, 2, 128, RANK), BF16)
        behind, ahead = call(halves_kernel, [VMEM] * 2, [half] * 2)(*near)
        parts = own, *near, shift(behind, axis, 1), shift(ahead, axis, -1)
        (stacked,) = call(slots_kernel, [VMEM] * 5, [shape((4, *own.shape), BF16)])(*parts)
        return stacked

    a_all, b_all = first_ring(a_own, "z"), first_ring(b_own, "x")
    kept, given = call(
        rows_kernel, [SMEM, VMEM, VMEM], [shape((2, 32, HALF), BF16)] * 2, moved=3 << 20
    )(place, tokens, targets)
    got = swap(given)
    rows = jnp.where(
        core == 0, jnp.concatenate([kept, got], 1), jnp.concatenate([got, kept], 1)
    )
    a_near = shift(a_all, "x", 1), shift(a_all, "x", -1)
    b_near = shift(b_all, "z", 1), shift(b_all, "z", -1)
    a_near, b_near, rows = lax.optimization_barrier((a_near, b_near, rows))
    a_all = [a_all, *a_near, *ring_far(*a_near, "x")]
    b_all = [b_all, *b_near, *ring_far(*b_near, "z")]
    h, goal = rows[0], rows[1]
    x = jnp.concatenate([h, jnp.zeros_like(h)], 0)

    wide = shape((2 * ROWS, HALF), BF16)
    sums = shape((ROWS, 640), F32)
    e_sums = shape((ROWS, 512), F32)
    work = 6 * 2 * ROWS * HALF * RANK

    def exchanged(part):
        return part, swap(part)

    states, fulls, cots, e_fulls = [x], [], {}, {}
    (part,) = call(first_kernel, [VMEM] * 6, [sums], work // 3, 3 << 20)(
        x, *a_all
    )
    for layer in range(1, LAYERS):
        x, part, full = call(
            functools.partial(forward_kernel, layer),
            [VMEM] * 13,
            [wide, sums, sums],
            work,
            5 << 20,
        )(x, part, swap(part), *b_all, *a_all)
        states.append(x)
        fulls.append(full)
    cot, part, full = call(
        seed_kernel,
        [VMEM] * 9,
        [wide, e_sums, sums],
        work,
        3 << 20,
    )(x, part, swap(part), goal, *b_all)
    fulls.append(full)

    def backward(layer, cot, e_own, e_got):
        return call(
            functools.partial(backward_kernel, layer),
            [VMEM] * 15,
            [wide, e_sums, e_sums],
            work,
            5 << 20,
        )(states[layer], cot, fulls[layer], e_own, e_got, *a_all, *b_all)

    operands = []
    for layer in (3, 2, 1):
        cots[layer] = cot
        cot, part, e_fulls[layer] = backward(layer, cot, part, swap(part))
    for layer in (1, 2, 3):
        operands += [states[layer], cots[layer], fulls[layer], e_fulls[layer]]
    operands += [states[0], cot, fulls[0], part, swap(part)]

    slot = shape((4, LAYERS, 128, RANK), BF16)
    cut = shape((2, LAYERS, 128, RANK), BF16)
    four = shape((LAYERS, 128, RANK), BF16)
    far = call(far_kernel, [VMEM] * 17, [cut] * 4, work, 6 << 20)(*operands)
    far = (
        shift(far[0], "z", 1),
        shift(far[1], "z", -1),
        shift(far[2], "x", 1),
        shift(far[3], "x", -1),
    )
    near = call(near_kernel, [VMEM] * 17, [slot] * 6, 3 * work, 10 << 20)(*operands)
    sent = call(step_kernel, [VMEM] * 8, [slot] * 4, moved=10 << 20)(
        *(near[1], near[2], far[0], far[1]), *(near[4], near[5], far[2], far[3])
    )
    down_parts = near[0], shift(sent[0], "z", 1), shift(sent[1], "z", -1)
    up_parts = near[3], shift(sent[2], "x", 1), shift(sent[3], "x", -1)
    downs = call(ring_kernel, [VMEM] * 3, [four] * 4, moved=4 << 20)(*down_parts)
    downs = received(downs, "x")
    ups = call(ring_kernel, [VMEM] * 3, [four] * 4, moved=4 << 20)(*up_parts)
    ups = received(ups, "z")
    blocks = call(
        layer_kernel, [SMEM] + [VMEM] * 8, [shape((256, RANK), BF16)] * 4, moved=2 << 20
    )(place, *downs, *ups)
    share, totals = call(
        totals_kernel,
        [VMEM] * 6,
        [shape((256, RANK), F32), shape((1, 128), F32)],
    )(*received(blocks, "y"), column, jnp.concatenate([down_vector[0], chunk[3]], 0))
    totals = jnp.broadcast_to(totals[None], (128, 1, 128))
    totals = lax.all_to_all(totals, ("y", "z", "x", "c"), 0, 0).reshape(128, 128)
    next_down, next_up, quotient = call(
        output_kernel,
        [VMEM] * 2,
        [shape((128, RANK), BF16), shape((RANK, 128), BF16), shape((1, 128), F32)],
    )(share, totals)
    return (next_down[None], next_up[None], quotient[0, 0])


def solution(mesh):
    fine = Mesh(mesh.devices.reshape(4, 4, 4, 2), ("y", "z", "x", "c"))
    fsdp = ("z", "x", "c")
    placed = (
        P(fsdp, None),
        P(fsdp, None),
        P("y", fsdp),
        P("y", fsdp, None),
        P("y", None, fsdp),
        P("y", fsdp, None),
        P("y", None, fsdp),
    )
    return jax.shard_map(
        local,
        mesh=fine,
        in_specs=placed,
        out_specs=(P("y", fsdp, None), P("y", None, fsdp), P()),
        check_vma=False,
    )
```
